512 devices in a mesh: tm: 32 (over z, core), space: 16 (over x, y).
Axes of the slice: x: 4, y: 4, z: 16, core: 2. Of those that a mesh axis runs over, the one named last changes fastest.
Arguments:
- right_side: float32 [32, 128, 2048], P('tm', 'space'), may hold values from -160 to 160
- cell_terms: float32 [3, 128, 2048], P(None, 'space'), may hold values from -0.3 to 0.3, as said below
- polynomial: float32 [4], replicated, may hold values from -0.98 to 1.84, as said below
Outputs:
- solution: float32 [32, 128, 2048], P('tm', 'space')
- history: float32 [4], replicated
The draws below stay inside these ranges and needn't reach their ends.
Inputs may be any that keep to these rules, and one draw needn't show every extreme that they name: `cell_terms`: component 0 lies in [0.06, 0.25]; components 1 and 2 in [-0.3, 0.3]. `polynomial`: each coefficient lies within 15 percent of 1.6, -0.85, 0.2, -0.018 in order.
All inputs are finite; a program needn't handle non-finite values.
Results may differ from the reference program's by a relative error of at most 0.0015.
Values sent between devices are 32-bit elements; how exact they have to be, the bound alone decides.
No kernel may reach another device: no remote copies, remote signals or barrier semaphores. Data moves between devices by JAX's collectives and lax.ppermute only.
A program may use at most 64 MiB of HBM per device.

```python
import math
import jax
import jax.numpy as jnp

NCOL = 2048
KRYLOV = 4
NX = 128
NT = 32


def draw_right_side(key, part):
    key = jax.random.fold_in(key, 11)
    key_noise, key_rows, key_cols = jax.random.split(key, 3)
    step_index = jnp.arange(NT, dtype=jnp.float32)[:, None, None]
    noise = jnp.clip(jax.random.normal(key_noise, (NT, NX, NCOL), jnp.float32), -4.0, 4.0)
    growth = 3.0
    ramp = jnp.power(growth, step_index / max(NT - 1, 1))
    row_scale = jnp.power(10.0, jax.random.uniform(key_rows, (NT, NX, 1), jnp.float32))
    col_scale = jnp.power(10.0, jax.random.uniform(key_cols, (1, 1, NCOL), jnp.float32))
    values = 0.1 * noise * ramp * row_scale * col_scale
    return values


def draw_cell_terms(key, part):
    key = jax.random.fold_in(key, 23)
    key_diffuse, key_along, key_across = jax.random.split(key, 3)
    diffuse = jnp.exp(jax.random.uniform(key_diffuse, (NX, NCOL), jnp.float32, math.log(0.06), math.log(0.25)))
    drift_x = jax.random.uniform(key_along, (NX, NCOL), jnp.float32, -0.3, 0.3)
    drift_y = jax.random.uniform(key_across, (NX, NCOL), jnp.float32, -0.3, 0.3)
    return jnp.stack([diffuse, drift_x, drift_y])


def draw_polynomial(key, part):
    key = jax.random.fold_in(key, 37)
    anchor = jnp.array([1.6, -0.85, 0.2, -0.018], jnp.float32)
    factor = 1.0 + jax.random.uniform(key, (4,), jnp.float32, -0.15, 0.15)
    return anchor * factor


def setup_inputs(seed: int = 0) -> dict:
    key_of = jax.random.split(jax.random.key(seed), 4)
    right_side = draw_right_side(jax.random.fold_in(key_of[3], 71), 0)
    cell_terms = draw_cell_terms(jax.random.fold_in(key_of[3], 71), 0)
    polynomial = draw_polynomial(jax.random.fold_in(key_of[3], 71), 0)
    return {"right_side": right_side, "cell_terms": cell_terms, "polynomial": polynomial}


def stencil(padded, cell_terms):
    middle = padded[:, 1:-1]
    upper_row = padded[:, :-2]
    lower_row = padded[:, 2:]
    sideways = jnp.pad(middle, ((0, 0), (0, 0), (1, 1)))
    left_col = sideways[:, :, :-2]
    right_col = sideways[:, :, 2:]
    diffuse = cell_terms[0]
    drift_x = cell_terms[1]
    drift_y = cell_terms[2]
    return (1.0 + 4.0 * diffuse) * middle - diffuse * (upper_row + lower_row + left_col + right_col) + 0.5 * drift_x * (right_col - left_col) + 0.5 * drift_y * (lower_row - upper_row)

def pad_rows(source):
    return jnp.pad(source, ((0, 0), (1, 1), (0, 0)))

def precondition(source, cell_terms, polynomial):
    running = polynomial[3] * source
    for degree in (2, 1, 0):
        running = polynomial[degree] * source + stencil(pad_rows(running), cell_terms)
    return running

def apply_system(source, cell_terms):
    earlier = jnp.concatenate([jnp.zeros_like(source[:1]), source[:-1]], axis=0)
    return stencil(pad_rows(source), cell_terms) - earlier

def least_squares(columns, beta_norm):
    num_columns = len(columns)
    cosines = []
    sines = []
    target = [beta_norm] + [jnp.zeros_like(beta_norm) for position in range(num_columns)]
    history = []
    triangle = []
    for column_at in range(num_columns):
        column = list(columns[column_at])
        for earlier in range(column_at):
            first_entry = column[earlier]
            second_entry = column[earlier + 1]
            column[earlier] = cosines[earlier] * first_entry + sines[earlier] * second_entry
            column[earlier + 1] = cosines[earlier] * second_entry - sines[earlier] * first_entry
        radius = jnp.sqrt(column[column_at] * column[column_at] + column[column_at + 1] * column[column_at + 1])
        cosine = column[column_at] / radius
        sine_part = column[column_at + 1] / radius
        column[column_at] = radius
        cosines.append(cosine)
        sines.append(sine_part)
        target[column_at + 1] = -sine_part * target[column_at]
        target[column_at] = cosine * target[column_at]
        history.append(jnp.abs(target[column_at + 1]))
        triangle.append(column[:column_at + 1])
    solved = [None for position in range(num_columns)]
    for row_at in reversed(range(num_columns)):
        running_sum = target[row_at]
        for later in range(row_at + 1, num_columns):
            running_sum = running_sum - triangle[later][row_at] * solved[later]
        solved[row_at] = running_sum / triangle[row_at][row_at]
    return (solved, history)

def reference(right_side, cell_terms, polynomial):
    beta_norm = jnp.sqrt(jnp.sum(right_side * right_side))
    krylov_basis = [right_side / beta_norm]
    columns = []
    for krylov_at in range(KRYLOV):
        mapped = apply_system(precondition(krylov_basis[krylov_at], cell_terms, polynomial), cell_terms)
        projections = [jnp.sum(mapped * vector) for vector in krylov_basis]
        remainder = mapped
        for vector, weight in zip(krylov_basis, projections):
            remainder = remainder - weight * vector
        length = jnp.sqrt(jnp.sum(remainder * remainder) + 1e-06)
        columns.append(projections + [length])
        krylov_basis.append(remainder / length)
    solved, history = least_squares(columns, beta_norm)
    combined = solved[0] * krylov_basis[0]
    for position in range(1, KRYLOV):
        combined = combined + solved[position] * krylov_basis[position]
    return (precondition(combined, cell_terms, polynomial), jnp.stack(history))
```

```python
import functools

import jax
import jax.numpy as jnp
from jax import lax
from jax.experimental import pallas as pl
from jax.experimental.pallas import tpu as pltpu
from jax.sharding import Mesh, PartitionSpec as P

KRYLOV = 4
OWN = 64
HALO = 32
LANES = 128
ROWS = 8
PAD = 8
CHUNK = 32
PAIRS = [(i, j) for i in range(KRYLOV + 1) for j in range(i, KRYLOV + 1)]
VMEM = pl.BlockSpec(memory_space=pltpu.VMEM)
SMEM = pl.BlockSpec(memory_space=pltpu.SMEM)
PARAMS = pltpu.CompilerParams(vmem_limit_bytes=40 * 1024 * 1024)


def windows(blocks, lane):
    zero = jnp.zeros_like(blocks[0])
    even = [zero] + [pltpu.roll(b, HALO, 1) for b in blocks]
    odd = [pltpu.roll(b, LANES - HALO, 1) for b in blocks] + [zero]
    out = []
    for k in range(len(blocks)):
        out.append(jnp.where(lane < HALO, even[k], even[k + 1]))
        out.append(jnp.where(lane < LANES - HALO, odd[k], odd[k + 1]))
    return out


def pack_kernel(now, before, earlier, terms, out):
    core = lax.axis_index("c")
    lane = lax.broadcasted_iota(jnp.int32, (ROWS, LANES), 1)
    tiles = now.shape[2] // LANES
    sources = [
        lambda cols: now[0, :, cols],
        lambda cols: before[0, :, cols],
        lambda cols: earlier[0, :, cols],
        lambda cols: terms[2 * core, :, cols],
        lambda cols: terms[1 + core, :, cols],
    ]
    for plane, source in enumerate(sources):
        blocks = [source(slice(k * LANES, (k + 1) * LANES)) for k in range(tiles)]
        for peer, window in enumerate(windows(blocks, lane)):
            out[peer, plane] = window


def krylov_kernel(strips, polynomial, got, out, coef, k0, k1, k2, k3, k4, z1, z2, z3, z4, work_x, work_y):
    rows = ROWS * strips
    times = KRYLOV + 2
    krylov = [k0, k1, k2, k3, k4]
    lifted = [z1, z2, z3, z4]
    lane = lax.broadcasted_iota(jnp.int32, (ROWS, LANES), 1)
    sub = lax.broadcasted_iota(jnp.int32, (ROWS, LANES), 0)
    block = lax.axis_index("c") * strips + lax.axis_index("s")
    first_col = (block == 0) & (lane == HALO)
    last_col = (block == 2 * strips - 1) & (lane == HALO + OWN - 1)

    edge = jnp.zeros((PAD, LANES), jnp.float32)
    for ref in krylov + lifted + [work_x, work_y]:
        for t in range(ref.shape[0]):
            ref[t, 0:PAD] = edge
            ref[t, PAD + rows :] = edge

    for s in range(strips):
        there = slice(s * ROWS, (s + 1) * ROWS)
        inner = slice(PAD + s * ROWS, PAD + (s + 1) * ROWS)
        for c in range(2):
            for plane in range(3):
                k0[times - 2 + c - 2 * plane, inner] = got[c * strips + s, plane]
        diffuse = got[s, 3]
        half_x = 0.5 * got[s, 4]
        half_y = 0.5 * got[strips + s, 3]
        north = -diffuse - half_y
        south = half_y - diffuse
        if s == 0:
            north = jnp.where(sub == 0, 0.0, north)
        if s == strips - 1:
            south = jnp.where(sub == ROWS - 1, 0.0, south)
        coef[0, there] = 1.0 + 4.0 * diffuse
        coef[1, there] = north
        coef[2, there] = south
        coef[3, there] = jnp.where(first_col, 0.0, -diffuse - half_x)
        coef[4, there] = jnp.where(last_col, 0.0, half_x - diffuse)

    def sweep(count, apply):
        def step(index, carry):
            at = pl.multiple_of(index * CHUNK, CHUNK)
            parts = [coef[i, pl.ds(at, CHUNK)] for i in range(5)]

            def stencil(ref, t):
                middle = ref[t, pl.ds(at + PAD, CHUNK)]
                north = ref[t, pl.ds(at + PAD - 1, CHUNK)]
                south = ref[t, pl.ds(at + PAD + 1, CHUNK)]
                west = pltpu.roll(middle, 1, 1)
                east = pltpu.roll(middle, LANES - 1, 1)
                value = (
                    (parts[0] * middle + parts[3] * west)
                    + (parts[1] * north + parts[2] * south)
                    + parts[4] * east
                )
                return value, middle

            for t in range(count):
                apply(t, pl.ds(at + PAD, CHUNK), stencil)
            return carry

        lax.fori_loop(0, rows // CHUNK, step, 0)

    for j in range(KRYLOV):
        source, target, upper = krylov[j], krylov[j + 1], lifted[j]
        count = times - j

        def first(t, at, stencil):
            value, middle = stencil(source, t)
            work_x[t, at] = polynomial[2] * middle + polynomial[3] * value

        def second(t, at, stencil):
            value, _ = stencil(work_x, t)
            work_y[t, at] = polynomial[1] * source[t, at] + value

        def third(t, at, stencil):
            value, _ = stencil(work_y, t)
            upper[t, at] = polynomial[0] * source[t, at] + value

        def fourth(t, at, stencil):
            value, _ = stencil(upper, t + 1)
            target[t, at] = value - upper[t, at] - source[t + 1, at]

        sweep(count, first)
        sweep(count, second)
        sweep(count, third)
        sweep(count - 1, fourth)

    sums = [jnp.zeros((ROWS, LANES), jnp.float32) for _ in PAIRS]

    def gram(index, sums):
        at = pl.ds(pl.multiple_of(index * ROWS, ROWS) + PAD, ROWS)
        sums = list(sums)
        for own in range(2):
            vectors = [ref[ref.shape[0] - 2 + own, at] for ref in krylov]
            for n, (i, j) in enumerate(PAIRS):
                sums[n] = sums[n] + vectors[i] * vectors[j]
        return tuple(sums)

    sums = lax.fori_loop(0, strips, gram, tuple(sums))
    row = lax.broadcasted_iota(jnp.int32, (ROWS, LANES), 0)
    mine = (lane >= HALO) & (lane < HALO + OWN)
    packed = jnp.zeros((1, LANES), jnp.float32)
    for n, total in enumerate(sums):
        value = jnp.sum(jnp.where(mine, total, 0.0), axis=0, keepdims=True)
        value = jnp.sum(value, axis=1, keepdims=True)
        packed = packed + jnp.where(lane[0:1] == n, value, 0.0)
    packed = jnp.where(row == 0, packed, 0.0)

    for c in range(2):
        for s in range(strips):
            peer = c * strips + s
            at = slice(PAD + s * ROWS, PAD + (s + 1) * ROWS)
            for pair in range(2):
                low = lifted[2 * pair]
                high = lifted[2 * pair + 1]
                left = pltpu.roll(low[low.shape[0] - 2 + c, at], LANES - HALO, 1)
                right = pltpu.roll(high[high.shape[0] - 2 + c, at], HALO, 1)
                out[peer, pair] = jnp.where(lane < OWN, left, right)
            out[peer, 2] = packed


def least_squares(columns, beta_norm):
    num_columns = len(columns)
    cosines = []
    sines = []
    target = [beta_norm] + [jnp.zeros_like(beta_norm) for position in range(num_columns)]
    history = []
    triangle = []
    for column_at in range(num_columns):
        column = list(columns[column_at])
        for earlier in range(column_at):
            first_entry = column[earlier]
            second_entry = column[earlier + 1]
            column[earlier] = cosines[earlier] * first_entry + sines[earlier] * second_entry
            column[earlier + 1] = cosines[earlier] * second_entry - sines[earlier] * first_entry
        radius = jnp.sqrt(
            column[column_at] * column[column_at] + column[column_at + 1] * column[column_at + 1]
        )
        cosine = column[column_at] / radius
        sine_part = column[column_at + 1] / radius
        column[column_at] = radius
        cosines.append(cosine)
        sines.append(sine_part)
        target[column_at + 1] = -sine_part * target[column_at]
        target[column_at] = cosine * target[column_at]
        history.append(jnp.abs(target[column_at + 1]))
        triangle.append(column[: column_at + 1])
    solved = [None for position in range(num_columns)]
    for row_at in reversed(range(num_columns)):
        running_sum = target[row_at]
        for later in range(row_at + 1, num_columns):
            running_sum = running_sum - triangle[later][row_at] * solved[later]
        solved[row_at] = running_sum / triangle[row_at][row_at]
    return (solved, history)


def cycle(gram):
    def product(left, right):
        total = None
        for i, a in enumerate(left):
            for j, b in enumerate(right):
                term = a * b * gram[min(i, j), max(i, j)]
                total = term if total is None else total + term
        return total

    beta_norm = jnp.sqrt(gram[0, 0])
    basis = [[1.0 / beta_norm]]
    columns = []
    for at in range(KRYLOV):
        newest = basis[-1]
        image = list(newest) + [None]
        for m, value in enumerate(newest):
            image[m + 1] = value if image[m + 1] is None else image[m + 1] + value
        projections = [product(image, vector) for vector in basis]
        rest = list(image)
        for vector, weight in zip(basis, projections):
            for m, value in enumerate(vector):
                rest[m] = rest[m] - weight * value
        length = jnp.sqrt(jnp.maximum(product(rest, rest), 0.0) + 1e-06)
        columns.append(projections + [length])
        basis.append([value / length for value in rest])
    solved, history = least_squares(columns, beta_norm)
    weights = []
    for m in range(KRYLOV):
        total = None
        for j in range(m, KRYLOV):
            term = solved[j] * basis[j][m]
            total = term if total is None else total + term
        weights.append(total)
    return weights, history


def combine_kernel(partial, got, solution, history):
    lane = lax.broadcasted_iota(jnp.int32, (ROWS, LANES), 1)
    total = jnp.sum(partial[:, 0, :], axis=0, keepdims=True)
    gram = {}
    for n, pair in enumerate(PAIRS):
        gram[pair] = jnp.sum(jnp.where(lane[0:1] == n, total, 0.0), axis=1, keepdims=True)
    weights, norms = cycle(gram)
    for n, norm in enumerate(norms):
        history[n] = jnp.max(norm)
    low = jnp.where(lane < OWN, weights[0], weights[1])
    high = jnp.where(lane < OWN, weights[2], weights[3])

    def block(index):
        value = low * got[index, 0] + high * got[index, 1]
        return value + pltpu.roll(value, OWN, 1)

    for k in range(got.shape[0] // 2):
        solution[0, :, k * LANES : (k + 1) * LANES] = jnp.where(lane < OWN, block(2 * k), block(2 * k + 1))


def body(layers, strips, right_side, cell_terms, polynomial):
    f32 = jnp.float32
    peers = 2 * strips
    rows = ROWS * strips
    layer = ("c", "s")
    before = lax.ppermute(right_side, "z", [(i, i + 1) for i in range(layers - 1)])
    earlier = lax.ppermute(right_side, "z", [(i, i + 2) for i in range(layers - 2)])
    sent = pl.pallas_call(
        pack_kernel,
        out_shape=jax.ShapeDtypeStruct((peers, 5, ROWS, LANES), f32),
        in_specs=[VMEM] * 4,
        out_specs=VMEM,
        compiler_params=PARAMS,
        name="pack",
    )(right_side, before, earlier, cell_terms)
    got = lax.all_to_all(sent, layer, 0, 0, tiled=True)
    times = KRYLOV + 2
    field = lambda count: pltpu.VMEM((count, rows + 2 * PAD, LANES), f32)
    sent = pl.pallas_call(
        functools.partial(krylov_kernel, strips),
        out_shape=jax.ShapeDtypeStruct((peers, 3, ROWS, LANES), f32),
        in_specs=[SMEM, VMEM],
        out_specs=VMEM,
        scratch_shapes=[pltpu.VMEM((5, rows, LANES), f32)]
        + [field(times - j) for j in range(KRYLOV + 1)]
        + [field(times - j) for j in range(KRYLOV)]
        + [field(times), field(times)],
        compiler_params=PARAMS,
        name="krylov",
    )(polynomial, got)
    got = lax.all_to_all(sent, layer, 0, 0, tiled=True)
    partial = jnp.sum(got[:, 2, 0:1, :], axis=0)
    partial = jnp.broadcast_to(partial[None], (layers, 1, LANES))
    partial = lax.all_to_all(partial, "z", 0, 0, tiled=True)
    return pl.pallas_call(
        combine_kernel,
        out_shape=(jax.ShapeDtypeStruct(right_side.shape, f32), jax.ShapeDtypeStruct((KRYLOV,), f32)),
        in_specs=[VMEM, VMEM],
        out_specs=(VMEM, SMEM),
        compiler_params=PARAMS,
        name="combine",
    )(partial, got)


def solution(mesh):
    layers = mesh.shape["tm"] // 2
    strips = mesh.shape["space"]
    fine = Mesh(mesh.devices.reshape(layers, 2, strips), ("z", "c", "s"))
    in_specs = (P(("z", "c"), "s", None), P(None, "s", None), P())
    out_specs = (P(("z", "c"), "s", None), P())
    return jax.shard_map(
        functools.partial(body, layers, strips), mesh=fine, in_specs=in_specs, out_specs=out_specs, check_vma=False
    )
```

```python
import functools

import jax
import jax.numpy as jnp
from jax import lax
from jax.experimental import pallas as pl
from jax.experimental.pallas import tpu as pltpu
from jax.sharding import Mesh, PartitionSpec as P

KRYLOV = 4
OWN = 64
HALO = 32
LANES = 128
ROWS = 8
PAD = 8
CHUNK = 128
PAIRS = [(i, j) for i in range(KRYLOV + 1) for j in range(i, KRYLOV + 1)]
VMEM = pl.BlockSpec(memory_space=pltpu.VMEM)
SMEM = pl.BlockSpec(memory_space=pltpu.SMEM)
PARAMS = pltpu.CompilerParams(vmem_limit_bytes=40 * 1024 * 1024)


def windows(blocks, lane):
    zero = jnp.zeros_like(blocks[0])
    even = [zero] + [pltpu.roll(b, HALO, 1) for b in blocks]
    odd = [pltpu.roll(b, LANES - HALO, 1) for b in blocks] + [zero]
    out = []
    for k in range(len(blocks)):
        out.append(jnp.where(lane < HALO, even[k], even[k + 1]))
        out.append(jnp.where(lane < LANES - HALO, odd[k], odd[k + 1]))
    return out


def spread(sources, out, plane):
    lane = lax.broadcasted_iota(jnp.int32, (ROWS, LANES), 1)
    for source in sources:
        blocks = [source[:, k * LANES : (k + 1) * LANES] for k in range(source.shape[1] // LANES)]
        for peer, window in enumerate(windows(blocks, lane)):
            out[peer, plane] = window
        plane += 1


def own_kernel(now, terms, out):
    core = lax.axis_index("c")
    spread([now.at[0], terms.at[2 * core], terms.at[1 + core]], out, 0)


def pack_kernel(own, before, earlier, out):
    for peer in range(out.shape[0]):
        for plane in range(3):
            out[peer, plane] = own[peer, plane]
    spread([before.at[0], earlier.at[0]], out, 3)


def krylov_kernel(strips, polynomial, got, out, coef, k0, k1, k2, k3, k4, z1, z2, z3, z4, work_x, work_y):
    rows = ROWS * strips
    times = KRYLOV + 2
    krylov = [k0, k1, k2, k3, k4]
    lifted = [z1, z2, z3, z4]
    lane = lax.broadcasted_iota(jnp.int32, (ROWS, LANES), 1)
    sub = lax.broadcasted_iota(jnp.int32, (ROWS, LANES), 0)
    block = lax.axis_index("c") * strips + lax.axis_index("s")
    first_col = (block == 0) & (lane == HALO)
    last_col = (block == 2 * strips - 1) & (lane == HALO + OWN - 1)

    edge = jnp.zeros((PAD, LANES), jnp.float32)
    for ref in krylov + lifted + [work_x, work_y]:
        for t in range(ref.shape[0]):
            ref[t, 0:PAD] = edge
            ref[t, PAD + rows :] = edge

    for s in range(strips):
        there = slice(s * ROWS, (s + 1) * ROWS)
        inner = slice(PAD + s * ROWS, PAD + (s + 1) * ROWS)
        for c in range(2):
            for plane in range(3):
                k0[times - 2 + c - 2 * plane, inner] = got[c * strips + s, (0, 3, 4)[plane]]
        diffuse = got[s, 1]
        half_x = 0.5 * got[s, 2]
        half_y = 0.5 * got[strips + s, 1]
        north = -diffuse - half_y
        south = half_y - diffuse
        if s == 0:
            north = jnp.where(sub == 0, 0.0, north)
        if s == strips - 1:
            south = jnp.where(sub == ROWS - 1, 0.0, south)
        coef[0, there] = 1.0 + 4.0 * diffuse
        coef[1, there] = north
        coef[2, there] = south
        coef[3, there] = jnp.where(first_col, 0.0, -diffuse - half_x)
        coef[4, there] = jnp.where(last_col, 0.0, half_x - diffuse)

    def sweep(count, apply):
        def step(index, carry):
            at = pl.multiple_of(index * CHUNK, CHUNK)
            parts = [coef[i, pl.ds(at, CHUNK)] for i in range(5)]

            def stencil(ref, t):
                middle = ref[t, pl.ds(at + PAD, CHUNK)]
                north = ref[t, pl.ds(at + PAD - 1, CHUNK)]
                south = ref[t, pl.ds(at + PAD + 1, CHUNK)]
                west = pltpu.roll(middle, 1, 1)
                east = pltpu.roll(middle, LANES - 1, 1)
                value = (
                    (parts[0] * middle + parts[3] * west)
                    + (parts[1] * north + parts[2] * south)
                    + parts[4] * east
                )
                return value, middle

            for t in range(count):
                apply(t, pl.ds(at + PAD, CHUNK), stencil)
            return carry

        lax.fori_loop(0, rows // CHUNK, step, 0)

    for j in range(KRYLOV):
        source, target, upper = krylov[j], krylov[j + 1], lifted[j]
        count = times - j

        def first(t, at, stencil):
            value, middle = stencil(source, t)
            work_x[t, at] = polynomial[2] * middle + polynomial[3] * value

        def second(t, at, stencil):
            value, _ = stencil(work_x, t)
            work_y[t, at] = polynomial[1] * source[t, at] + value

        def third(t, at, stencil):
            value, _ = stencil(work_y, t)
            upper[t, at] = polynomial[0] * source[t, at] + value

        def fourth(t, at, stencil):
            value, _ = stencil(upper, t + 1)
            target[t, at] = value - upper[t, at] - source[t + 1, at]

        sweep(count, first)
        sweep(count, second)
        sweep(count, third)
        sweep(count - 1, fourth)

    sums = [jnp.zeros((ROWS, LANES), jnp.float32) for _ in PAIRS]

    def gram(index, sums):
        at = pl.ds(pl.multiple_of(index * ROWS, ROWS) + PAD, ROWS)
        sums = list(sums)
        for own in range(2):
            vectors = [ref[ref.shape[0] - 2 + own, at] for ref in krylov]
            for n, (i, j) in enumerate(PAIRS):
                sums[n] = sums[n] + vectors[i] * vectors[j]
        return tuple(sums)

    sums = lax.fori_loop(0, strips, gram, tuple(sums))
    row = lax.broadcasted_iota(jnp.int32, (ROWS, LANES), 0)
    mine = (lane >= HALO) & (lane < HALO + OWN)
    packed = jnp.zeros((1, LANES), jnp.float32)
    for n, total in enumerate(sums):
        value = jnp.sum(jnp.where(mine, total, 0.0), axis=0, keepdims=True)
        value = jnp.sum(value, axis=1, keepdims=True)
        packed = packed + jnp.where(lane[0:1] == n, value, 0.0)
    packed = jnp.where(row == 0, packed, 0.0)

    for c in range(2):
        for s in range(strips):
            peer = c * strips + s
            at = slice(PAD + s * ROWS, PAD + (s + 1) * ROWS)
            for pair in range(2):
                low = lifted[2 * pair]
                high = lifted[2 * pair + 1]
                left = pltpu.roll(low[low.shape[0] - 2 + c, at], LANES - HALO, 1)
                right = pltpu.roll(high[high.shape[0] - 2 + c, at], HALO, 1)
                out[peer, pair] = jnp.where(lane < OWN, left, right)
            out[peer, 2] = packed


def least_squares(columns, beta_norm):
    num_columns = len(columns)
    cosines = []
    sines = []
    target = [beta_norm] + [jnp.zeros_like(beta_norm) for position in range(num_columns)]
    history = []
    triangle = []
    for column_at in range(num_columns):
        column = list(columns[column_at])
        for earlier in range(column_at):
            first_entry = column[earlier]
            second_entry = column[earlier + 1]
            column[earlier] = cosines[earlier] * first_entry + sines[earlier] * second_entry
            column[earlier + 1] = cosines[earlier] * second_entry - sines[earlier] * first_entry
        radius = jnp.sqrt(
            column[column_at] * column[column_at] + column[column_at + 1] * column[column_at + 1]
        )
        cosine = column[column_at] / radius
        sine_part = column[column_at + 1] / radius
        column[column_at] = radius
        cosines.append(cosine)
        sines.append(sine_part)
        target[column_at + 1] = -sine_part * target[column_at]
        target[column_at] = cosine * target[column_at]
        history.append(jnp.abs(target[column_at + 1]))
        triangle.append(column[: column_at + 1])
    solved = [None for position in range(num_columns)]
    for row_at in reversed(range(num_columns)):
        running_sum = target[row_at]
        for later in range(row_at + 1, num_columns):
            running_sum = running_sum - triangle[later][row_at] * solved[later]
        solved[row_at] = running_sum / triangle[row_at][row_at]
    return (solved, history)


def cycle(gram):
    def product(left, right):
        total = None
        for i, a in enumerate(left):
            for j, b in enumerate(right):
                term = a * b * gram[min(i, j), max(i, j)]
                total = term if total is None else total + term
        return total

    beta_norm = jnp.sqrt(gram[0, 0])
    basis = [[1.0 / beta_norm]]
    columns = []
    for at in range(KRYLOV):
        newest = basis[-1]
        image = list(newest) + [None]
        for m, value in enumerate(newest):
            image[m + 1] = value if image[m + 1] is None else image[m + 1] + value
        projections = [product(image, vector) for vector in basis]
        rest = list(image)
        for vector, weight in zip(basis, projections):
            for m, value in enumerate(vector):
                rest[m] = rest[m] - weight * value
        length = jnp.sqrt(jnp.maximum(product(rest, rest), 0.0) + 1e-06)
        columns.append(projections + [length])
        basis.append([value / length for value in rest])
    solved, history = least_squares(columns, beta_norm)
    weights = []
    for m in range(KRYLOV):
        total = None
        for j in range(m, KRYLOV):
            term = solved[j] * basis[j][m]
            total = term if total is None else total + term
        weights.append(total)
    return weights, history


def combine_kernel(partial, got, solution, history):
    lane = lax.broadcasted_iota(jnp.int32, (ROWS, LANES), 1)
    total = jnp.sum(partial[:, 0, :], axis=0, keepdims=True)
    gram = {}
    for n, pair in enumerate(PAIRS):
        gram[pair] = jnp.sum(jnp.where(lane[0:1] == n, total, 0.0), axis=1, keepdims=True)
    weights, norms = cycle(gram)
    for n, norm in enumerate(norms):
        history[n] = jnp.max(norm)
    low = jnp.where(lane < OWN, weights[0], weights[1])
    high = jnp.where(lane < OWN, weights[2], weights[3])

    def block(index):
        value = low * got[index, 0] + high * got[index, 1]
        return value + pltpu.roll(value, OWN, 1)

    for k in range(got.shape[0] // 2):
        solution[0, :, k * LANES : (k + 1) * LANES] = jnp.where(lane < OWN, block(2 * k), block(2 * k + 1))


def body(layers, strips, right_side, cell_terms, polynomial):
    f32 = jnp.float32
    peers = 2 * strips
    rows = ROWS * strips
    layer = ("c", "s")
    earlier = lax.ppermute(right_side, "z", [(i, i + 2) for i in range(layers - 2)])
    before = lax.ppermute(right_side, "z", [(i, i + 1) for i in range(layers - 1)])
    own = pl.pallas_call(
        own_kernel,
        out_shape=jax.ShapeDtypeStruct((peers, 3, ROWS, LANES), f32),
        in_specs=[VMEM] * 2,
        out_specs=VMEM,
        compiler_params=PARAMS,
        cost_estimate=pl.CostEstimate(flops=1000000, bytes_accessed=4000000, transcendentals=0),
        name="own",
    )(right_side, cell_terms)
    sent = pl.pallas_call(
        pack_kernel,
        out_shape=jax.ShapeDtypeStruct((peers, 5, ROWS, LANES), f32),
        in_specs=[VMEM] * 3,
        out_specs=VMEM,
        compiler_params=PARAMS,
        name="pack",
    )(own, before, earlier)
    got = lax.all_to_all(sent, layer, 0, 0, tiled=True)
    times = KRYLOV + 2
    field = lambda count: pltpu.VMEM((count, rows + 2 * PAD, LANES), f32)
    sent = pl.pallas_call(
        functools.partial(krylov_kernel, strips),
        out_shape=jax.ShapeDtypeStruct((peers, 3, ROWS, LANES), f32),
        in_specs=[SMEM, VMEM],
        out_specs=VMEM,
        scratch_shapes=[pltpu.VMEM((5, rows, LANES), f32)]
        + [field(times - j) for j in range(KRYLOV + 1)]
        + [field(times - j) for j in range(KRYLOV)]
        + [field(times), field(times)],
        compiler_params=PARAMS,
        name="krylov",
    )(polynomial, got)
    got = lax.all_to_all(sent, layer, 0, 0, tiled=True)
    partial = jnp.sum(got[:, 2, 0:1, :], axis=0)
    partial = jnp.broadcast_to(partial[None], (layers, 1, LANES))
    partial = lax.all_to_all(partial, "z", 0, 0, tiled=True)
    return pl.pallas_call(
        combine_kernel,
        out_shape=(jax.ShapeDtypeStruct(right_side.shape, f32), jax.ShapeDtypeStruct((KRYLOV,), f32)),
        in_specs=[VMEM, VMEM],
        out_specs=(VMEM, SMEM),
        compiler_params=PARAMS,
        name="combine",
    )(partial, got)


def solution(mesh):
    layers = mesh.shape["tm"] // 2
    strips = mesh.shape["space"]
    fine = Mesh(mesh.devices.reshape(layers, 2, strips), ("z", "c", "s"))
    in_specs = (P(("z", "c"), "s", None), P(None, "s", None), P())
    out_specs = (P(("z", "c"), "s", None), P())
    return jax.shard_map(
        functools.partial(body, layers, strips), mesh=fine, in_specs=in_specs, out_specs=out_specs, check_vma=False
    )
```

```python
import functools

import jax
import jax.numpy as jnp
from jax import lax
from jax.experimental import pallas as pl
from jax.experimental.pallas import tpu as pltpu
from jax.sharding import Mesh, PartitionSpec as P

KRYLOV = 4
OWN = 64
HALO = 16
WIDE = OWN + 2 * HALO
HALF = 4
LANES = 128
ROWS = 8
PAD = 8
CHUNK = 128
PAIRS = [(i, j) for i in range(KRYLOV + 1) for j in range(i, KRYLOV + 1)]
VMEM = pl.BlockSpec(memory_space=pltpu.VMEM)
SMEM = pl.BlockSpec(memory_space=pltpu.SMEM)
PARAMS = pltpu.CompilerParams(vmem_limit_bytes=40 * 1024 * 1024)


def tiles_of(source):
    return [source[:, k * LANES : (k + 1) * LANES] for k in range(source.shape[1] // LANES)]


def windows(tiles, lane):
    zero = jnp.zeros_like(tiles[0])
    even = [zero] + [pltpu.roll(tile, HALO, 1) for tile in tiles]
    odd = [pltpu.roll(tile, LANES - OWN + HALO, 1) for tile in tiles] + [zero]
    out = []
    for k in range(len(tiles)):
        out.append(jnp.where(lane < HALO, even[k], even[k + 1]))
        out.append(jnp.where(lane < LANES - OWN + HALO, odd[k], odd[k + 1]))
    return out


def riders(tiles, lane):
    zero = jnp.zeros_like(tiles[0])
    turned = {shift: [pltpu.roll(tile, shift, 1) for tile in tiles] for shift in (16, 48, 80, 112)}
    edge = [zero] + turned[112] + [zero]
    out = []
    for k in range(len(tiles)):
        out.append([jnp.where(lane < 112, edge[k], edge[k + 1]), turned[80][k], turned[48][k]])
        out.append([turned[48][k], turned[16][k], jnp.where(lane < 112, edge[k + 1], edge[k + 2])])
    return out


def put(out, peer, plane, value):
    out[peer, 2 * plane] = value[:HALF]
    out[peer, 2 * plane + 1] = value[HALF:]


def own_kernel(now, terms, out):
    core = lax.axis_index("c")
    lane = lax.broadcasted_iota(jnp.int32, (ROWS, LANES), 1)
    fields = windows(tiles_of(now.at[0]), lane)
    parts = riders(tiles_of(terms.at[2 * core]), lane)
    across = windows(tiles_of(terms.at[1]), lane)
    upper = (lane >= 0) & (core == 0)
    for peer, (field, part, drift) in enumerate(zip(fields, parts, across)):
        put(out, peer, 0, jnp.where(lane < WIDE, field, part[0]))
        put(out, peer, 1, part[1])
        put(out, peer, 2, part[2])
        out[peer, 6] = jnp.where(upper[:HALF], drift[:HALF], drift[HALF:])


def pack_kernel(own, before, earlier, out):
    lane = lax.broadcasted_iota(jnp.int32, (ROWS, LANES), 1)
    narrow = lane[:HALF] < WIDE
    for peer in range(out.shape[0]):
        for half in (0, 1, 6):
            out[peer, half] = own[peer, half]
    for plane, source in ((1, before), (2, earlier)):
        for peer, window in enumerate(windows(tiles_of(source.at[0]), lane)):
            out[peer, 2 * plane] = jnp.where(narrow, window[:HALF], own[peer, 2 * plane])
            out[peer, 2 * plane + 1] = jnp.where(narrow, window[HALF:], own[peer, 2 * plane + 1])


def krylov_kernel(strips, polynomial, got, out, coef, k0, k1, k2, k3, k4, z1, z2, z3, z4, work_x, work_y):
    rows = ROWS * strips
    times = KRYLOV + 2
    krylov = [k0, k1, k2, k3, k4]
    lifted = [z1, z2, z3, z4]
    lane = lax.broadcasted_iota(jnp.int32, (ROWS, LANES), 1)
    sub = lax.broadcasted_iota(jnp.int32, (ROWS, LANES), 0)
    block = lax.axis_index("c") * strips + lax.axis_index("s")
    first_col = (block == 0) & (lane == HALO)
    last_col = (block == 2 * strips - 1) & (lane == HALO + OWN - 1)

    edge = jnp.zeros((PAD, LANES), jnp.float32)
    for ref in krylov + lifted + [work_x, work_y]:
        for t in range(ref.shape[0]):
            ref[t, 0:PAD] = edge
            ref[t, PAD + rows :] = edge

    for s in range(strips):
        for c in range(2):
            peer = c * strips + s
            at = PAD + s * ROWS
            for plane in range(3):
                k0[times - 2 + c - 2 * plane, at : at + HALF] = got[peer, 2 * plane]
                k0[times - 2 + c - 2 * plane, at + HALF : at + ROWS] = got[peer, 2 * plane + 1]
            coef[3, s * ROWS + c * HALF : s * ROWS + (c + 1) * HALF] = got[peer, 6]

    def rider(at, c):
        last = [pltpu.roll(k0[times - 2 + c - 2 * plane, at], 32 * (plane + 1), 1) for plane in range(3)]
        last[2] = jnp.where(lane < WIDE, last[2], 0.0)
        return jnp.where(lane < 32, last[0], jnp.where(lane < 64, last[1], last[2]))

    for s in range(strips):
        there = slice(s * ROWS, (s + 1) * ROWS)
        inner = slice(PAD + s * ROWS, PAD + (s + 1) * ROWS)
        diffuse = rider(inner, 0)
        half_x = 0.5 * coef[3, there]
        half_y = 0.5 * rider(inner, 1)
        north = -diffuse - half_y
        south = half_y - diffuse
        if s == 0:
            north = jnp.where(sub == 0, 0.0, north)
        if s == strips - 1:
            south = jnp.where(sub == ROWS - 1, 0.0, south)
        coef[0, there] = 1.0 + 4.0 * diffuse
        coef[1, there] = north
        coef[2, there] = south
        coef[3, there] = jnp.where(first_col, 0.0, -diffuse - half_x)
        coef[4, there] = jnp.where(last_col, 0.0, half_x - diffuse)

    def sweep(count, apply):
        def step(index, carry):
            at = pl.multiple_of(index * CHUNK, CHUNK)
            parts = [coef[i, pl.ds(at, CHUNK)] for i in range(5)]

            def stencil(ref, t):
                middle = ref[t, pl.ds(at + PAD, CHUNK)]
                north = ref[t, pl.ds(at + PAD - 1, CHUNK)]
                south = ref[t, pl.ds(at + PAD + 1, CHUNK)]
                west = pltpu.roll(middle, 1, 1)
                east = pltpu.roll(middle, LANES - 1, 1)
                value = (
                    (parts[0] * middle + parts[3] * west)
                    + (parts[1] * north + parts[2] * south)
                    + parts[4] * east
                )
                return value, middle

            for t in range(count):
                apply(t, pl.ds(at + PAD, CHUNK), stencil)
            return carry

        lax.fori_loop(0, rows // CHUNK, step, 0)

    for j in range(KRYLOV):
        source, target, upper = krylov[j], krylov[j + 1], lifted[j]
        count = times - j

        def first(t, at, stencil):
            value, middle = stencil(source, t)
            work_x[t, at] = polynomial[2] * middle + polynomial[3] * value

        def second(t, at, stencil):
            value, _ = stencil(work_x, t)
            work_y[t, at] = polynomial[1] * source[t, at] + value

        def third(t, at, stencil):
            value, _ = stencil(work_y, t)
            upper[t, at] = polynomial[0] * source[t, at] + value

        def fourth(t, at, stencil):
            value, _ = stencil(upper, t + 1)
            target[t, at] = value - upper[t, at] - source[t + 1, at]

        sweep(count, first)
        sweep(count, second)
        sweep(count, third)
        sweep(count - 1, fourth)

    sums = [jnp.zeros((ROWS, LANES), jnp.float32) for _ in PAIRS]

    def gram(index, sums):
        at = pl.ds(pl.multiple_of(index * ROWS, ROWS) + PAD, ROWS)
        sums = list(sums)
        for own in range(2):
            vectors = [ref[ref.shape[0] - 2 + own, at] for ref in krylov]
            for n, (i, j) in enumerate(PAIRS):
                sums[n] = sums[n] + vectors[i] * vectors[j]
        return tuple(sums)

    sums = lax.fori_loop(0, strips, gram, tuple(sums))
    row = lax.broadcasted_iota(jnp.int32, (ROWS, LANES), 0)
    mine = (lane >= HALO) & (lane < HALO + OWN)
    packed = jnp.zeros((1, LANES), jnp.float32)
    for n, total in enumerate(sums):
        value = jnp.sum(jnp.where(mine, total, 0.0), axis=0, keepdims=True)
        value = jnp.sum(value, axis=1, keepdims=True)
        packed = packed + jnp.where(lane[0:1] == n, value, 0.0)
    packed = jnp.where(row[:HALF] == 0, packed, 0.0)

    for c in range(2):
        for s in range(strips):
            peer = c * strips + s
            at = slice(PAD + s * ROWS, PAD + (s + 1) * ROWS)
            for pair in range(2):
                low = lifted[2 * pair]
                high = lifted[2 * pair + 1]
                turned = pltpu.roll(high[high.shape[0] - 2 + c, at], OWN, 1)
                put(out, peer, pair, jnp.where(mine, low[low.shape[0] - 2 + c, at], turned))
            out[peer, 4] = packed


def least_squares(columns, beta_norm):
    num_columns = len(columns)
    cosines = []
    sines = []
    target = [beta_norm] + [jnp.zeros_like(beta_norm) for position in range(num_columns)]
    history = []
    triangle = []
    for column_at in range(num_columns):
        column = list(columns[column_at])
        for earlier in range(column_at):
            first_entry = column[earlier]
            second_entry = column[earlier + 1]
            column[earlier] = cosines[earlier] * first_entry + sines[earlier] * second_entry
            column[earlier + 1] = cosines[earlier] * second_entry - sines[earlier] * first_entry
        radius = jnp.sqrt(
            column[column_at] * column[column_at] + column[column_at + 1] * column[column_at + 1]
        )
        cosine = column[column_at] / radius
        sine_part = column[column_at + 1] / radius
        column[column_at] = radius
        cosines.append(cosine)
        sines.append(sine_part)
        target[column_at + 1] = -sine_part * target[column_at]
        target[column_at] = cosine * target[column_at]
        history.append(jnp.abs(target[column_at + 1]))
        triangle.append(column[: column_at + 1])
    solved = [None for position in range(num_columns)]
    for row_at in reversed(range(num_columns)):
        running_sum = target[row_at]
        for later in range(row_at + 1, num_columns):
            running_sum = running_sum - triangle[later][row_at] * solved[later]
        solved[row_at] = running_sum / triangle[row_at][row_at]
    return (solved, history)


def cycle(gram):
    def product(left, right):
        total = None
        for i, a in enumerate(left):
            for j, b in enumerate(right):
                term = a * b * gram[min(i, j), max(i, j)]
                total = term if total is None else total + term
        return total

    beta_norm = jnp.sqrt(gram[0, 0])
    basis = [[1.0 / beta_norm]]
    columns = []
    for at in range(KRYLOV):
        newest = basis[-1]
        image = list(newest) + [None]
        for m, value in enumerate(newest):
            image[m + 1] = value if image[m + 1] is None else image[m + 1] + value
        projections = [product(image, vector) for vector in basis]
        rest = list(image)
        for vector, weight in zip(basis, projections):
            for m, value in enumerate(vector):
                rest[m] = rest[m] - weight * value
        length = jnp.sqrt(jnp.maximum(product(rest, rest), 0.0) + 1e-06)
        columns.append(projections + [length])
        basis.append([value / length for value in rest])
    solved, history = least_squares(columns, beta_norm)
    weights = []
    for m in range(KRYLOV):
        total = None
        for j in range(m, KRYLOV):
            term = solved[j] * basis[j][m]
            total = term if total is None else total + term
        weights.append(total)
    return weights, history


def combine_kernel(partial, got, solution, history):
    lane = lax.broadcasted_iota(jnp.int32, (ROWS, LANES), 1)
    total = jnp.sum(partial[:, 0, :], axis=0, keepdims=True)
    gram = {}
    for n, pair in enumerate(PAIRS):
        gram[pair] = jnp.sum(jnp.where(lane[0:1] == n, total, 0.0), axis=1, keepdims=True)
    weights, norms = cycle(gram)
    for n, norm in enumerate(norms):
        history[n] = jnp.max(norm)
    half = lane[:HALF]
    mine = (half >= HALO) & (half < HALO + OWN)
    low = jnp.where(mine, weights[0], weights[1])
    high = jnp.where(mine, weights[2], weights[3])

    def block(index, part):
        value = low * got[index, part] + high * got[index, 2 + part]
        return pltpu.roll(value, LANES - HALO, 1) + pltpu.roll(value, OWN - HALO, 1)

    for k in range(got.shape[0] // 2):
        for part in range(2):
            value = jnp.where(half < OWN, block(2 * k, part), block(2 * k + 1, part))
            solution[0, part * HALF : (part + 1) * HALF, k * LANES : (k + 1) * LANES] = value


def body(layers, strips, right_side, cell_terms, polynomial):
    f32 = jnp.float32
    peers = 2 * strips
    rows = ROWS * strips
    layer = ("c", "s")
    earlier = lax.ppermute(right_side, "z", [(i, i + 2) for i in range(layers - 2)])
    before = lax.ppermute(right_side, "z", [(i, i + 1) for i in range(layers - 1)])
    own = pl.pallas_call(
        own_kernel,
        out_shape=jax.ShapeDtypeStruct((peers, 7, HALF, LANES), f32),
        in_specs=[VMEM] * 2,
        out_specs=VMEM,
        compiler_params=PARAMS,
        cost_estimate=pl.CostEstimate(flops=1000000, bytes_accessed=4000000, transcendentals=0),
        name="own",
    )(right_side, cell_terms)
    sent = pl.pallas_call(
        pack_kernel,
        out_shape=jax.ShapeDtypeStruct((peers, 7, HALF, LANES), f32),
        in_specs=[VMEM] * 3,
        out_specs=VMEM,
        compiler_params=PARAMS,
        name="pack",
    )(own, before, earlier)
    got = lax.all_to_all(sent, layer, 0, 0, tiled=True)
    times = KRYLOV + 2
    field = lambda count: pltpu.VMEM((count, rows + 2 * PAD, LANES), f32)
    sent = pl.pallas_call(
        functools.partial(krylov_kernel, strips),
        out_shape=jax.ShapeDtypeStruct((peers, 5, HALF, LANES), f32),
        in_specs=[SMEM, VMEM],
        out_specs=VMEM,
        scratch_shapes=[pltpu.VMEM((5, rows, LANES), f32)]
        + [field(times - j) for j in range(KRYLOV + 1)]
        + [field(times - j) for j in range(KRYLOV)]
        + [field(times), field(times)],
        compiler_params=PARAMS,
        name="krylov",
    )(polynomial, got)
    got = lax.all_to_all(sent, layer, 0, 0, tiled=True)
    partial = jnp.sum(got[:, 4, 0:1, :], axis=0)
    partial = jnp.broadcast_to(partial[None], (layers, 1, LANES))
    partial = lax.all_to_all(partial, "z", 0, 0, tiled=True)
    return pl.pallas_call(
        combine_kernel,
        out_shape=(jax.ShapeDtypeStruct(right_side.shape, f32), jax.ShapeDtypeStruct((KRYLOV,), f32)),
        in_specs=[VMEM, VMEM],
        out_specs=(VMEM, SMEM),
        compiler_params=PARAMS,
        name="combine",
    )(partial, got)


def solution(mesh):
    layers = mesh.shape["tm"] // 2
    strips = mesh.shape["space"]
    fine = Mesh(mesh.devices.reshape(layers, 2, strips), ("z", "c", "s"))
    in_specs = (P(("z", "c"), "s", None), P(None, "s", None), P())
    out_specs = (P(("z", "c"), "s", None), P())
    return jax.shard_map(
        functools.partial(body, layers, strips), mesh=fine, in_specs=in_specs, out_specs=out_specs, check_vma=False
    )
```

```python
import functools

import jax
import jax.numpy as jnp
from jax import lax
from jax.experimental import pallas as pl
from jax.experimental.pallas import tpu as pltpu
from jax.sharding import Mesh, PartitionSpec as P

KRYLOV = 4
OWN = 64
HALO = 16
WIDE = OWN + 2 * HALO
HALF = 4
LANES = 128
ROWS = 8
PAD = 8
CHUNK = 128
PAIRS = [(i, j) for i in range(KRYLOV + 1) for j in range(i, KRYLOV + 1)]
VMEM = pl.BlockSpec(memory_space=pltpu.VMEM)
SMEM = pl.BlockSpec(memory_space=pltpu.SMEM)
PARAMS = pltpu.CompilerParams(vmem_limit_bytes=40 * 1024 * 1024)


def tiles_of(source):
    return [source[:, k * LANES : (k + 1) * LANES] for k in range(source.shape[1] // LANES)]


def windows(tiles, lane):
    zero = jnp.zeros_like(tiles[0])
    even = [zero] + [pltpu.roll(tile, HALO, 1) for tile in tiles]
    odd = [pltpu.roll(tile, LANES - OWN + HALO, 1) for tile in tiles] + [zero]
    out = []
    for k in range(len(tiles)):
        out.append(jnp.where(lane < HALO, even[k], even[k + 1]))
        out.append(jnp.where(lane < LANES - OWN + HALO, odd[k], odd[k + 1]))
    return out


def riders(tiles, lane):
    zero = jnp.zeros_like(tiles[0])
    turned = {shift: [pltpu.roll(tile, shift, 1) for tile in tiles] for shift in (16, 48, 80, 112)}
    edge = [zero] + turned[112] + [zero]
    out = []
    for k in range(len(tiles)):
        out.append([jnp.where(lane < 112, edge[k], edge[k + 1]), turned[80][k], turned[48][k]])
        out.append([turned[48][k], turned[16][k], jnp.where(lane < 112, edge[k + 1], edge[k + 2])])
    return out


def put(out, peer, plane, value):
    out[peer, 2 * plane] = value[:HALF]
    out[peer, 2 * plane + 1] = value[HALF:]


def own_kernel(now, terms, out):
    core = lax.axis_index("c")
    lane = lax.broadcasted_iota(jnp.int32, (ROWS, LANES), 1)
    fields = windows(tiles_of(now.at[0]), lane)
    parts = riders(tiles_of(terms.at[2 * core]), lane)
    across = windows(tiles_of(terms.at[1]), lane)
    upper = (lane >= 0) & (core == 0)
    for peer, (field, part, drift) in enumerate(zip(fields, parts, across)):
        put(out, peer, 0, jnp.where(lane < WIDE, field, part[0]))
        put(out, peer, 1, part[1])
        put(out, peer, 2, part[2])
        out[peer, 6] = jnp.where(upper[:HALF], drift[:HALF], drift[HALF:])


def pack_kernel(own, before, earlier, out):
    lane = lax.broadcasted_iota(jnp.int32, (ROWS, LANES), 1)
    narrow = lane[:HALF] < WIDE
    for peer in range(out.shape[0]):
        for half in (0, 1, 6):
            out[peer, half] = own[peer, half]
    for plane, source in ((1, before), (2, earlier)):
        for peer, window in enumerate(windows(tiles_of(source.at[0]), lane)):
            out[peer, 2 * plane] = jnp.where(narrow, window[:HALF], own[peer, 2 * plane])
            out[peer, 2 * plane + 1] = jnp.where(narrow, window[HALF:], own[peer, 2 * plane + 1])


def two_sum(a, b):
    total = a + b
    moved = total - a
    return total, (a - (total - moved)) + (b - moved)


def split(a):
    scaled = 4097.0 * a
    upper = scaled - (scaled - a)
    return upper, a - upper


def exact_sum(top, low, axis):
    quantum = 1024.0 * jnp.max(jnp.abs(top), axis=axis, keepdims=True)
    upper = (top + quantum) - quantum
    rest = (top - upper) + low
    return jnp.sum(upper, axis=axis, keepdims=True), jnp.sum(rest, axis=axis, keepdims=True)


class Pair:
    def __init__(self, top, low):
        self.top = top + low
        self.low = low - (self.top - top)
        self.parts = split(self.top)

    def times(self, other):
        value = self.top * other.top
        (a, b), (c, d) = self.parts, other.parts
        error = (((a * c - value) + a * d) + b * c) + b * d
        return Pair(value, error + (self.top * other.low + self.low * other.top))

    def minus(self, other):
        value, error = two_sum(self.top, -other.top)
        return Pair(value, error + (self.low - other.low))

    def inverse(self):
        guess = 1.0 / self.top
        value = guess * self.top
        (a, b), (c, d) = split(guess), self.parts
        error = (((a * c - value) + a * d) + b * c) + b * d
        return Pair(guess, guess * (((1.0 - value) - error) - guess * self.low))


def krylov_kernel(strips, polynomial, got, out, coef, k0, k1, k2, k3, k4, z1, z2, z3, z4, work_x, work_y):
    rows = ROWS * strips
    times = KRYLOV + 2
    krylov = [k0, k1, k2, k3, k4]
    lifted = [z1, z2, z3, z4]
    lane = lax.broadcasted_iota(jnp.int32, (ROWS, LANES), 1)
    sub = lax.broadcasted_iota(jnp.int32, (ROWS, LANES), 0)
    block = lax.axis_index("c") * strips + lax.axis_index("s")
    first_col = (block == 0) & (lane == HALO)
    last_col = (block == 2 * strips - 1) & (lane == HALO + OWN - 1)

    edge = jnp.zeros((PAD, LANES), jnp.float32)
    for ref in krylov + lifted + [work_x, work_y]:
        for t in range(ref.shape[0]):
            ref[t, 0:PAD] = edge
            ref[t, PAD + rows :] = edge

    for s in range(strips):
        for c in range(2):
            peer = c * strips + s
            at = PAD + s * ROWS
            for plane in range(3):
                k0[times - 2 + c - 2 * plane, at : at + HALF] = got[peer, 2 * plane]
                k0[times - 2 + c - 2 * plane, at + HALF : at + ROWS] = got[peer, 2 * plane + 1]
            coef[3, s * ROWS + c * HALF : s * ROWS + (c + 1) * HALF] = got[peer, 6]

    def rider(at, c):
        last = [pltpu.roll(k0[times - 2 + c - 2 * plane, at], 32 * (plane + 1), 1) for plane in range(3)]
        last[2] = jnp.where(lane < WIDE, last[2], 0.0)
        return jnp.where(lane < 32, last[0], jnp.where(lane < 64, last[1], last[2]))

    for s in range(strips):
        there = slice(s * ROWS, (s + 1) * ROWS)
        inner = slice(PAD + s * ROWS, PAD + (s + 1) * ROWS)
        diffuse = rider(inner, 0)
        half_x = 0.5 * coef[3, there]
        half_y = 0.5 * rider(inner, 1)
        north = -diffuse - half_y
        south = half_y - diffuse
        if s == 0:
            north = jnp.where(sub == 0, 0.0, north)
        if s == strips - 1:
            south = jnp.where(sub == ROWS - 1, 0.0, south)
        coef[0, there] = 1.0 + 4.0 * diffuse
        coef[1, there] = north
        coef[2, there] = south
        coef[3, there] = jnp.where(first_col, 0.0, -diffuse - half_x)
        coef[4, there] = jnp.where(last_col, 0.0, half_x - diffuse)

    def sweep(count, apply):
        def step(index, carry):
            at = pl.multiple_of(index * CHUNK, CHUNK)
            parts = [coef[i, pl.ds(at, CHUNK)] for i in range(5)]

            def stencil(ref, t):
                middle = ref[t, pl.ds(at + PAD, CHUNK)]
                north = ref[t, pl.ds(at + PAD - 1, CHUNK)]
                south = ref[t, pl.ds(at + PAD + 1, CHUNK)]
                west = pltpu.roll(middle, 1, 1)
                east = pltpu.roll(middle, LANES - 1, 1)
                value = (
                    (parts[0] * middle + parts[3] * west)
                    + (parts[1] * north + parts[2] * south)
                    + parts[4] * east
                )
                return value, middle

            for t in range(count):
                apply(t, pl.ds(at + PAD, CHUNK), stencil)
            return carry

        lax.fori_loop(0, rows // CHUNK, step, 0)

    for j in range(KRYLOV):
        source, target, upper = krylov[j], krylov[j + 1], lifted[j]
        count = times - j

        def first(t, at, stencil):
            value, middle = stencil(source, t)
            work_x[t, at] = polynomial[2] * middle + polynomial[3] * value

        def second(t, at, stencil):
            value, _ = stencil(work_x, t)
            work_y[t, at] = polynomial[1] * source[t, at] + value

        def third(t, at, stencil):
            value, _ = stencil(work_y, t)
            upper[t, at] = polynomial[0] * source[t, at] + value

        def fourth(t, at, stencil):
            value, _ = stencil(upper, t + 1)
            target[t, at] = value - upper[t, at] - source[t + 1, at]

        sweep(count, first)
        sweep(count, second)
        sweep(count, third)
        sweep(count - 1, fourth)

    mine = (lane >= HALO) & (lane < HALO + OWN)
    nothing = jnp.zeros((ROWS, LANES), jnp.float32)

    def gram(index, sums):
        at = pl.ds(pl.multiple_of(index * ROWS, ROWS) + PAD, ROWS)
        vectors = []
        for ref in krylov:
            newest = pltpu.roll(ref[ref.shape[0] - 1, at], OWN, 1)
            value = jnp.where(mine, ref[ref.shape[0] - 2, at], newest)
            vectors.append((value,) + split(value))
        out = []
        for (i, j), (top, low) in zip(PAIRS, sums):
            (_, upper, lower), (other, other_upper, other_lower) = vectors[i], vectors[j]
            top, error = two_sum(top, upper * other_upper)
            out.append((top, low + (error + (upper * other_lower + lower * other))))
        return tuple(out)

    sums = lax.fori_loop(0, strips, gram, tuple((nothing, nothing) for _ in PAIRS))
    tops = [nothing, nothing]
    lows = [nothing, nothing]
    for n, (top, low) in enumerate(sums):
        for shift in (4, 2, 1):
            top, error = two_sum(top, pltpu.roll(top, shift, 0))
            low = low + pltpu.roll(low, shift, 0) + error
        tops[n // ROWS] = jnp.where(sub == n % ROWS, top, tops[n // ROWS])
        lows[n // ROWS] = jnp.where(sub == n % ROWS, low, lows[n // ROWS])
    packed = [nothing, nothing]
    for n in range(2):
        parts = exact_sum(tops[n], lows[n], 1)
        for kind in range(2):
            packed[kind] = jnp.where(lane == sub + n * ROWS, parts[kind], packed[kind])
    packed = [jnp.sum(value, axis=0, keepdims=True) for value in packed]
    packed = jnp.where(sub[:HALF] == 0, packed[0], jnp.where(sub[:HALF] == 1, packed[1], 0.0))

    for c in range(2):
        for s in range(strips):
            peer = c * strips + s
            at = slice(PAD + s * ROWS, PAD + (s + 1) * ROWS)
            for pair in range(2):
                low = lifted[2 * pair]
                high = lifted[2 * pair + 1]
                turned = pltpu.roll(high[high.shape[0] - 2 + c, at], OWN, 1)
                put(out, peer, pair, jnp.where(mine, low[low.shape[0] - 2 + c, at], turned))
            out[peer, 4] = packed


def least_squares(columns, beta_norm):
    num_columns = len(columns)
    cosines = []
    sines = []
    target = [beta_norm] + [jnp.zeros_like(beta_norm) for position in range(num_columns)]
    history = []
    triangle = []
    for column_at in range(num_columns):
        column = list(columns[column_at])
        for earlier in range(column_at):
            first_entry = column[earlier]
            second_entry = column[earlier + 1]
            column[earlier] = cosines[earlier] * first_entry + sines[earlier] * second_entry
            column[earlier + 1] = cosines[earlier] * second_entry - sines[earlier] * first_entry
        radius = jnp.sqrt(
            column[column_at] * column[column_at] + column[column_at + 1] * column[column_at + 1]
        )
        cosine = column[column_at] / radius
        sine_part = column[column_at + 1] / radius
        column[column_at] = radius
        cosines.append(cosine)
        sines.append(sine_part)
        target[column_at + 1] = -sine_part * target[column_at]
        target[column_at] = cosine * target[column_at]
        history.append(jnp.abs(target[column_at + 1]))
        triangle.append(column[: column_at + 1])
    solved = [None for position in range(num_columns)]
    for row_at in reversed(range(num_columns)):
        running_sum = target[row_at]
        for later in range(row_at + 1, num_columns):
            running_sum = running_sum - triangle[later][row_at] * solved[later]
        solved[row_at] = running_sum / triangle[row_at][row_at]
    return (solved, history)


def cycle(gram):
    size = KRYLOV + 1
    floors = [1e-12 * gram[k, k].top + 1e-30 for k in range(size)]
    upper = {}
    for k in range(size):
        pivot = jnp.maximum(gram[k, k].top, floors[k])
        root = jnp.sqrt(pivot)
        upper[k, k] = root
        for j in range(k + 1, size):
            upper[k, j] = gram[k, j].top / root
        if k + 1 < size:
            inverse = Pair(pivot, jnp.where(gram[k, k].top < floors[k], 0.0, gram[k, k].low)).inverse()
            for i in range(k + 1, size):
                factor = gram[k, i].times(inverse)
                for j in range(i, size):
                    gram[i, j] = gram[i, j].minus(factor.times(gram[k, j]))

    mapped = []
    for i in range(KRYLOV):
        column = []
        for row in range(i + 2):
            value = upper[row, i + 1]
            if row <= i:
                value = value + upper[row, i]
            for k in range(max(row - 1, 0), i):
                value = value - upper[k, i] * mapped[k][row]
            column.append(value / upper[i, i])
        mapped.append(column)

    beta_norm = upper[0, 0]
    basis = [[jnp.ones_like(beta_norm)]]
    columns = []
    for at in range(KRYLOV):
        newest = basis[-1]
        image = []
        for row in range(at + 2):
            terms = [mapped[i][row] * newest[i] for i in range(max(row - 1, 0), at + 1)]
            image.append(functools.reduce(lambda a, b: a + b, terms))
        projections = []
        rest = list(image)
        for vector in basis:
            terms = [a * b for a, b in zip(image, vector)]
            projections.append(functools.reduce(lambda a, b: a + b, terms))
        for vector, weight in zip(basis, projections):
            for row, value in enumerate(vector):
                rest[row] = rest[row] - weight * value
        terms = [value * value for value in rest]
        length = jnp.sqrt(functools.reduce(lambda a, b: a + b, terms) + 1e-06)
        columns.append(projections + [length])
        basis.append([value / length for value in rest])
    solved, history = least_squares(columns, beta_norm)
    weights = [None] * KRYLOV
    for row in reversed(range(KRYLOV)):
        terms = [solved[j] * basis[j][row] for j in range(row, KRYLOV)]
        value = functools.reduce(lambda a, b: a + b, terms)
        for later in range(row + 1, KRYLOV):
            value = value - upper[row, later] * weights[later]
        weights[row] = value / upper[row, row]
    return weights, history


def combine_kernel(partial, got, solution, history):
    lane = lax.broadcasted_iota(jnp.int32, (ROWS, LANES), 1)
    top, low = exact_sum(partial[:, 0, :], partial[:, 1, :], 0)
    gram = {}
    for n, pair in enumerate(PAIRS):
        values = [jnp.sum(jnp.where(lane[0:1] == n, row, 0.0), axis=1, keepdims=True) for row in (top, low)]
        gram[pair] = Pair(*values)
    weights, norms = cycle(gram)
    for n, norm in enumerate(norms):
        history[n] = jnp.max(norm)
    half = lane[:HALF]
    mine = (half >= HALO) & (half < HALO + OWN)
    low = jnp.where(mine, weights[0], weights[1])
    high = jnp.where(mine, weights[2], weights[3])

    def block(index, part):
        value = low * got[index, part] + high * got[index, 2 + part]
        return pltpu.roll(value, LANES - HALO, 1) + pltpu.roll(value, OWN - HALO, 1)

    for k in range(got.shape[0] // 2):
        for part in range(2):
            value = jnp.where(half < OWN, block(2 * k, part), block(2 * k + 1, part))
            solution[0, part * HALF : (part + 1) * HALF, k * LANES : (k + 1) * LANES] = value


def body(layers, strips, right_side, cell_terms, polynomial):
    f32 = jnp.float32
    peers = 2 * strips
    rows = ROWS * strips
    layer = ("c", "s")
    earlier = lax.ppermute(right_side, "z", [(i, i + 2) for i in range(layers - 2)])
    before = lax.ppermute(right_side, "z", [(i, i + 1) for i in range(layers - 1)])
    own = pl.pallas_call(
        own_kernel,
        out_shape=jax.ShapeDtypeStruct((peers, 7, HALF, LANES), f32),
        in_specs=[VMEM] * 2,
        out_specs=VMEM,
        compiler_params=PARAMS,
        cost_estimate=pl.CostEstimate(flops=1000000, bytes_accessed=4000000, transcendentals=0),
        name="own",
    )(right_side, cell_terms)
    sent = pl.pallas_call(
        pack_kernel,
        out_shape=jax.ShapeDtypeStruct((peers, 7, HALF, LANES), f32),
        in_specs=[VMEM] * 3,
        out_specs=VMEM,
        compiler_params=PARAMS,
        name="pack",
    )(own, before, earlier)
    got = lax.all_to_all(sent, layer, 0, 0, tiled=True)
    times = KRYLOV + 2
    field = lambda count: pltpu.VMEM((count, rows + 2 * PAD, LANES), f32)
    sent = pl.pallas_call(
        functools.partial(krylov_kernel, strips),
        out_shape=jax.ShapeDtypeStruct((peers, 5, HALF, LANES), f32),
        in_specs=[SMEM, VMEM],
        out_specs=VMEM,
        scratch_shapes=[pltpu.VMEM((5, rows, LANES), f32)]
        + [field(times - j) for j in range(KRYLOV + 1)]
        + [field(times - j) for j in range(KRYLOV)]
        + [field(times), field(times)],
        compiler_params=PARAMS,
        name="krylov",
    )(polynomial, got)
    got = lax.all_to_all(sent, layer, 0, 0, tiled=True)
    partial = jnp.concatenate(exact_sum(got[:, 4, 0, :], got[:, 4, 1, :], 0))
    partial = jnp.broadcast_to(partial[None], (layers, 2, LANES))
    partial = lax.all_to_all(partial, "z", 0, 0, tiled=True)
    return pl.pallas_call(
        combine_kernel,
        out_shape=(jax.ShapeDtypeStruct(right_side.shape, f32), jax.ShapeDtypeStruct((KRYLOV,), f32)),
        in_specs=[VMEM, VMEM],
        out_specs=(VMEM, SMEM),
        compiler_params=PARAMS,
        name="combine",
    )(partial, got)


def solution(mesh):
    layers = mesh.shape["tm"] // 2
    strips = mesh.shape["space"]
    fine = Mesh(mesh.devices.reshape(layers, 2, strips), ("z", "c", "s"))
    in_specs = (P(("z", "c"), "s", None), P(None, "s", None), P())
    out_specs = (P(("z", "c"), "s", None), P())
    return jax.shard_map(
        functools.partial(body, layers, strips), mesh=fine, in_specs=in_specs, out_specs=out_specs, check_vma=False
    )
```

```python
import functools

import jax
import jax.numpy as jnp
from jax import lax
from jax.experimental import pallas as pl
from jax.experimental.pallas import tpu as pltpu
from jax.sharding import Mesh, PartitionSpec as P

KRYLOV = 4
OWN = 64
HALO = 16
WIDE = OWN + 2 * HALO
HALF = 4
LANES = 128
ROWS = 8
PAD = 8
CHUNK = 64
PAIRS = [(i, j) for i in range(KRYLOV + 1) for j in range(i, KRYLOV + 1)]
VMEM = pl.BlockSpec(memory_space=pltpu.VMEM)
SMEM = pl.BlockSpec(memory_space=pltpu.SMEM)
PARAMS = pltpu.CompilerParams(vmem_limit_bytes=40 * 1024 * 1024)


def tiles_of(source):
    return [source[:, k * LANES : (k + 1) * LANES] for k in range(source.shape[1] // LANES)]


def windows(tiles, lane):
    zero = jnp.zeros_like(tiles[0])
    even = [zero] + [pltpu.roll(tile, HALO, 1) for tile in tiles]
    odd = [pltpu.roll(tile, LANES - OWN + HALO, 1) for tile in tiles] + [zero]
    out = []
    for k in range(len(tiles)):
        out.append(jnp.where(lane < HALO, even[k], even[k + 1]))
        out.append(jnp.where(lane < LANES - OWN + HALO, odd[k], odd[k + 1]))
    return out


def riders(tiles, lane):
    zero = jnp.zeros_like(tiles[0])
    turned = {shift: [pltpu.roll(tile, shift, 1) for tile in tiles] for shift in (16, 48, 80, 112)}
    edge = [zero] + turned[112] + [zero]
    out = []
    for k in range(len(tiles)):
        out.append([jnp.where(lane < 112, edge[k], edge[k + 1]), turned[80][k], turned[48][k]])
        out.append([turned[48][k], turned[16][k], jnp.where(lane < 112, edge[k + 1], edge[k + 2])])
    return out


def put(out, peer, plane, value):
    out[peer, 2 * plane] = value[:HALF]
    out[peer, 2 * plane + 1] = value[HALF:]


def own_kernel(now, terms, out):
    core = lax.axis_index("c")
    lane = lax.broadcasted_iota(jnp.int32, (ROWS, LANES), 1)
    fields = windows(tiles_of(now.at[0]), lane)
    parts = riders(tiles_of(terms.at[2 * core]), lane)
    across = windows(tiles_of(terms.at[1]), lane)
    upper = (lane >= 0) & (core == 0)
    for peer, (field, part, drift) in enumerate(zip(fields, parts, across)):
        put(out, peer, 0, jnp.where(lane < WIDE, field, part[0]))
        put(out, peer, 1, part[1])
        put(out, peer, 2, part[2])
        out[peer, 6] = jnp.where(upper[:HALF], drift[:HALF], drift[HALF:])


def pack_kernel(own, before, earlier, out):
    lane = lax.broadcasted_iota(jnp.int32, (ROWS, LANES), 1)
    narrow = lane[:HALF] < WIDE
    for peer in range(out.shape[0]):
        for half in (0, 1, 6):
            out[peer, half] = own[peer, half]
    for plane, source in ((1, before), (2, earlier)):
        for peer, window in enumerate(windows(tiles_of(source.at[0]), lane)):
            out[peer, 2 * plane] = jnp.where(narrow, window[:HALF], own[peer, 2 * plane])
            out[peer, 2 * plane + 1] = jnp.where(narrow, window[HALF:], own[peer, 2 * plane + 1])


def two_sum(a, b):
    total = a + b
    moved = total - a
    return total, (a - (total - moved)) + (b - moved)


def split(a):
    scaled = 4097.0 * a
    upper = scaled - (scaled - a)
    return upper, a - upper


def exact_sum(top, low, axis):
    quantum = 1024.0 * jnp.max(jnp.abs(top), axis=axis, keepdims=True)
    upper = (top + quantum) - quantum
    rest = (top - upper) + low
    return jnp.sum(upper, axis=axis, keepdims=True), jnp.sum(rest, axis=axis, keepdims=True)


class Pair:
    def __init__(self, top, low):
        self.top = top + low
        self.low = low - (self.top - top)
        self.parts = split(self.top)

    def times(self, other):
        value = self.top * other.top
        (a, b), (c, d) = self.parts, other.parts
        error = (((a * c - value) + a * d) + b * c) + b * d
        return Pair(value, error + (self.top * other.low + self.low * other.top))

    def minus(self, other):
        value, error = two_sum(self.top, -other.top)
        return Pair(value, error + (self.low - other.low))

    def inverse(self):
        guess = 1.0 / self.top
        value = guess * self.top
        (a, b), (c, d) = split(guess), self.parts
        error = (((a * c - value) + a * d) + b * c) + b * d
        return Pair(guess, guess * (((1.0 - value) - error) - guess * self.low))


def krylov_kernel(strips, polynomial, got, out, coef, inner_coef, k0, k1, k2, k3, k4, z1, z2, z3, z4, work_x, work_y):
    rows = ROWS * strips
    times = KRYLOV + 2
    krylov = [k0, k1, k2, k3, k4]
    lifted = [z1, z2, z3, z4]
    lane = lax.broadcasted_iota(jnp.int32, (ROWS, LANES), 1)
    sub = lax.broadcasted_iota(jnp.int32, (ROWS, LANES), 0)
    block = lax.axis_index("c") * strips + lax.axis_index("s")
    first_col = (block == 0) & (lane == HALO)
    last_col = (block == 2 * strips - 1) & (lane == HALO + OWN - 1)

    edge = jnp.zeros((PAD, LANES), jnp.float32)
    for ref in krylov + lifted + [work_x, work_y]:
        for t in range(ref.shape[0]):
            ref[t, 0:PAD] = edge
            ref[t, PAD + rows :] = edge

    for s in range(strips):
        for c in range(2):
            peer = c * strips + s
            at = PAD + s * ROWS
            for plane in range(3):
                k0[times - 2 + c - 2 * plane, at : at + HALF] = got[peer, 2 * plane]
                k0[times - 2 + c - 2 * plane, at + HALF : at + ROWS] = got[peer, 2 * plane + 1]
            coef[3, s * ROWS + c * HALF : s * ROWS + (c + 1) * HALF] = got[peer, 6]

    def rider(at, c):
        last = [pltpu.roll(k0[times - 2 + c - 2 * plane, at], 32 * (plane + 1), 1) for plane in range(3)]
        last[2] = jnp.where(lane < WIDE, last[2], 0.0)
        return jnp.where(lane < 32, last[0], jnp.where(lane < 64, last[1], last[2]))

    for s in range(strips):
        there = slice(s * ROWS, (s + 1) * ROWS)
        inner = slice(PAD + s * ROWS, PAD + (s + 1) * ROWS)
        diffuse = rider(inner, 0)
        half_x = 0.5 * coef[3, there]
        half_y = 0.5 * rider(inner, 1)
        north = -diffuse - half_y
        south = half_y - diffuse
        if s == 0:
            north = jnp.where(sub == 0, 0.0, north)
        if s == strips - 1:
            south = jnp.where(sub == ROWS - 1, 0.0, south)
        coef[0, there] = 1.0 + 4.0 * diffuse
        coef[1, there] = north
        coef[2, there] = south
        coef[3, there] = jnp.where(first_col, 0.0, -diffuse - half_x)
        coef[4, there] = jnp.where(last_col, 0.0, half_x - diffuse)
        for i in range(5):
            scaled = polynomial[3] * coef[i, there]
            inner_coef[i, there] = polynomial[2] + scaled if i == 0 else scaled

    def sweep(count, terms, apply):
        chunk = min(CHUNK, rows)
        for at in range(0, rows, chunk):
            parts = [terms[i, at : at + chunk] for i in range(5)]

            def stencil(ref, t):
                middle = ref[t, at + PAD : at + PAD + chunk]
                north = ref[t, at + PAD - 1 : at + PAD - 1 + chunk]
                south = ref[t, at + PAD + 1 : at + PAD + 1 + chunk]
                west = pltpu.roll(middle, 1, 1)
                east = pltpu.roll(middle, LANES - 1, 1)
                return (
                    (parts[0] * middle + parts[3] * west)
                    + (parts[1] * north + parts[2] * south)
                    + parts[4] * east
                )

            for t in range(count):
                apply(t, slice(at + PAD, at + PAD + chunk), stencil)

    for j in range(KRYLOV):
        source, target, upper = krylov[j], krylov[j + 1], lifted[j]
        count = times - j

        def first(t, at, stencil):
            work_x[t, at] = stencil(source, t)

        def second(t, at, stencil):
            work_y[t, at] = polynomial[1] * source[t, at] + stencil(work_x, t)

        def third(t, at, stencil):
            upper[t, at] = polynomial[0] * source[t, at] + stencil(work_y, t)

        def fourth(t, at, stencil):
            target[t, at] = stencil(upper, t + 1) - upper[t, at] - source[t + 1, at]

        sweep(count, inner_coef, first)
        sweep(count, coef, second)
        sweep(count, coef, third)
        sweep(count - 1, coef, fourth)

    mine = (lane >= HALO) & (lane < HALO + OWN)
    nothing = jnp.zeros((ROWS, LANES), jnp.float32)

    def gram(index, sums):
        at = slice(PAD + index * ROWS, PAD + (index + 1) * ROWS)
        vectors = []
        for ref in krylov:
            newest = pltpu.roll(ref[ref.shape[0] - 1, at], OWN, 1)
            value = jnp.where(mine, ref[ref.shape[0] - 2, at], newest)
            vectors.append((value,) + split(value))
        out = []
        for (i, j), (top, low) in zip(PAIRS, sums):
            (_, upper, lower), (other, other_upper, other_lower) = vectors[i], vectors[j]
            top, error = two_sum(top, upper * other_upper)
            out.append((top, low + (error + (upper * other_lower + lower * other))))
        return out

    sums = [(nothing, nothing) for _ in PAIRS]
    for index in range(strips):
        sums = gram(index, sums)
    tops = [nothing, nothing]
    lows = [nothing, nothing]
    for n, (top, low) in enumerate(sums):
        for shift in (4, 2, 1):
            top, error = two_sum(top, pltpu.roll(top, shift, 0))
            low = low + pltpu.roll(low, shift, 0) + error
        tops[n // ROWS] = jnp.where(sub == n % ROWS, top, tops[n // ROWS])
        lows[n // ROWS] = jnp.where(sub == n % ROWS, low, lows[n // ROWS])
    packed = [nothing, nothing]
    for n in range(2):
        parts = exact_sum(tops[n], lows[n], 1)
        for kind in range(2):
            packed[kind] = jnp.where(lane == sub + n * ROWS, parts[kind], packed[kind])
    packed = [jnp.sum(value, axis=0, keepdims=True) for value in packed]
    packed = jnp.where(sub[:HALF] == 0, packed[0], jnp.where(sub[:HALF] == 1, packed[1], 0.0))

    for c in range(2):
        for s in range(strips):
            peer = c * strips + s
            at = slice(PAD + s * ROWS, PAD + (s + 1) * ROWS)
            for pair in range(2):
                low = lifted[2 * pair]
                high = lifted[2 * pair + 1]
                turned = pltpu.roll(high[high.shape[0] - 2 + c, at], OWN, 1)
                put(out, peer, pair, jnp.where(mine, low[low.shape[0] - 2 + c, at], turned))
            out[peer, 4] = packed


def least_squares(columns, beta_norm):
    num_columns = len(columns)
    cosines = []
    sines = []
    target = [beta_norm] + [jnp.zeros_like(beta_norm) for position in range(num_columns)]
    history = []
    triangle = []
    for column_at in range(num_columns):
        column = list(columns[column_at])
        for earlier in range(column_at):
            first_entry = column[earlier]
            second_entry = column[earlier + 1]
            column[earlier] = cosines[earlier] * first_entry + sines[earlier] * second_entry
            column[earlier + 1] = cosines[earlier] * second_entry - sines[earlier] * first_entry
        radius = jnp.sqrt(
            column[column_at] * column[column_at] + column[column_at + 1] * column[column_at + 1]
        )
        cosine = column[column_at] / radius
        sine_part = column[column_at + 1] / radius
        column[column_at] = radius
        cosines.append(cosine)
        sines.append(sine_part)
        target[column_at + 1] = -sine_part * target[column_at]
        target[column_at] = cosine * target[column_at]
        history.append(jnp.abs(target[column_at + 1]))
        triangle.append(column[: column_at + 1])
    solved = [None for position in range(num_columns)]
    for row_at in reversed(range(num_columns)):
        running_sum = target[row_at]
        for later in range(row_at + 1, num_columns):
            running_sum = running_sum - triangle[later][row_at] * solved[later]
        solved[row_at] = running_sum / triangle[row_at][row_at]
    return (solved, history)


def cycle(gram):
    size = KRYLOV + 1
    floors = [1e-12 * gram[k, k].top + 1e-30 for k in range(size)]
    upper = {}
    for k in range(size):
        pivot = jnp.maximum(gram[k, k].top, floors[k])
        root = jnp.sqrt(pivot)
        upper[k, k] = root
        for j in range(k + 1, size):
            upper[k, j] = gram[k, j].top / root
        if k + 1 < size:
            inverse = Pair(pivot, jnp.where(gram[k, k].top < floors[k], 0.0, gram[k, k].low)).inverse()
            for i in range(k + 1, size):
                factor = gram[k, i].times(inverse)
                for j in range(i, size):
                    gram[i, j] = gram[i, j].minus(factor.times(gram[k, j]))

    mapped = []
    for i in range(KRYLOV):
        column = []
        for row in range(i + 2):
            value = upper[row, i + 1]
            if row <= i:
                value = value + upper[row, i]
            for k in range(max(row - 1, 0), i):
                value = value - upper[k, i] * mapped[k][row]
            column.append(value / upper[i, i])
        mapped.append(column)

    beta_norm = upper[0, 0]
    basis = [[jnp.ones_like(beta_norm)]]
    columns = []
    for at in range(KRYLOV):
        newest = basis[-1]
        image = []
        for row in range(at + 2):
            terms = [mapped[i][row] * newest[i] for i in range(max(row - 1, 0), at + 1)]
            image.append(functools.reduce(lambda a, b: a + b, terms))
        projections = []
        rest = list(image)
        for vector in basis:
            terms = [a * b for a, b in zip(image, vector)]
            projections.append(functools.reduce(lambda a, b: a + b, terms))
        for vector, weight in zip(basis, projections):
            for row, value in enumerate(vector):
                rest[row] = rest[row] - weight * value
        terms = [value * value for value in rest]
        length = jnp.sqrt(functools.reduce(lambda a, b: a + b, terms) + 1e-06)
        columns.append(projections + [length])
        basis.append([value / length for value in rest])
    solved, history = least_squares(columns, beta_norm)
    weights = [None] * KRYLOV
    for row in reversed(range(KRYLOV)):
        terms = [solved[j] * basis[j][row] for j in range(row, KRYLOV)]
        value = functools.reduce(lambda a, b: a + b, terms)
        for later in range(row + 1, KRYLOV):
            value = value - upper[row, later] * weights[later]
        weights[row] = value / upper[row, row]
    return weights, history


def combine_kernel(partial, got, solution, history):
    lane = lax.broadcasted_iota(jnp.int32, (ROWS, LANES), 1)
    top, low = exact_sum(partial[:, 0, :], partial[:, 1, :], 0)
    gram = {}
    for n, pair in enumerate(PAIRS):
        values = [jnp.sum(jnp.where(lane[0:1] == n, row, 0.0), axis=1, keepdims=True) for row in (top, low)]
        gram[pair] = Pair(*values)
    weights, norms = cycle(gram)
    for n, norm in enumerate(norms):
        history[n] = jnp.max(norm)
    half = lane[:HALF]
    mine = (half >= HALO) & (half < HALO + OWN)
    low = jnp.where(mine, weights[0], weights[1])
    high = jnp.where(mine, weights[2], weights[3])

    def block(index, part):
        value = low * got[index, part] + high * got[index, 2 + part]
        return pltpu.roll(value, LANES - HALO, 1) + pltpu.roll(value, OWN - HALO, 1)

    for k in range(got.shape[0] // 2):
        for part in range(2):
            value = jnp.where(half < OWN, block(2 * k, part), block(2 * k + 1, part))
            solution[0, part * HALF : (part + 1) * HALF, k * LANES : (k + 1) * LANES] = value


def body(layers, strips, right_side, cell_terms, polynomial):
    f32 = jnp.float32
    peers = 2 * strips
    rows = ROWS * strips
    layer = ("c", "s")
    earlier = lax.ppermute(right_side, "z", [(i, i + 2) for i in range(layers - 2)])
    before = lax.ppermute(right_side, "z", [(i, i + 1) for i in range(layers - 1)])
    own = pl.pallas_call(
        own_kernel,
        out_shape=jax.ShapeDtypeStruct((peers, 7, HALF, LANES), f32),
        in_specs=[VMEM] * 2,
        out_specs=VMEM,
        compiler_params=PARAMS,
        cost_estimate=pl.CostEstimate(flops=1000000, bytes_accessed=4000000, transcendentals=0),
        name="own",
    )(right_side, cell_terms)
    sent = pl.pallas_call(
        pack_kernel,
        out_shape=jax.ShapeDtypeStruct((peers, 7, HALF, LANES), f32),
        in_specs=[VMEM] * 3,
        out_specs=VMEM,
        compiler_params=PARAMS,
        name="pack",
    )(own, before, earlier)
    got = lax.all_to_all(sent, layer, 0, 0, tiled=True)
    times = KRYLOV + 2
    field = lambda count: pltpu.VMEM((count, rows + 2 * PAD, LANES), f32)
    sent = pl.pallas_call(
        functools.partial(krylov_kernel, strips),
        out_shape=jax.ShapeDtypeStruct((peers, 5, HALF, LANES), f32),
        in_specs=[SMEM, VMEM],
        out_specs=VMEM,
        scratch_shapes=[pltpu.VMEM((5, rows, LANES), f32)] * 2
        + [field(times - j) for j in range(KRYLOV + 1)]
        + [field(times - j) for j in range(KRYLOV)]
        + [field(times), field(times)],
        compiler_params=PARAMS,
        name="krylov",
    )(polynomial, got)
    got = lax.all_to_all(sent, layer, 0, 0, tiled=True)
    partial = jnp.concatenate(exact_sum(got[:, 4, 0, :], got[:, 4, 1, :], 0))
    partial = jnp.broadcast_to(partial[None], (layers, 2, LANES))
    partial = lax.all_to_all(partial, "z", 0, 0, tiled=True)
    return pl.pallas_call(
        combine_kernel,
        out_shape=(jax.ShapeDtypeStruct(right_side.shape, f32), jax.ShapeDtypeStruct((KRYLOV,), f32)),
        in_specs=[VMEM, VMEM],
        out_specs=(VMEM, SMEM),
        compiler_params=PARAMS,
        name="combine",
    )(partial, got)


def solution(mesh):
    layers = mesh.shape["tm"] // 2
    strips = mesh.shape["space"]
    fine = Mesh(mesh.devices.reshape(layers, 2, strips), ("z", "c", "s"))
    in_specs = (P(("z", "c"), "s", None), P(None, "s", None), P())
    out_specs = (P(("z", "c"), "s", None), P())
    return jax.shard_map(
        functools.partial(body, layers, strips), mesh=fine, in_specs=in_specs, out_specs=out_specs, check_vma=False
    )
```

```python
import functools

import jax
import jax.numpy as jnp
from jax import lax
from jax.experimental import pallas as pl
from jax.experimental.pallas import tpu as pltpu
from jax.sharding import Mesh, PartitionSpec as P

KRYLOV = 4
OWN = 64
HALO = 16
WIDE = OWN + 2 * HALO
HALF = 4
LANES = 128
ROWS = 8
PAD = 8
CHUNK = 64
PAIRS = [(i, j) for i in range(KRYLOV + 1) for j in range(i, KRYLOV + 1)]
VMEM = pl.BlockSpec(memory_space=pltpu.VMEM)
SMEM = pl.BlockSpec(memory_space=pltpu.SMEM)
PARAMS = pltpu.CompilerParams(vmem_limit_bytes=40 * 1024 * 1024)


def tiles_of(source):
    return [source[:, k * LANES : (k + 1) * LANES] for k in range(source.shape[1] // LANES)]


def windows(tiles, lane):
    zero = jnp.zeros_like(tiles[0])
    even = [zero] + [pltpu.roll(tile, HALO, 1) for tile in tiles]
    odd = [pltpu.roll(tile, LANES - OWN + HALO, 1) for tile in tiles] + [zero]
    out = []
    for k in range(len(tiles)):
        out.append(jnp.where(lane < HALO, even[k], even[k + 1]))
        out.append(jnp.where(lane < LANES - OWN + HALO, odd[k], odd[k + 1]))
    return out


def riders(tiles, lane):
    zero = jnp.zeros_like(tiles[0])
    turned = {shift: [pltpu.roll(tile, shift, 1) for tile in tiles] for shift in (16, 48, 80, 112)}
    edge = [zero] + turned[112] + [zero]
    out = []
    for k in range(len(tiles)):
        out.append([jnp.where(lane < 112, edge[k], edge[k + 1]), turned[80][k], turned[48][k]])
        out.append([turned[48][k], turned[16][k], jnp.where(lane < 112, edge[k + 1], edge[k + 2])])
    return out


def put(out, peer, plane, value):
    out[peer, 2 * plane] = value[:HALF]
    out[peer, 2 * plane + 1] = value[HALF:]


def own_kernel(now, terms, out):
    core = lax.axis_index("c")
    lane = lax.broadcasted_iota(jnp.int32, (ROWS, LANES), 1)
    fields = windows(tiles_of(now.at[0]), lane)
    parts = riders(tiles_of(terms.at[2 * core]), lane)
    across = windows(tiles_of(terms.at[1]), lane)
    upper = (lane >= 0) & (core == 0)
    for peer, (field, part, drift) in enumerate(zip(fields, parts, across)):
        put(out, peer, 0, jnp.where(lane < WIDE, field, part[0]))
        put(out, peer, 1, part[1])
        put(out, peer, 2, part[2])
        out[peer, 6] = jnp.where(upper[:HALF], drift[:HALF], drift[HALF:])


def pack_kernel(own, before, earlier, out):
    lane = lax.broadcasted_iota(jnp.int32, (ROWS, LANES), 1)
    narrow = lane[:HALF] < WIDE
    for peer in range(out.shape[0]):
        for half in (0, 1, 6):
            out[peer, half] = own[peer, half]
    for plane, source in ((1, before), (2, earlier)):
        for peer, window in enumerate(windows(tiles_of(source.at[0]), lane)):
            out[peer, 2 * plane] = jnp.where(narrow, window[:HALF], own[peer, 2 * plane])
            out[peer, 2 * plane + 1] = jnp.where(narrow, window[HALF:], own[peer, 2 * plane + 1])


def two_sum(a, b):
    total = a + b
    moved = total - a
    return total, (a - (total - moved)) + (b - moved)


def split(a):
    scaled = 4097.0 * a
    upper = scaled - (scaled - a)
    return upper, a - upper


def exact_sum(top, low, axis):
    quantum = 1024.0 * jnp.max(jnp.abs(top), axis=axis, keepdims=True)
    upper = (top + quantum) - quantum
    rest = (top - upper) + low
    return jnp.sum(upper, axis=axis, keepdims=True), jnp.sum(rest, axis=axis, keepdims=True)


class Pair:
    def __init__(self, top, low):
        self.top = top + low
        self.low = low - (self.top - top)
        self.parts = split(self.top)

    def times(self, other):
        value = self.top * other.top
        (a, b), (c, d) = self.parts, other.parts
        error = (((a * c - value) + a * d) + b * c) + b * d
        return Pair(value, error + (self.top * other.low + self.low * other.top))

    def minus(self, other):
        value, error = two_sum(self.top, -other.top)
        return Pair(value, error + (self.low - other.low))

    def inverse(self):
        guess = 1.0 / self.top
        value = guess * self.top
        (a, b), (c, d) = split(guess), self.parts
        error = (((a * c - value) + a * d) + b * c) + b * d
        return Pair(guess, guess * (((1.0 - value) - error) - guess * self.low))


def krylov_kernel(strips, polynomial, got, out, coef, inner_coef, k0, k1, k2, k3, k4, z1, z2, z3, z4, work_x, work_y):
    rows = ROWS * strips
    times = KRYLOV + 2
    krylov = [k0, k1, k2, k3, k4]
    lifted = [z1, z2, z3, z4]
    lane = lax.broadcasted_iota(jnp.int32, (ROWS, LANES), 1)
    sub = lax.broadcasted_iota(jnp.int32, (ROWS, LANES), 0)
    block = lax.axis_index("c") * strips + lax.axis_index("s")
    first_col = (block == 0) & (lane == HALO)
    last_col = (block == 2 * strips - 1) & (lane == HALO + OWN - 1)

    edge = jnp.zeros((PAD, LANES), jnp.float32)
    for ref in krylov + lifted + [work_x, work_y]:
        for t in range(ref.shape[0]):
            ref[t, 0:PAD] = edge
            ref[t, PAD + rows :] = edge

    for s in range(strips):
        for c in range(2):
            peer = c * strips + s
            at = PAD + s * ROWS
            for plane in range(3):
                k0[times - 2 + c - 2 * plane, at : at + HALF] = got[peer, 2 * plane]
                k0[times - 2 + c - 2 * plane, at + HALF : at + ROWS] = got[peer, 2 * plane + 1]
            coef[3, s * ROWS + c * HALF : s * ROWS + (c + 1) * HALF] = got[peer, 6]

    def rider(at, c):
        last = [pltpu.roll(k0[times - 2 + c - 2 * plane, at], 32 * (plane + 1), 1) for plane in range(3)]
        last[2] = jnp.where(lane < WIDE, last[2], 0.0)
        return jnp.where(lane < 32, last[0], jnp.where(lane < 64, last[1], last[2]))

    for s in range(strips):
        there = slice(s * ROWS, (s + 1) * ROWS)
        inner = slice(PAD + s * ROWS, PAD + (s + 1) * ROWS)
        diffuse = rider(inner, 0)
        half_x = 0.5 * coef[3, there]
        half_y = 0.5 * rider(inner, 1)
        north = -diffuse - half_y
        south = half_y - diffuse
        if s == 0:
            north = jnp.where(sub == 0, 0.0, north)
        if s == strips - 1:
            south = jnp.where(sub == ROWS - 1, 0.0, south)
        coef[0, there] = 1.0 + 4.0 * diffuse
        coef[1, there] = north
        coef[2, there] = south
        coef[3, there] = jnp.where(first_col, 0.0, -diffuse - half_x)
        coef[4, there] = jnp.where(last_col, 0.0, half_x - diffuse)
        for i in range(5):
            scaled = polynomial[3] * coef[i, there]
            inner_coef[i, there] = polynomial[2] + scaled if i == 0 else scaled

    def sweep(count, terms, apply):
        chunk = min(CHUNK, rows)
        for at in range(0, rows, chunk):
            parts = [terms[i, at : at + chunk] for i in range(5)]

            def stencil(ref, t):
                middle = ref[t, at + PAD : at + PAD + chunk]
                north = ref[t, at + PAD - 1 : at + PAD - 1 + chunk]
                south = ref[t, at + PAD + 1 : at + PAD + 1 + chunk]
                west = pltpu.roll(middle, 1, 1)
                east = pltpu.roll(middle, LANES - 1, 1)
                return (
                    (parts[0] * middle + parts[3] * west)
                    + (parts[1] * north + parts[2] * south)
                    + parts[4] * east
                )

            for t in range(count):
                apply(t, slice(at + PAD, at + PAD + chunk), stencil)

    for j in range(KRYLOV):
        source, target, upper = krylov[j], krylov[j + 1], lifted[j]
        count = times - j

        def first(t, at, stencil):
            work_x[t, at] = stencil(source, t)

        def second(t, at, stencil):
            work_y[t, at] = polynomial[1] * source[t, at] + stencil(work_x, t)

        def third(t, at, stencil):
            upper[t, at] = polynomial[0] * source[t, at] + stencil(work_y, t)

        def fourth(t, at, stencil):
            target[t, at] = stencil(upper, t + 1) - upper[t, at] - source[t + 1, at]

        sweep(count, inner_coef, first)
        sweep(count, coef, second)
        sweep(count, coef, third)
        sweep(count - 1, coef, fourth)

    mine = (lane >= HALO) & (lane < HALO + OWN)
    nothing = jnp.zeros((ROWS, LANES), jnp.float32)

    def gram(index, sums):
        at = slice(PAD + index * ROWS, PAD + (index + 1) * ROWS)
        vectors = []
        for ref in krylov:
            newest = pltpu.roll(ref[ref.shape[0] - 1, at], OWN, 1)
            value = jnp.where(mine, ref[ref.shape[0] - 2, at], newest)
            vectors.append((value,) + split(value))
        out = []
        for (i, j), (top, low) in zip(PAIRS, sums):
            (_, upper, lower), (other, other_upper, other_lower) = vectors[i], vectors[j]
            top, error = two_sum(top, upper * other_upper)
            out.append((top, low + (error + (upper * other_lower + lower * other))))
        return out

    sums = [(nothing, nothing) for _ in PAIRS]
    for index in range(strips):
        sums = gram(index, sums)
    tops = [nothing, nothing]
    lows = [nothing, nothing]
    for n, (top, low) in enumerate(sums):
        for shift in (4, 2, 1):
            top, error = two_sum(top, pltpu.roll(top, shift, 0))
            low = low + pltpu.roll(low, shift, 0) + error
        tops[n // ROWS] = jnp.where(sub == n % ROWS, top, tops[n // ROWS])
        lows[n // ROWS] = jnp.where(sub == n % ROWS, low, lows[n // ROWS])
    packed = [nothing, nothing]
    for n in range(2):
        parts = exact_sum(tops[n], lows[n], 1)
        for kind in range(2):
            packed[kind] = jnp.where(lane == sub + n * ROWS, parts[kind], packed[kind])
    packed = [jnp.sum(value, axis=0, keepdims=True) for value in packed]
    packed = jnp.where(sub[:HALF] == 0, packed[0], jnp.where(sub[:HALF] == 1, packed[1], 0.0))

    for c in range(2):
        for s in range(strips):
            peer = c * strips + s
            at = slice(PAD + s * ROWS, PAD + (s + 1) * ROWS)
            for pair in range(2):
                low = lifted[2 * pair]
                high = lifted[2 * pair + 1]
                turned = pltpu.roll(high[high.shape[0] - 2 + c, at], OWN, 1)
                put(out, peer, pair, jnp.where(mine, low[low.shape[0] - 2 + c, at], turned))
            out[peer, 4] = packed


def least_squares(columns, beta_norm):
    num_columns = len(columns)
    cosines = []
    sines = []
    target = [beta_norm] + [jnp.zeros_like(beta_norm) for position in range(num_columns)]
    history = []
    triangle = []
    for column_at in range(num_columns):
        column = list(columns[column_at])
        for earlier in range(column_at):
            first_entry = column[earlier]
            second_entry = column[earlier + 1]
            column[earlier] = cosines[earlier] * first_entry + sines[earlier] * second_entry
            column[earlier + 1] = cosines[earlier] * second_entry - sines[earlier] * first_entry
        radius = jnp.sqrt(
            column[column_at] * column[column_at] + column[column_at + 1] * column[column_at + 1]
        )
        cosine = column[column_at] / radius
        sine_part = column[column_at + 1] / radius
        column[column_at] = radius
        cosines.append(cosine)
        sines.append(sine_part)
        target[column_at + 1] = -sine_part * target[column_at]
        target[column_at] = cosine * target[column_at]
        history.append(jnp.abs(target[column_at + 1]))
        triangle.append(column[: column_at + 1])
    solved = [None for position in range(num_columns)]
    for row_at in reversed(range(num_columns)):
        running_sum = target[row_at]
        for later in range(row_at + 1, num_columns):
            running_sum = running_sum - triangle[later][row_at] * solved[later]
        solved[row_at] = running_sum / triangle[row_at][row_at]
    return (solved, history)


def cycle(gram):
    size = KRYLOV + 1
    floors = [1e-12 * gram[k, k].top + 1e-30 for k in range(size)]
    upper = {}
    for k in range(size):
        pivot = jnp.maximum(gram[k, k].top, floors[k])
        root = jnp.sqrt(pivot)
        upper[k, k] = root
        for j in range(k + 1, size):
            upper[k, j] = gram[k, j].top / root
        if k + 1 < size:
            inverse = Pair(pivot, jnp.where(gram[k, k].top < floors[k], 0.0, gram[k, k].low)).inverse()
            for i in range(k + 1, size):
                factor = gram[k, i].times(inverse)
                for j in range(i, size):
                    gram[i, j] = gram[i, j].minus(factor.times(gram[k, j]))

    mapped = []
    for i in range(KRYLOV):
        column = []
        for row in range(i + 2):
            value = upper[row, i + 1]
            if row <= i:
                value = value + upper[row, i]
            for k in range(max(row - 1, 0), i):
                value = value - upper[k, i] * mapped[k][row]
            column.append(value / upper[i, i])
        mapped.append(column)

    beta_norm = upper[0, 0]
    basis = [[jnp.ones_like(beta_norm)]]
    columns = []
    for at in range(KRYLOV):
        newest = basis[-1]
        image = []
        for row in range(at + 2):
            terms = [mapped[i][row] * newest[i] for i in range(max(row - 1, 0), at + 1)]
            image.append(functools.reduce(lambda a, b: a + b, terms))
        projections = []
        rest = list(image)
        for vector in basis:
            terms = [a * b for a, b in zip(image, vector)]
            projections.append(functools.reduce(lambda a, b: a + b, terms))
        for vector, weight in zip(basis, projections):
            for row, value in enumerate(vector):
                rest[row] = rest[row] - weight * value
        terms = [value * value for value in rest]
        length = jnp.sqrt(functools.reduce(lambda a, b: a + b, terms) + 1e-06)
        columns.append(projections + [length])
        basis.append([value / length for value in rest])
    solved, history = least_squares(columns, beta_norm)
    weights = [None] * KRYLOV
    for row in reversed(range(KRYLOV)):
        terms = [solved[j] * basis[j][row] for j in range(row, KRYLOV)]
        value = functools.reduce(lambda a, b: a + b, terms)
        for later in range(row + 1, KRYLOV):
            value = value - upper[row, later] * weights[later]
        weights[row] = value / upper[row, row]
    return weights, history


def combine_kernel(partial, got, solution, history):
    lane = lax.broadcasted_iota(jnp.int32, (ROWS, LANES), 1)
    top, low = exact_sum(partial[:, 0, :], partial[:, 1, :], 0)
    gram = {}
    for n, pair in enumerate(PAIRS):
        values = [jnp.sum(jnp.where(lane[0:1] == n, row, 0.0), axis=1, keepdims=True) for row in (top, low)]
        gram[pair] = Pair(*values)
    weights, norms = cycle(gram)
    for n, norm in enumerate(norms):
        history[n] = jnp.max(norm)
    half = lane[:HALF]
    mine = (half >= HALO) & (half < HALO + OWN)
    low = jnp.where(mine, weights[0], weights[1])
    high = jnp.where(mine, weights[2], weights[3])

    def block(index, part):
        value = low * got[index, part] + high * got[index, 2 + part]
        return pltpu.roll(value, LANES - HALO, 1) + pltpu.roll(value, OWN - HALO, 1)

    for k in range(got.shape[0] // 2):
        for part in range(2):
            value = jnp.where(half < OWN, block(2 * k, part), block(2 * k + 1, part))
            solution[0, part * HALF : (part + 1) * HALF, k * LANES : (k + 1) * LANES] = value


def body(layers, strips, right_side, cell_terms, polynomial):
    f32 = jnp.float32
    peers = 2 * strips
    rows = ROWS * strips
    layer = ("c", "s")
    earlier = lax.ppermute(right_side, "z", [(i, i + 2) for i in range(layers - 2)])
    before = lax.ppermute(right_side, "z", [(i, i + 1) for i in range(layers - 1)])
    own = pl.pallas_call(
        own_kernel,
        out_shape=jax.ShapeDtypeStruct((peers, 7, HALF, LANES), f32),
        in_specs=[VMEM] * 2,
        out_specs=VMEM,
        compiler_params=PARAMS,
        cost_estimate=pl.CostEstimate(flops=1000000, bytes_accessed=4000000, transcendentals=0),
        name="own",
    )(right_side, cell_terms)
    sent = pl.pallas_call(
        pack_kernel,
        out_shape=jax.ShapeDtypeStruct((peers, 7, HALF, LANES), f32),
        in_specs=[VMEM] * 3,
        out_specs=VMEM,
        compiler_params=PARAMS,
        name="pack",
    )(own, before, earlier)
    got = lax.all_to_all(sent, layer, 0, 0, tiled=True)
    times = KRYLOV + 2
    field = lambda count: pltpu.VMEM((count, rows + 2 * PAD, LANES), f32)
    sent = pl.pallas_call(
        functools.partial(krylov_kernel, strips),
        out_shape=jax.ShapeDtypeStruct((peers, 5, HALF, LANES), f32),
        in_specs=[SMEM, VMEM],
        out_specs=VMEM,
        scratch_shapes=[pltpu.VMEM((5, rows, LANES), f32)] * 2
        + [field(times - j) for j in range(KRYLOV + 1)]
        + [field(times - j) for j in range(KRYLOV)]
        + [field(times), field(times)],
        compiler_params=PARAMS,
        name="krylov",
    )(polynomial, got)
    got = lax.all_to_all(sent, layer, 0, 0, tiled=True)
    partial = jnp.concatenate(exact_sum(got[:, 4, 0, :], got[:, 4, 1, :], 0))
    partial = jnp.broadcast_to(partial[None], (layers, 2, LANES))
    order = [(layers // 2 + i) % layers for i in range(layers)]
    partial = lax.all_to_all(partial, "z", 0, 0, axis_index_groups=[order], tiled=True)
    return pl.pallas_call(
        combine_kernel,
        out_shape=(jax.ShapeDtypeStruct(right_side.shape, f32), jax.ShapeDtypeStruct((KRYLOV,), f32)),
        in_specs=[VMEM, VMEM],
        out_specs=(VMEM, SMEM),
        compiler_params=PARAMS,
        name="combine",
    )(partial, got)


def solution(mesh):
    layers = mesh.shape["tm"] // 2
    strips = mesh.shape["space"]
    fine = Mesh(mesh.devices.reshape(layers, 2, strips), ("z", "c", "s"))
    in_specs = (P(("z", "c"), "s", None), P(None, "s", None), P())
    out_specs = (P(("z", "c"), "s", None), P())
    return jax.shard_map(
        functools.partial(body, layers, strips), mesh=fine, in_specs=in_specs, out_specs=out_specs, check_vma=False
    )
```

```python
import functools

import jax
import jax.numpy as jnp
from jax import lax
from jax.experimental import pallas as pl
from jax.experimental.pallas import tpu as pltpu
from jax.sharding import Mesh, PartitionSpec as P

KRYLOV = 4
OWN = 64
HALO = 16
WIDE = OWN + 2 * HALO
HALF = 4
LANES = 128
ROWS = 8
PAD = 8
CHUNK = 64
PAIRS = [(i, j) for i in range(KRYLOV + 1) for j in range(i, KRYLOV + 1)]
VMEM = pl.BlockSpec(memory_space=pltpu.VMEM)
SMEM = pl.BlockSpec(memory_space=pltpu.SMEM)
PARAMS = pltpu.CompilerParams(vmem_limit_bytes=40 * 1024 * 1024)


def first_of(strips):
    return strips // 2 + strips // 8


def place(device, strips):
    return (device - first_of(strips)) % (2 * strips)


def tiles_of(source):
    return [source[:, k * LANES : (k + 1) * LANES] for k in range(source.shape[1] // LANES)]


def windows(tiles, lane):
    zero = jnp.zeros_like(tiles[0])
    even = [zero] + [pltpu.roll(tile, HALO, 1) for tile in tiles]
    odd = [pltpu.roll(tile, LANES - OWN + HALO, 1) for tile in tiles] + [zero]
    out = []
    for k in range(len(tiles)):
        out.append(jnp.where(lane < HALO, even[k], even[k + 1]))
        out.append(jnp.where(lane < LANES - OWN + HALO, odd[k], odd[k + 1]))
    return out


def riders(tiles, lane):
    zero = jnp.zeros_like(tiles[0])
    turned = {shift: [pltpu.roll(tile, shift, 1) for tile in tiles] for shift in (16, 48, 80, 112)}
    edge = [zero] + turned[112] + [zero]
    out = []
    for k in range(len(tiles)):
        out.append([jnp.where(lane < 112, edge[k], edge[k + 1]), turned[80][k], turned[48][k]])
        out.append([turned[48][k], turned[16][k], jnp.where(lane < 112, edge[k + 1], edge[k + 2])])
    return out


def put(out, peer, plane, value):
    out[peer, 2 * plane] = value[:HALF]
    out[peer, 2 * plane + 1] = value[HALF:]


def own_kernel(now, terms, out):
    core = lax.axis_index("c")
    lane = lax.broadcasted_iota(jnp.int32, (ROWS, LANES), 1)
    fields = windows(tiles_of(now.at[0]), lane)
    parts = riders(tiles_of(terms.at[2 * core]), lane)
    across = windows(tiles_of(terms.at[1]), lane)
    upper = (lane >= 0) & (core == 0)
    for device, (field, part, drift) in enumerate(zip(fields, parts, across)):
        peer = place(device, out.shape[0] // 2)
        put(out, peer, 0, jnp.where(lane < WIDE, field, part[0]))
        put(out, peer, 1, part[1])
        put(out, peer, 2, part[2])
        out[peer, 6] = jnp.where(upper[:HALF], drift[:HALF], drift[HALF:])


def pack_kernel(own, before, earlier, out):
    lane = lax.broadcasted_iota(jnp.int32, (ROWS, LANES), 1)
    narrow = lane[:HALF] < WIDE
    for peer in range(out.shape[0]):
        for half in (0, 1, 6):
            out[peer, half] = own[peer, half]
    for plane, source in ((1, before), (2, earlier)):
        for device, window in enumerate(windows(tiles_of(source.at[0]), lane)):
            peer = place(device, out.shape[0] // 2)
            out[peer, 2 * plane] = jnp.where(narrow, window[:HALF], own[peer, 2 * plane])
            out[peer, 2 * plane + 1] = jnp.where(narrow, window[HALF:], own[peer, 2 * plane + 1])


def two_sum(a, b):
    total = a + b
    moved = total - a
    return total, (a - (total - moved)) + (b - moved)


def split(a):
    scaled = 4097.0 * a
    upper = scaled - (scaled - a)
    return upper, a - upper


def exact_sum(top, low, axis):
    quantum = 1024.0 * jnp.max(jnp.abs(top), axis=axis, keepdims=True)
    upper = (top + quantum) - quantum
    rest = (top - upper) + low
    return jnp.sum(upper, axis=axis, keepdims=True), jnp.sum(rest, axis=axis, keepdims=True)


class Pair:
    def __init__(self, top, low):
        self.top = top + low
        self.low = low - (self.top - top)
        self.parts = split(self.top)

    def times(self, other):
        value = self.top * other.top
        (a, b), (c, d) = self.parts, other.parts
        error = (((a * c - value) + a * d) + b * c) + b * d
        return Pair(value, error + (self.top * other.low + self.low * other.top))

    def minus(self, other):
        value, error = two_sum(self.top, -other.top)
        return Pair(value, error + (self.low - other.low))

    def inverse(self):
        guess = 1.0 / self.top
        value = guess * self.top
        (a, b), (c, d) = split(guess), self.parts
        error = (((a * c - value) + a * d) + b * c) + b * d
        return Pair(guess, guess * (((1.0 - value) - error) - guess * self.low))


def krylov_kernel(strips, polynomial, got, out, coef, inner_coef, k0, k1, k2, k3, k4, z1, z2, z3, z4, work_x, work_y):
    rows = ROWS * strips
    times = KRYLOV + 2
    krylov = [k0, k1, k2, k3, k4]
    lifted = [z1, z2, z3, z4]
    lane = lax.broadcasted_iota(jnp.int32, (ROWS, LANES), 1)
    sub = lax.broadcasted_iota(jnp.int32, (ROWS, LANES), 0)
    block = lax.axis_index("c") * strips + lax.axis_index("s")
    first_col = (block == 0) & (lane == HALO)
    last_col = (block == 2 * strips - 1) & (lane == HALO + OWN - 1)

    edge = jnp.zeros((PAD, LANES), jnp.float32)
    for ref in krylov + lifted + [work_x, work_y]:
        for t in range(ref.shape[0]):
            ref[t, 0:PAD] = edge
            ref[t, PAD + rows :] = edge

    for s in range(strips):
        for c in range(2):
            peer = place(c * strips + s, strips)
            at = PAD + s * ROWS
            for plane in range(3):
                k0[times - 2 + c - 2 * plane, at : at + HALF] = got[peer, 2 * plane]
                k0[times - 2 + c - 2 * plane, at + HALF : at + ROWS] = got[peer, 2 * plane + 1]
            coef[3, s * ROWS + c * HALF : s * ROWS + (c + 1) * HALF] = got[peer, 6]

    def rider(at, c):
        last = [pltpu.roll(k0[times - 2 + c - 2 * plane, at], 32 * (plane + 1), 1) for plane in range(3)]
        last[2] = jnp.where(lane < WIDE, last[2], 0.0)
        return jnp.where(lane < 32, last[0], jnp.where(lane < 64, last[1], last[2]))

    for s in range(strips):
        there = slice(s * ROWS, (s + 1) * ROWS)
        inner = slice(PAD + s * ROWS, PAD + (s + 1) * ROWS)
        diffuse = rider(inner, 0)
        half_x = 0.5 * coef[3, there]
        half_y = 0.5 * rider(inner, 1)
        north = -diffuse - half_y
        south = half_y - diffuse
        if s == 0:
            north = jnp.where(sub == 0, 0.0, north)
        if s == strips - 1:
            south = jnp.where(sub == ROWS - 1, 0.0, south)
        coef[0, there] = 1.0 + 4.0 * diffuse
        coef[1, there] = north
        coef[2, there] = south
        coef[3, there] = jnp.where(first_col, 0.0, -diffuse - half_x)
        coef[4, there] = jnp.where(last_col, 0.0, half_x - diffuse)
        for i in range(5):
            scaled = polynomial[3] * coef[i, there]
            inner_coef[i, there] = polynomial[2] + scaled if i == 0 else scaled

    def sweep(count, terms, apply):
        chunk = min(CHUNK, rows)
        for at in range(0, rows, chunk):
            parts = [terms[i, at : at + chunk] for i in range(5)]

            def stencil(ref, t):
                middle = ref[t, at + PAD : at + PAD + chunk]
                north = ref[t, at + PAD - 1 : at + PAD - 1 + chunk]
                south = ref[t, at + PAD + 1 : at + PAD + 1 + chunk]
                west = pltpu.roll(middle, 1, 1)
                east = pltpu.roll(middle, LANES - 1, 1)
                return (
                    (parts[0] * middle + parts[3] * west)
                    + (parts[1] * north + parts[2] * south)
                    + parts[4] * east
                )

            for t in range(count):
                apply(t, slice(at + PAD, at + PAD + chunk), stencil)

    for j in range(KRYLOV):
        source, target, upper = krylov[j], krylov[j + 1], lifted[j]
        count = times - j

        def first(t, at, stencil):
            work_x[t, at] = stencil(source, t)

        def second(t, at, stencil):
            work_y[t, at] = polynomial[1] * source[t, at] + stencil(work_x, t)

        def third(t, at, stencil):
            upper[t, at] = polynomial[0] * source[t, at] + stencil(work_y, t)

        def fourth(t, at, stencil):
            target[t, at] = stencil(upper, t + 1) - upper[t, at] - source[t + 1, at]

        sweep(count, inner_coef, first)
        sweep(count, coef, second)
        sweep(count, coef, third)
        sweep(count - 1, coef, fourth)

    mine = (lane >= HALO) & (lane < HALO + OWN)
    nothing = jnp.zeros((ROWS, LANES), jnp.float32)

    def gram(index, sums):
        at = slice(PAD + index * ROWS, PAD + (index + 1) * ROWS)
        vectors = []
        for ref in krylov:
            newest = pltpu.roll(ref[ref.shape[0] - 1, at], OWN, 1)
            value = jnp.where(mine, ref[ref.shape[0] - 2, at], newest)
            vectors.append((value,) + split(value))
        out = []
        for (i, j), (top, low) in zip(PAIRS, sums):
            (_, upper, lower), (other, other_upper, other_lower) = vectors[i], vectors[j]
            top, error = two_sum(top, upper * other_upper)
            out.append((top, low + (error + (upper * other_lower + lower * other))))
        return out

    sums = [(nothing, nothing) for _ in PAIRS]
    for index in range(strips):
        sums = gram(index, sums)
    tops = [nothing, nothing]
    lows = [nothing, nothing]
    for n, (top, low) in enumerate(sums):
        for shift in (4, 2, 1):
            top, error = two_sum(top, pltpu.roll(top, shift, 0))
            low = low + pltpu.roll(low, shift, 0) + error
        tops[n // ROWS] = jnp.where(sub == n % ROWS, top, tops[n // ROWS])
        lows[n // ROWS] = jnp.where(sub == n % ROWS, low, lows[n // ROWS])
    packed = [nothing, nothing]
    for n in range(2):
        parts = exact_sum(tops[n], lows[n], 1)
        for kind in range(2):
            packed[kind] = jnp.where(lane == sub + n * ROWS, parts[kind], packed[kind])
    packed = [jnp.sum(value, axis=0, keepdims=True) for value in packed]
    packed = jnp.where(sub[:HALF] == 0, packed[0], jnp.where(sub[:HALF] == 1, packed[1], 0.0))

    for c in range(2):
        for s in range(strips):
            peer = place(c * strips + s, strips)
            at = slice(PAD + s * ROWS, PAD + (s + 1) * ROWS)
            for pair in range(2):
                low = lifted[2 * pair]
                high = lifted[2 * pair + 1]
                turned = pltpu.roll(high[high.shape[0] - 2 + c, at], OWN, 1)
                put(out, peer, pair, jnp.where(mine, low[low.shape[0] - 2 + c, at], turned))
            out[peer, 4] = packed


def least_squares(columns, beta_norm):
    num_columns = len(columns)
    cosines = []
    sines = []
    target = [beta_norm] + [jnp.zeros_like(beta_norm) for position in range(num_columns)]
    history = []
    triangle = []
    for column_at in range(num_columns):
        column = list(columns[column_at])
        for earlier in range(column_at):
            first_entry = column[earlier]
            second_entry = column[earlier + 1]
            column[earlier] = cosines[earlier] * first_entry + sines[earlier] * second_entry
            column[earlier + 1] = cosines[earlier] * second_entry - sines[earlier] * first_entry
        radius = jnp.sqrt(
            column[column_at] * column[column_at] + column[column_at + 1] * column[column_at + 1]
        )
        cosine = column[column_at] / radius
        sine_part = column[column_at + 1] / radius
        column[column_at] = radius
        cosines.append(cosine)
        sines.append(sine_part)
        target[column_at + 1] = -sine_part * target[column_at]
        target[column_at] = cosine * target[column_at]
        history.append(jnp.abs(target[column_at + 1]))
        triangle.append(column[: column_at + 1])
    solved = [None for position in range(num_columns)]
    for row_at in reversed(range(num_columns)):
        running_sum = target[row_at]
        for later in range(row_at + 1, num_columns):
            running_sum = running_sum - triangle[later][row_at] * solved[later]
        solved[row_at] = running_sum / triangle[row_at][row_at]
    return (solved, history)


def cycle(gram):
    size = KRYLOV + 1
    floors = [1e-12 * gram[k, k].top + 1e-30 for k in range(size)]
    upper = {}
    for k in range(size):
        pivot = jnp.maximum(gram[k, k].top, floors[k])
        root = jnp.sqrt(pivot)
        upper[k, k] = root
        for j in range(k + 1, size):
            upper[k, j] = gram[k, j].top / root
        if k + 1 < size:
            inverse = Pair(pivot, jnp.where(gram[k, k].top < floors[k], 0.0, gram[k, k].low)).inverse()
            for i in range(k + 1, size):
                factor = gram[k, i].times(inverse)
                for j in range(i, size):
                    gram[i, j] = gram[i, j].minus(factor.times(gram[k, j]))

    mapped = []
    for i in range(KRYLOV):
        column = []
        for row in range(i + 2):
            value = upper[row, i + 1]
            if row <= i:
                value = value + upper[row, i]
            for k in range(max(row - 1, 0), i):
                value = value - upper[k, i] * mapped[k][row]
            column.append(value / upper[i, i])
        mapped.append(column)

    beta_norm = upper[0, 0]
    basis = [[jnp.ones_like(beta_norm)]]
    columns = []
    for at in range(KRYLOV):
        newest = basis[-1]
        image = []
        for row in range(at + 2):
            terms = [mapped[i][row] * newest[i] for i in range(max(row - 1, 0), at + 1)]
            image.append(functools.reduce(lambda a, b: a + b, terms))
        projections = []
        rest = list(image)
        for vector in basis:
            terms = [a * b for a, b in zip(image, vector)]
            projections.append(functools.reduce(lambda a, b: a + b, terms))
        for vector, weight in zip(basis, projections):
            for row, value in enumerate(vector):
                rest[row] = rest[row] - weight * value
        terms = [value * value for value in rest]
        length = jnp.sqrt(functools.reduce(lambda a, b: a + b, terms) + 1e-06)
        columns.append(projections + [length])
        basis.append([value / length for value in rest])
    solved, history = least_squares(columns, beta_norm)
    weights = [None] * KRYLOV
    for row in reversed(range(KRYLOV)):
        terms = [solved[j] * basis[j][row] for j in range(row, KRYLOV)]
        value = functools.reduce(lambda a, b: a + b, terms)
        for later in range(row + 1, KRYLOV):
            value = value - upper[row, later] * weights[later]
        weights[row] = value / upper[row, row]
    return weights, history


def combine_kernel(partial, got, solution, history):
    lane = lax.broadcasted_iota(jnp.int32, (ROWS, LANES), 1)
    top, low = exact_sum(partial[:, 0, :], partial[:, 1, :], 0)
    gram = {}
    for n, pair in enumerate(PAIRS):
        values = [jnp.sum(jnp.where(lane[0:1] == n, row, 0.0), axis=1, keepdims=True) for row in (top, low)]
        gram[pair] = Pair(*values)
    weights, norms = cycle(gram)
    for n, norm in enumerate(norms):
        history[n] = jnp.max(norm)
    half = lane[:HALF]
    mine = (half >= HALO) & (half < HALO + OWN)
    low = jnp.where(mine, weights[0], weights[1])
    high = jnp.where(mine, weights[2], weights[3])

    def block(device, part):
        index = place(device, got.shape[0] // 2)
        value = low * got[index, part] + high * got[index, 2 + part]
        return pltpu.roll(value, LANES - HALO, 1) + pltpu.roll(value, OWN - HALO, 1)

    for k in range(got.shape[0] // 2):
        for part in range(2):
            value = jnp.where(half < OWN, block(2 * k, part), block(2 * k + 1, part))
            solution[0, part * HALF : (part + 1) * HALF, k * LANES : (k + 1) * LANES] = value


def body(layers, strips, right_side, cell_terms, polynomial):
    f32 = jnp.float32
    peers = 2 * strips
    rows = ROWS * strips
    circle = [(first_of(strips) + i) % peers for i in range(peers)]

    def exchange(value):
        return lax.all_to_all(value, ("c", "s"), 0, 0, axis_index_groups=[circle], tiled=True)

    earlier = lax.ppermute(right_side, "z", [(i, i + 2) for i in range(layers - 2)])
    before = lax.ppermute(right_side, "z", [(i, i + 1) for i in range(layers - 1)])
    own = pl.pallas_call(
        own_kernel,
        out_shape=jax.ShapeDtypeStruct((peers, 7, HALF, LANES), f32),
        in_specs=[VMEM] * 2,
        out_specs=VMEM,
        compiler_params=PARAMS,
        cost_estimate=pl.CostEstimate(flops=1000000, bytes_accessed=4000000, transcendentals=0),
        name="own",
    )(right_side, cell_terms)
    sent = pl.pallas_call(
        pack_kernel,
        out_shape=jax.ShapeDtypeStruct((peers, 7, HALF, LANES), f32),
        in_specs=[VMEM] * 3,
        out_specs=VMEM,
        compiler_params=PARAMS,
        name="pack",
    )(own, before, earlier)
    got = exchange(sent)
    times = KRYLOV + 2
    field = lambda count: pltpu.VMEM((count, rows + 2 * PAD, LANES), f32)
    sent = pl.pallas_call(
        functools.partial(krylov_kernel, strips),
        out_shape=jax.ShapeDtypeStruct((peers, 5, HALF, LANES), f32),
        in_specs=[SMEM, VMEM],
        out_specs=VMEM,
        scratch_shapes=[pltpu.VMEM((5, rows, LANES), f32)] * 2
        + [field(times - j) for j in range(KRYLOV + 1)]
        + [field(times - j) for j in range(KRYLOV)]
        + [field(times), field(times)],
        compiler_params=PARAMS,
        name="krylov",
    )(polynomial, got)
    got = exchange(sent)
    partial = jnp.concatenate(exact_sum(got[:, 4, 0, :], got[:, 4, 1, :], 0))
    partial = jnp.broadcast_to(partial[None], (layers, 2, LANES))
    order = [(layers // 2 + i) % layers for i in range(layers)]
    partial = lax.all_to_all(partial, "z", 0, 0, axis_index_groups=[order], tiled=True)
    return pl.pallas_call(
        combine_kernel,
        out_shape=(jax.ShapeDtypeStruct(right_side.shape, f32), jax.ShapeDtypeStruct((KRYLOV,), f32)),
        in_specs=[VMEM, VMEM],
        out_specs=(VMEM, SMEM),
        compiler_params=PARAMS,
        name="combine",
    )(partial, got)


def solution(mesh):
    layers = mesh.shape["tm"] // 2
    strips = mesh.shape["space"]
    fine = Mesh(mesh.devices.reshape(layers, 2, strips), ("z", "c", "s"))
    in_specs = (P(("z", "c"), "s", None), P(None, "s", None), P())
    out_specs = (P(("z", "c"), "s", None), P())
    return jax.shard_map(
        functools.partial(body, layers, strips), mesh=fine, in_specs=in_specs, out_specs=out_specs, check_vma=False
    )
```

```python
import functools

import jax
import jax.numpy as jnp
from jax import lax
from jax.experimental import pallas as pl
from jax.experimental.pallas import tpu as pltpu
from jax.sharding import Mesh, PartitionSpec as P

KRYLOV = 4
OWN = 64
HALO = 16
WIDE = OWN + 2 * HALO
HALF = 4
LANES = 128
ROWS = 8
PAD = 8
CHUNK = 64
PAIRS = [(i, j) for i in range(KRYLOV + 1) for j in range(i, KRYLOV + 1)]
VMEM = pl.BlockSpec(memory_space=pltpu.VMEM)
SMEM = pl.BlockSpec(memory_space=pltpu.SMEM)
PARAMS = pltpu.CompilerParams(vmem_limit_bytes=40 * 1024 * 1024)


def first_of(strips):
    return strips // 2 + strips // 8


def place(device, strips):
    return (device - first_of(strips)) % (2 * strips)


def tiles_of(source):
    return [source[:, k * LANES : (k + 1) * LANES] for k in range(source.shape[1] // LANES)]


def windows(tiles, lane):
    zero = jnp.zeros_like(tiles[0])
    even = [zero] + [pltpu.roll(tile, HALO, 1) for tile in tiles]
    odd = [pltpu.roll(tile, LANES - OWN + HALO, 1) for tile in tiles] + [zero]
    out = []
    for k in range(len(tiles)):
        out.append(jnp.where(lane < HALO, even[k], even[k + 1]))
        out.append(jnp.where(lane < LANES - OWN + HALO, odd[k], odd[k + 1]))
    return out


def riders(tiles, lane):
    zero = jnp.zeros_like(tiles[0])
    turned = {shift: [pltpu.roll(tile, shift, 1) for tile in tiles] for shift in (16, 48, 80, 112)}
    edge = [zero] + turned[112] + [zero]
    out = []
    for k in range(len(tiles)):
        out.append([jnp.where(lane < 112, edge[k], edge[k + 1]), turned[80][k], turned[48][k]])
        out.append([turned[48][k], turned[16][k], jnp.where(lane < 112, edge[k + 1], edge[k + 2])])
    return out


def put(out, peer, plane, value):
    out[peer, 2 * plane] = value[:HALF]
    out[peer, 2 * plane + 1] = value[HALF:]


def own_kernel(now, terms, out):
    core = lax.axis_index("c")
    lane = lax.broadcasted_iota(jnp.int32, (ROWS, LANES), 1)
    fields = windows(tiles_of(now.at[0]), lane)
    parts = riders(tiles_of(terms.at[2 * core]), lane)
    across = windows(tiles_of(terms.at[1]), lane)
    upper = (lane >= 0) & (core == 0)
    for device, (field, part, drift) in enumerate(zip(fields, parts, across)):
        peer = place(device, out.shape[0] // 2)
        put(out, peer, 0, jnp.where(lane < WIDE, field, part[0]))
        put(out, peer, 1, part[1])
        put(out, peer, 2, part[2])
        out[peer, 6] = jnp.where(upper[:HALF], drift[:HALF], drift[HALF:])


def pack_kernel(own, before, earlier, out):
    lane = lax.broadcasted_iota(jnp.int32, (ROWS, LANES), 1)
    narrow = lane[:HALF] < WIDE
    for peer in range(out.shape[0]):
        for half in (0, 1, 6):
            out[peer, half] = own[peer, half]
    for plane, source in ((1, before), (2, earlier)):
        for device, window in enumerate(windows(tiles_of(source.at[0]), lane)):
            peer = place(device, out.shape[0] // 2)
            out[peer, 2 * plane] = jnp.where(narrow, window[:HALF], own[peer, 2 * plane])
            out[peer, 2 * plane + 1] = jnp.where(narrow, window[HALF:], own[peer, 2 * plane + 1])


def two_sum(a, b):
    total = a + b
    moved = total - a
    return total, (a - (total - moved)) + (b - moved)


def split(a):
    scaled = 4097.0 * a
    upper = scaled - (scaled - a)
    return upper, a - upper


def exact_sum(top, low, axis):
    quantum = 1024.0 * jnp.max(jnp.abs(top), axis=axis, keepdims=True)
    upper = (top + quantum) - quantum
    rest = (top - upper) + low
    return jnp.sum(upper, axis=axis, keepdims=True), jnp.sum(rest, axis=axis, keepdims=True)


class Pair:
    def __init__(self, top, low):
        self.top = top + low
        self.low = low - (self.top - top)
        self.parts = split(self.top)

    def times(self, other):
        value = self.top * other.top
        (a, b), (c, d) = self.parts, other.parts
        error = (((a * c - value) + a * d) + b * c) + b * d
        return Pair(value, error + (self.top * other.low + self.low * other.top))

    def minus(self, other):
        value, error = two_sum(self.top, -other.top)
        return Pair(value, error + (self.low - other.low))

    def inverse(self):
        guess = 1.0 / self.top
        value = guess * self.top
        (a, b), (c, d) = split(guess), self.parts
        error = (((a * c - value) + a * d) + b * c) + b * d
        return Pair(guess, guess * (((1.0 - value) - error) - guess * self.low))


def krylov_kernel(strips, polynomial, got, out, coef, inner_coef, k0, k1, k2, k3, k4, z1, z2, z3, z4, work_x, work_y):
    rows = ROWS * strips
    times = KRYLOV + 2
    krylov = [k0, k1, k2, k3, k4]
    lifted = [z1, z2, z3, z4]
    lane = lax.broadcasted_iota(jnp.int32, (ROWS, LANES), 1)
    sub = lax.broadcasted_iota(jnp.int32, (ROWS, LANES), 0)
    block = lax.axis_index("c") * strips + lax.axis_index("s")
    first_col = (block == 0) & (lane == HALO)
    last_col = (block == 2 * strips - 1) & (lane == HALO + OWN - 1)

    edge = jnp.zeros((PAD, LANES), jnp.float32)
    for ref in krylov + lifted + [work_x, work_y]:
        for t in range(ref.shape[0]):
            ref[t, 0:PAD] = edge
            ref[t, PAD + rows :] = edge

    for s in range(strips):
        for c in range(2):
            peer = place(c * strips + s, strips)
            at = PAD + s * ROWS
            for plane in range(3):
                k0[times - 2 + c - 2 * plane, at : at + HALF] = got[peer, 2 * plane]
                k0[times - 2 + c - 2 * plane, at + HALF : at + ROWS] = got[peer, 2 * plane + 1]
            coef[3, s * ROWS + c * HALF : s * ROWS + (c + 1) * HALF] = got[peer, 6]

    def rider(at, c):
        last = [pltpu.roll(k0[times - 2 + c - 2 * plane, at], 32 * (plane + 1), 1) for plane in range(3)]
        last[2] = jnp.where(lane < WIDE, last[2], 0.0)
        return jnp.where(lane < 32, last[0], jnp.where(lane < 64, last[1], last[2]))

    for s in range(strips):
        there = slice(s * ROWS, (s + 1) * ROWS)
        inner = slice(PAD + s * ROWS, PAD + (s + 1) * ROWS)
        diffuse = rider(inner, 0)
        half_x = 0.5 * coef[3, there]
        half_y = 0.5 * rider(inner, 1)
        north = -diffuse - half_y
        south = half_y - diffuse
        if s == 0:
            north = jnp.where(sub == 0, 0.0, north)
        if s == strips - 1:
            south = jnp.where(sub == ROWS - 1, 0.0, south)
        coef[0, there] = 1.0 + 4.0 * diffuse
        coef[1, there] = north
        coef[2, there] = south
        coef[3, there] = jnp.where(first_col, 0.0, -diffuse - half_x)
        coef[4, there] = jnp.where(last_col, 0.0, half_x - diffuse)
        for i in range(5):
            scaled = polynomial[3] * coef[i, there]
            inner_coef[i, there] = polynomial[2] + scaled if i == 0 else scaled

    def sweep(count, terms, apply):
        chunk = min(CHUNK, rows)
        for at in range(0, rows, chunk):
            parts = [terms[i, at : at + chunk] for i in range(5)]

            def stencil(ref, t):
                middle = ref[t, at + PAD : at + PAD + chunk]
                north = ref[t, at + PAD - 1 : at + PAD - 1 + chunk]
                south = ref[t, at + PAD + 1 : at + PAD + 1 + chunk]
                west = pltpu.roll(middle, 1, 1)
                east = pltpu.roll(middle, LANES - 1, 1)
                return (
                    (parts[0] * middle + parts[3] * west)
                    + (parts[1] * north + parts[2] * south)
                    + parts[4] * east
                )

            for t in range(count):
                apply(t, slice(at + PAD, at + PAD + chunk), stencil)

    for j in range(KRYLOV):
        source, target, upper = krylov[j], krylov[j + 1], lifted[j]
        count = times - j

        def first(t, at, stencil):
            work_x[t, at] = stencil(source, t)

        def second(t, at, stencil):
            work_y[t, at] = polynomial[1] * source[t, at] + stencil(work_x, t)

        def third(t, at, stencil):
            upper[t, at] = polynomial[0] * source[t, at] + stencil(work_y, t)

        def fourth(t, at, stencil):
            target[t, at] = stencil(upper, t + 1) - upper[t, at] - source[t + 1, at]

        sweep(count, inner_coef, first)
        sweep(count, coef, second)
        sweep(count, coef, third)
        sweep(count - 1, coef, fourth)

    mine = (lane >= HALO) & (lane < HALO + OWN)
    nothing = jnp.zeros((ROWS, LANES), jnp.float32)

    def gram(index, sums):
        at = slice(PAD + index * ROWS, PAD + (index + 1) * ROWS)
        vectors = []
        for ref in krylov:
            newest = pltpu.roll(ref[ref.shape[0] - 1, at], OWN, 1)
            value = jnp.where(mine, ref[ref.shape[0] - 2, at], newest)
            vectors.append((value,) + split(value))
        out = []
        for (i, j), (top, low) in zip(PAIRS, sums):
            (_, upper, lower), (other, other_upper, other_lower) = vectors[i], vectors[j]
            top, error = two_sum(top, upper * other_upper)
            out.append((top, low + (error + (upper * other_lower + lower * other))))
        return out

    sums = [(nothing, nothing) for _ in PAIRS]
    for index in range(strips):
        sums = gram(index, sums)
    tops = [nothing, nothing]
    lows = [nothing, nothing]
    for n, (top, low) in enumerate(sums):
        for shift in (4, 2, 1):
            top, error = two_sum(top, pltpu.roll(top, shift, 0))
            low = low + pltpu.roll(low, shift, 0) + error
        tops[n // ROWS] = jnp.where(sub == n % ROWS, top, tops[n // ROWS])
        lows[n // ROWS] = jnp.where(sub == n % ROWS, low, lows[n // ROWS])
    packed = [nothing, nothing]
    for n in range(2):
        parts = exact_sum(tops[n], lows[n], 1)
        for kind in range(2):
            packed[kind] = jnp.where(lane == sub + n * ROWS, parts[kind], packed[kind])
    packed = [jnp.sum(value, axis=0, keepdims=True) for value in packed]
    packed = jnp.where(sub[:HALF] == 0, packed[0], jnp.where(sub[:HALF] == 1, packed[1], 0.0))

    for c in range(2):
        for s in range(strips):
            peer = place(c * strips + s, strips)
            at = slice(PAD + s * ROWS, PAD + (s + 1) * ROWS)
            for pair in range(2):
                low = lifted[2 * pair]
                high = lifted[2 * pair + 1]
                turned = pltpu.roll(high[high.shape[0] - 2 + c, at], OWN, 1)
                put(out, peer, pair, jnp.where(mine, low[low.shape[0] - 2 + c, at], turned))
            out[peer, 4] = packed


def least_squares(columns, beta_norm):
    num_columns = len(columns)
    cosines = []
    sines = []
    target = [beta_norm] + [jnp.zeros_like(beta_norm) for position in range(num_columns)]
    history = []
    triangle = []
    for column_at in range(num_columns):
        column = list(columns[column_at])
        for earlier in range(column_at):
            first_entry = column[earlier]
            second_entry = column[earlier + 1]
            column[earlier] = cosines[earlier] * first_entry + sines[earlier] * second_entry
            column[earlier + 1] = cosines[earlier] * second_entry - sines[earlier] * first_entry
        radius = jnp.sqrt(
            column[column_at] * column[column_at] + column[column_at + 1] * column[column_at + 1]
        )
        cosine = column[column_at] / radius
        sine_part = column[column_at + 1] / radius
        column[column_at] = radius
        cosines.append(cosine)
        sines.append(sine_part)
        target[column_at + 1] = -sine_part * target[column_at]
        target[column_at] = cosine * target[column_at]
        history.append(jnp.abs(target[column_at + 1]))
        triangle.append(column[: column_at + 1])
    solved = [None for position in range(num_columns)]
    for row_at in reversed(range(num_columns)):
        running_sum = target[row_at]
        for later in range(row_at + 1, num_columns):
            running_sum = running_sum - triangle[later][row_at] * solved[later]
        solved[row_at] = running_sum / triangle[row_at][row_at]
    return (solved, history)


def cycle(gram):
    size = KRYLOV + 1
    floors = [1e-12 * gram[k, k].top + 1e-30 for k in range(size)]
    upper = {}
    for k in range(size):
        pivot = jnp.maximum(gram[k, k].top, floors[k])
        root = jnp.sqrt(pivot)
        upper[k, k] = root
        for j in range(k + 1, size):
            upper[k, j] = gram[k, j].top / root
        if k + 1 < size:
            inverse = Pair(pivot, jnp.where(gram[k, k].top < floors[k], 0.0, gram[k, k].low)).inverse()
            for i in range(k + 1, size):
                factor = gram[k, i].times(inverse)
                for j in range(i, size):
                    gram[i, j] = gram[i, j].minus(factor.times(gram[k, j]))

    mapped = []
    for i in range(KRYLOV):
        column = []
        for row in range(i + 2):
            value = upper[row, i + 1]
            if row <= i:
                value = value + upper[row, i]
            for k in range(max(row - 1, 0), i):
                value = value - upper[k, i] * mapped[k][row]
            column.append(value / upper[i, i])
        mapped.append(column)

    beta_norm = upper[0, 0]
    basis = [[jnp.ones_like(beta_norm)]]
    columns = []
    for at in range(KRYLOV):
        newest = basis[-1]
        image = []
        for row in range(at + 2):
            terms = [mapped[i][row] * newest[i] for i in range(max(row - 1, 0), at + 1)]
            image.append(functools.reduce(lambda a, b: a + b, terms))
        projections = []
        rest = list(image)
        for vector in basis:
            terms = [a * b for a, b in zip(image, vector)]
            projections.append(functools.reduce(lambda a, b: a + b, terms))
        for vector, weight in zip(basis, projections):
            for row, value in enumerate(vector):
                rest[row] = rest[row] - weight * value
        terms = [value * value for value in rest]
        length = jnp.sqrt(functools.reduce(lambda a, b: a + b, terms) + 1e-06)
        columns.append(projections + [length])
        basis.append([value / length for value in rest])
    solved, history = least_squares(columns, beta_norm)
    weights = [None] * KRYLOV
    for row in reversed(range(KRYLOV)):
        terms = [solved[j] * basis[j][row] for j in range(row, KRYLOV)]
        value = functools.reduce(lambda a, b: a + b, terms)
        for later in range(row + 1, KRYLOV):
            value = value - upper[row, later] * weights[later]
        weights[row] = value / upper[row, row]
    return weights, history


def combine_kernel(partial, got, solution, history):
    lane = lax.broadcasted_iota(jnp.int32, (ROWS, LANES), 1)
    top, low = exact_sum(partial[:, 0, :], partial[:, 1, :], 0)
    gram = {}
    for n, pair in enumerate(PAIRS):
        values = [jnp.sum(jnp.where(lane[0:1] == n, row, 0.0), axis=1, keepdims=True) for row in (top, low)]
        gram[pair] = Pair(*values)
    weights, norms = cycle(gram)
    for n, norm in enumerate(norms):
        history[n] = jnp.max(norm)
    half = lane[:HALF]
    mine = (half >= HALO) & (half < HALO + OWN)
    low = jnp.where(mine, weights[0], weights[1])
    high = jnp.where(mine, weights[2], weights[3])

    def block(device, part):
        index = place(device, got.shape[0] // 2)
        value = low * got[index, part] + high * got[index, 2 + part]
        return pltpu.roll(value, LANES - HALO, 1) + pltpu.roll(value, OWN - HALO, 1)

    for k in range(got.shape[0] // 2):
        for part in range(2):
            value = jnp.where(half < OWN, block(2 * k, part), block(2 * k + 1, part))
            solution[0, part * HALF : (part + 1) * HALF, k * LANES : (k + 1) * LANES] = value


def body(layers, strips, right_side, cell_terms, polynomial):
    f32 = jnp.float32
    peers = 2 * strips
    rows = ROWS * strips
    circle = [(first_of(strips) + i) % peers for i in range(peers)]

    def exchange(value):
        return lax.all_to_all(value, ("c", "s"), 0, 0, axis_index_groups=[circle], tiled=True)

    earlier = lax.ppermute(right_side, "z", [(i, i + 2) for i in range(layers - 2)])
    before = lax.ppermute(right_side, "z", [(i, i + 1) for i in range(layers - 1)])
    own = pl.pallas_call(
        own_kernel,
        out_shape=jax.ShapeDtypeStruct((peers, 7, HALF, LANES), f32),
        in_specs=[VMEM] * 2,
        out_specs=VMEM,
        compiler_params=PARAMS,
        cost_estimate=pl.CostEstimate(flops=1000000, bytes_accessed=4000000, transcendentals=0),
        name="own",
    )(right_side, cell_terms)
    sent = pl.pallas_call(
        pack_kernel,
        out_shape=jax.ShapeDtypeStruct((peers, 7, HALF, LANES), f32),
        in_specs=[VMEM] * 3,
        out_specs=VMEM,
        compiler_params=PARAMS,
        name="pack",
    )(own, before, earlier)
    got = exchange(sent)
    times = KRYLOV + 2
    field = lambda count: pltpu.VMEM((count, rows + 2 * PAD, LANES), f32)
    sent = pl.pallas_call(
        functools.partial(krylov_kernel, strips),
        out_shape=jax.ShapeDtypeStruct((peers, 5, HALF, LANES), f32),
        in_specs=[SMEM, VMEM],
        out_specs=VMEM,
        scratch_shapes=[pltpu.VMEM((5, rows, LANES), f32)] * 2
        + [field(times - j) for j in range(KRYLOV + 1)]
        + [field(times - j) for j in range(KRYLOV)]
        + [field(times), field(times)],
        compiler_params=PARAMS,
        name="krylov",
    )(polynomial, got)
    got = exchange(sent)
    partial = jnp.concatenate(exact_sum(got[:, 4, 0, :], got[:, 4, 1, :], 0))
    partial = jnp.broadcast_to(partial[None], (layers, 2, LANES))
    order = sorted(range(layers), key=lambda i: (i != layers // 2, min(i, layers - i), i))
    partial = lax.all_to_all(partial, "z", 0, 0, axis_index_groups=[order], tiled=True)
    return pl.pallas_call(
        combine_kernel,
        out_shape=(jax.ShapeDtypeStruct(right_side.shape, f32), jax.ShapeDtypeStruct((KRYLOV,), f32)),
        in_specs=[VMEM, VMEM],
        out_specs=(VMEM, SMEM),
        compiler_params=PARAMS,
        name="combine",
    )(partial, got)


def solution(mesh):
    layers = mesh.shape["tm"] // 2
    strips = mesh.shape["space"]
    fine = Mesh(mesh.devices.reshape(layers, 2, strips), ("z", "c", "s"))
    in_specs = (P(("z", "c"), "s", None), P(None, "s", None), P())
    out_specs = (P(("z", "c"), "s", None), P())
    return jax.shard_map(
        functools.partial(body, layers, strips), mesh=fine, in_specs=in_specs, out_specs=out_specs, check_vma=False
    )
```

```python
import functools

import jax
import jax.numpy as jnp
from jax import lax
from jax.experimental import pallas as pl
from jax.experimental.pallas import tpu as pltpu
from jax.sharding import Mesh, PartitionSpec as P

KRYLOV = 4
OWN = 64
HALO = 16
WIDE = OWN + 2 * HALO
HALF = 4
FINE = 2
LANES = 128
ROWS = 8
PAD = 8
CHUNK = 64
PAIRS = [(i, j) for i in range(KRYLOV + 1) for j in range(i, KRYLOV + 1)]
VMEM = pl.BlockSpec(memory_space=pltpu.VMEM)
SMEM = pl.BlockSpec(memory_space=pltpu.SMEM)
PARAMS = pltpu.CompilerParams(vmem_limit_bytes=40 * 1024 * 1024)


def first_of(strips):
    return strips // 2 + strips // 8


def place(device, strips):
    return (device - first_of(strips)) % (2 * strips)


def tiles_of(source):
    return [source[:, k * LANES : (k + 1) * LANES] for k in range(source.shape[1] // LANES)]


def windows(tiles, lane):
    zero = jnp.zeros_like(tiles[0])
    even = [zero] + [pltpu.roll(tile, HALO, 1) for tile in tiles]
    odd = [pltpu.roll(tile, LANES - OWN + HALO, 1) for tile in tiles] + [zero]
    out = []
    for k in range(len(tiles)):
        out.append(jnp.where(lane < HALO, even[k], even[k + 1]))
        out.append(jnp.where(lane < LANES - OWN + HALO, odd[k], odd[k + 1]))
    return out


def riders(tiles, lane):
    zero = jnp.zeros_like(tiles[0])
    turned = {shift: [pltpu.roll(tile, shift, 1) for tile in tiles] for shift in (16, 48, 80, 112)}
    edge = [zero] + turned[112] + [zero]
    out = []
    for k in range(len(tiles)):
        out.append([jnp.where(lane < 112, edge[k], edge[k + 1]), turned[80][k], turned[48][k]])
        out.append([turned[48][k], turned[16][k], jnp.where(lane < 112, edge[k + 1], edge[k + 2])])
    return out


def put(out, peer, plane, value):
    out[peer, 2 * plane] = value[:HALF]
    out[peer, 2 * plane + 1] = value[HALF:]


def own_kernel(now, terms, out):
    core = lax.axis_index("c")
    lane = lax.broadcasted_iota(jnp.int32, (ROWS, LANES), 1)
    fields = windows(tiles_of(now.at[0]), lane)
    parts = riders(tiles_of(terms.at[2 * core]), lane)
    across = windows(tiles_of(terms.at[1]), lane)
    upper = (lane >= 0) & (core == 0)
    for device, (field, part, drift) in enumerate(zip(fields, parts, across)):
        peer = place(device, out.shape[0] // 2)
        put(out, peer, 0, jnp.where(lane < WIDE, field, part[0]))
        put(out, peer, 1, part[1])
        put(out, peer, 2, part[2])
        out[peer, 6] = jnp.where(upper[:HALF], drift[:HALF], drift[HALF:])


def pack_kernel(own, before, earlier, out):
    lane = lax.broadcasted_iota(jnp.int32, (ROWS, LANES), 1)
    narrow = lane[:HALF] < WIDE
    for peer in range(out.shape[0]):
        for half in (0, 1, 6):
            out[peer, half] = own[peer, half]
    for plane, source in ((1, before), (2, earlier)):
        for device, window in enumerate(windows(tiles_of(source.at[0]), lane)):
            peer = place(device, out.shape[0] // 2)
            out[peer, 2 * plane] = jnp.where(narrow, window[:HALF], own[peer, 2 * plane])
            out[peer, 2 * plane + 1] = jnp.where(narrow, window[HALF:], own[peer, 2 * plane + 1])


def two_sum(a, b):
    total = a + b
    moved = total - a
    return total, (a - (total - moved)) + (b - moved)


def split(a):
    scaled = 4097.0 * a
    upper = scaled - (scaled - a)
    return upper, a - upper


def exact_sum(top, low, axis):
    quantum = 1024.0 * jnp.max(jnp.abs(top), axis=axis, keepdims=True)
    upper = (top + quantum) - quantum
    rest = (top - upper) + low
    return jnp.sum(upper, axis=axis, keepdims=True), jnp.sum(rest, axis=axis, keepdims=True)


class Pair:
    def __init__(self, top, low):
        self.top = top + low
        self.low = low - (self.top - top)
        self.parts = split(self.top)

    def times(self, other):
        value = self.top * other.top
        (a, b), (c, d) = self.parts, other.parts
        error = (((a * c - value) + a * d) + b * c) + b * d
        return Pair(value, error + (self.top * other.low + self.low * other.top))

    def minus(self, other):
        value, error = two_sum(self.top, -other.top)
        return Pair(value, error + (self.low - other.low))

    def inverse(self):
        guess = 1.0 / self.top
        value = guess * self.top
        (a, b), (c, d) = split(guess), self.parts
        error = (((a * c - value) + a * d) + b * c) + b * d
        return Pair(guess, guess * (((1.0 - value) - error) - guess * self.low))


def krylov_kernel(strips, polynomial, got, out, coef, inner_coef, k0, k1, k2, k3, k4, z1, z2, z3, z4, work_x, work_y):
    rows = ROWS * strips
    times = KRYLOV + 2
    krylov = [k0, k1, k2, k3, k4]
    lifted = [z1, z2, z3, z4]
    lane = lax.broadcasted_iota(jnp.int32, (ROWS, LANES), 1)
    sub = lax.broadcasted_iota(jnp.int32, (ROWS, LANES), 0)
    block = lax.axis_index("c") * strips + lax.axis_index("s")
    first_col = (block == 0) & (lane == HALO)
    last_col = (block == 2 * strips - 1) & (lane == HALO + OWN - 1)

    edge = jnp.zeros((PAD, LANES), jnp.float32)
    for ref in krylov + lifted + [work_x, work_y]:
        for t in range(ref.shape[0]):
            ref[t, 0:PAD] = edge
            ref[t, PAD + rows :] = edge

    for s in range(strips):
        for c in range(2):
            peer = place(c * strips + s, strips)
            at = PAD + s * ROWS
            for plane in range(3):
                k0[times - 2 + c - 2 * plane, at : at + HALF] = got[peer, 2 * plane]
                k0[times - 2 + c - 2 * plane, at + HALF : at + ROWS] = got[peer, 2 * plane + 1]
            coef[3, s * ROWS + c * HALF : s * ROWS + (c + 1) * HALF] = got[peer, 6]

    def rider(at, c):
        last = [pltpu.roll(k0[times - 2 + c - 2 * plane, at], 32 * (plane + 1), 1) for plane in range(3)]
        last[2] = jnp.where(lane < WIDE, last[2], 0.0)
        return jnp.where(lane < 32, last[0], jnp.where(lane < 64, last[1], last[2]))

    for s in range(strips):
        there = slice(s * ROWS, (s + 1) * ROWS)
        inner = slice(PAD + s * ROWS, PAD + (s + 1) * ROWS)
        diffuse = rider(inner, 0)
        half_x = 0.5 * coef[3, there]
        half_y = 0.5 * rider(inner, 1)
        north = -diffuse - half_y
        south = half_y - diffuse
        if s == 0:
            north = jnp.where(sub == 0, 0.0, north)
        if s == strips - 1:
            south = jnp.where(sub == ROWS - 1, 0.0, south)
        coef[0, there] = 1.0 + 4.0 * diffuse
        coef[1, there] = north
        coef[2, there] = south
        coef[3, there] = jnp.where(first_col, 0.0, -diffuse - half_x)
        coef[4, there] = jnp.where(last_col, 0.0, half_x - diffuse)
        for i in range(5):
            scaled = polynomial[3] * coef[i, there]
            inner_coef[i, there] = polynomial[2] + scaled if i == 0 else scaled

    def sweep(count, terms, apply):
        chunk = min(CHUNK, rows)
        for at in range(0, rows, chunk):
            parts = [terms[i, at : at + chunk] for i in range(5)]

            def stencil(ref, t):
                middle = ref[t, at + PAD : at + PAD + chunk]
                north = ref[t, at + PAD - 1 : at + PAD - 1 + chunk]
                south = ref[t, at + PAD + 1 : at + PAD + 1 + chunk]
                west = pltpu.roll(middle, 1, 1)
                east = pltpu.roll(middle, LANES - 1, 1)
                return (
                    (parts[0] * middle + parts[3] * west)
                    + (parts[1] * north + parts[2] * south)
                    + parts[4] * east
                )

            for t in range(count):
                apply(t, slice(at + PAD, at + PAD + chunk), stencil)

    for j in range(KRYLOV):
        source, target, upper = krylov[j], krylov[j + 1], lifted[j]
        count = times - j

        def first(t, at, stencil):
            work_x[t, at] = stencil(source, t)

        def second(t, at, stencil):
            work_y[t, at] = polynomial[1] * source[t, at] + stencil(work_x, t)

        def third(t, at, stencil):
            upper[t, at] = polynomial[0] * source[t, at] + stencil(work_y, t)

        def fourth(t, at, stencil):
            target[t, at] = stencil(upper, t + 1) - upper[t, at] - source[t + 1, at]

        sweep(count, inner_coef, first)
        sweep(count, coef, second)
        sweep(count, coef, third)
        sweep(count - 1, coef, fourth)

    mine = (lane >= HALO) & (lane < HALO + OWN)
    nothing = jnp.zeros((ROWS, LANES), jnp.float32)

    def gram(index, sums):
        at = slice(PAD + index * ROWS, PAD + (index + 1) * ROWS)
        vectors = []
        for ref in krylov:
            newest = pltpu.roll(ref[ref.shape[0] - 1, at], OWN, 1)
            value = jnp.where(mine, ref[ref.shape[0] - 2, at], newest)
            vectors.append((value,) + split(value))
        out = []
        for (i, j), (top, low) in zip(PAIRS, sums):
            (_, upper, lower), (other, other_upper, other_lower) = vectors[i], vectors[j]
            top, error = two_sum(top, upper * other_upper)
            out.append((top, low + (error + (upper * other_lower + lower * other))))
        return out

    sums = [(nothing, nothing) for _ in PAIRS]
    for index in range(strips):
        sums = gram(index, sums)
    tops = [nothing, nothing]
    lows = [nothing, nothing]
    for n, (top, low) in enumerate(sums):
        for shift in (4, 2, 1):
            top, error = two_sum(top, pltpu.roll(top, shift, 0))
            low = low + pltpu.roll(low, shift, 0) + error
        tops[n // ROWS] = jnp.where(sub == n % ROWS, top, tops[n // ROWS])
        lows[n // ROWS] = jnp.where(sub == n % ROWS, low, lows[n // ROWS])
    packed = [nothing, nothing]
    for n in range(2):
        parts = exact_sum(tops[n], lows[n], 1)
        for kind in range(2):
            packed[kind] = jnp.where(lane == sub + n * ROWS, parts[kind], packed[kind])
    packed = [jnp.sum(value, axis=0, keepdims=True) for value in packed]
    packed = jnp.where(sub[:FINE] == 0, packed[0], packed[1])

    for c in range(2):
        for s in range(strips):
            peer = place(c * strips + s, strips)
            at = slice(PAD + s * ROWS, PAD + (s + 1) * ROWS)
            for pair in range(2):
                low = lifted[2 * pair]
                high = lifted[2 * pair + 1]
                turned = pltpu.roll(high[high.shape[0] - 2 + c, at], OWN, 1)
                value = jnp.where(mine, low[low.shape[0] - 2 + c, at], turned)
                for part in range(ROWS // FINE):
                    out[peer, 4 * pair + part] = value[part * FINE : (part + 1) * FINE]
            out[peer, 8] = packed


def least_squares(columns, beta_norm):
    num_columns = len(columns)
    cosines = []
    sines = []
    target = [beta_norm] + [jnp.zeros_like(beta_norm) for position in range(num_columns)]
    history = []
    triangle = []
    for column_at in range(num_columns):
        column = list(columns[column_at])
        for earlier in range(column_at):
            first_entry = column[earlier]
            second_entry = column[earlier + 1]
            column[earlier] = cosines[earlier] * first_entry + sines[earlier] * second_entry
            column[earlier + 1] = cosines[earlier] * second_entry - sines[earlier] * first_entry
        radius = jnp.sqrt(
            column[column_at] * column[column_at] + column[column_at + 1] * column[column_at + 1]
        )
        cosine = column[column_at] / radius
        sine_part = column[column_at + 1] / radius
        column[column_at] = radius
        cosines.append(cosine)
        sines.append(sine_part)
        target[column_at + 1] = -sine_part * target[column_at]
        target[column_at] = cosine * target[column_at]
        history.append(jnp.abs(target[column_at + 1]))
        triangle.append(column[: column_at + 1])
    solved = [None for position in range(num_columns)]
    for row_at in reversed(range(num_columns)):
        running_sum = target[row_at]
        for later in range(row_at + 1, num_columns):
            running_sum = running_sum - triangle[later][row_at] * solved[later]
        solved[row_at] = running_sum / triangle[row_at][row_at]
    return (solved, history)


def cycle(gram):
    size = KRYLOV + 1
    floors = [1e-12 * gram[k, k].top + 1e-30 for k in range(size)]
    upper = {}
    for k in range(size):
        pivot = jnp.maximum(gram[k, k].top, floors[k])
        root = jnp.sqrt(pivot)
        upper[k, k] = root
        for j in range(k + 1, size):
            upper[k, j] = gram[k, j].top / root
        if k + 1 < size:
            inverse = Pair(pivot, jnp.where(gram[k, k].top < floors[k], 0.0, gram[k, k].low)).inverse()
            for i in range(k + 1, size):
                factor = gram[k, i].times(inverse)
                for j in range(i, size):
                    gram[i, j] = gram[i, j].minus(factor.times(gram[k, j]))

    mapped = []
    for i in range(KRYLOV):
        column = []
        for row in range(i + 2):
            value = upper[row, i + 1]
            if row <= i:
                value = value + upper[row, i]
            for k in range(max(row - 1, 0), i):
                value = value - upper[k, i] * mapped[k][row]
            column.append(value / upper[i, i])
        mapped.append(column)

    beta_norm = upper[0, 0]
    basis = [[jnp.ones_like(beta_norm)]]
    columns = []
    for at in range(KRYLOV):
        newest = basis[-1]
        image = []
        for row in range(at + 2):
            terms = [mapped[i][row] * newest[i] for i in range(max(row - 1, 0), at + 1)]
            image.append(functools.reduce(lambda a, b: a + b, terms))
        projections = []
        rest = list(image)
        for vector in basis:
            terms = [a * b for a, b in zip(image, vector)]
            projections.append(functools.reduce(lambda a, b: a + b, terms))
        for vector, weight in zip(basis, projections):
            for row, value in enumerate(vector):
                rest[row] = rest[row] - weight * value
        terms = [value * value for value in rest]
        length = jnp.sqrt(functools.reduce(lambda a, b: a + b, terms) + 1e-06)
        columns.append(projections + [length])
        basis.append([value / length for value in rest])
    solved, history = least_squares(columns, beta_norm)
    weights = [None] * KRYLOV
    for row in reversed(range(KRYLOV)):
        terms = [solved[j] * basis[j][row] for j in range(row, KRYLOV)]
        value = functools.reduce(lambda a, b: a + b, terms)
        for later in range(row + 1, KRYLOV):
            value = value - upper[row, later] * weights[later]
        weights[row] = value / upper[row, row]
    return weights, history


def combine_kernel(partial, got, solution, history):
    lane = lax.broadcasted_iota(jnp.int32, (ROWS, LANES), 1)
    top, low = exact_sum(partial[:, 0, :], partial[:, 1, :], 0)
    gram = {}
    for n, pair in enumerate(PAIRS):
        values = [jnp.sum(jnp.where(lane[0:1] == n, row, 0.0), axis=1, keepdims=True) for row in (top, low)]
        gram[pair] = Pair(*values)
    weights, norms = cycle(gram)
    for n, norm in enumerate(norms):
        history[n] = jnp.max(norm)
    half = lane[:FINE]
    mine = (half >= HALO) & (half < HALO + OWN)
    low = jnp.where(mine, weights[0], weights[1])
    high = jnp.where(mine, weights[2], weights[3])

    def block(device, part):
        index = place(device, got.shape[0] // 2)
        value = low * got[index, part] + high * got[index, 4 + part]
        return pltpu.roll(value, LANES - HALO, 1) + pltpu.roll(value, OWN - HALO, 1)

    for k in range(got.shape[0] // 2):
        for part in range(ROWS // FINE):
            value = jnp.where(half < OWN, block(2 * k, part), block(2 * k + 1, part))
            solution[0, part * FINE : (part + 1) * FINE, k * LANES : (k + 1) * LANES] = value


def body(layers, strips, right_side, cell_terms, polynomial):
    f32 = jnp.float32
    peers = 2 * strips
    rows = ROWS * strips
    circle = [(first_of(strips) + i) % peers for i in range(peers)]

    def exchange(value):
        return lax.all_to_all(value, ("c", "s"), 0, 0, axis_index_groups=[circle], tiled=True)

    earlier = lax.ppermute(right_side, "z", [(i, i + 2) for i in range(layers - 2)])
    before = lax.ppermute(right_side, "z", [(i, i + 1) for i in range(layers - 1)])
    own = pl.pallas_call(
        own_kernel,
        out_shape=jax.ShapeDtypeStruct((peers, 7, HALF, LANES), f32),
        in_specs=[VMEM] * 2,
        out_specs=VMEM,
        compiler_params=PARAMS,
        cost_estimate=pl.CostEstimate(flops=1000000, bytes_accessed=4000000, transcendentals=0),
        name="own",
    )(right_side, cell_terms)
    sent = pl.pallas_call(
        pack_kernel,
        out_shape=jax.ShapeDtypeStruct((peers, 7, HALF, LANES), f32),
        in_specs=[VMEM] * 3,
        out_specs=VMEM,
        compiler_params=PARAMS,
        name="pack",
    )(own, before, earlier)
    got = exchange(sent)
    times = KRYLOV + 2
    field = lambda count: pltpu.VMEM((count, rows + 2 * PAD, LANES), f32)
    sent = pl.pallas_call(
        functools.partial(krylov_kernel, strips),
        out_shape=jax.ShapeDtypeStruct((peers, 9, FINE, LANES), f32),
        in_specs=[SMEM, VMEM],
        out_specs=VMEM,
        scratch_shapes=[pltpu.VMEM((5, rows, LANES), f32)] * 2
        + [field(times - j) for j in range(KRYLOV + 1)]
        + [field(times - j) for j in range(KRYLOV)]
        + [field(times), field(times)],
        compiler_params=PARAMS,
        name="krylov",
    )(polynomial, got)
    got = exchange(sent)
    partial = jnp.concatenate(exact_sum(got[:, 8, 0, :], got[:, 8, 1, :], 0))
    partial = jnp.broadcast_to(partial[None], (layers, 2, LANES))
    order = sorted(range(layers), key=lambda i: (i != layers // 2, min(i, layers - i), i))
    partial = lax.all_to_all(partial, "z", 0, 0, axis_index_groups=[order], tiled=True)
    return pl.pallas_call(
        combine_kernel,
        out_shape=(jax.ShapeDtypeStruct(right_side.shape, f32), jax.ShapeDtypeStruct((KRYLOV,), f32)),
        in_specs=[VMEM, VMEM],
        out_specs=(VMEM, SMEM),
        compiler_params=PARAMS,
        name="combine",
    )(partial, got)


def solution(mesh):
    layers = mesh.shape["tm"] // 2
    strips = mesh.shape["space"]
    fine = Mesh(mesh.devices.reshape(layers, 2, strips), ("z", "c", "s"))
    in_specs = (P(("z", "c"), "s", None), P(None, "s", None), P())
    out_specs = (P(("z", "c"), "s", None), P())
    return jax.shard_map(
        functools.partial(body, layers, strips), mesh=fine, in_specs=in_specs, out_specs=out_specs, check_vma=False
    )
```

```python
import functools

import jax
import jax.numpy as jnp
from jax import lax
from jax.experimental import pallas as pl
from jax.experimental.pallas import tpu as pltpu
from jax.sharding import Mesh, PartitionSpec as P

KRYLOV = 4
OWN = 64
HALO = 16
WIDE = OWN + 2 * HALO
HALF = 4
FINE = 2
LANES = 128
ROWS = 8
PAD = 8
CHUNK = 64
PAIRS = [(i, j) for i in range(KRYLOV + 1) for j in range(i, KRYLOV + 1)]
VMEM = pl.BlockSpec(memory_space=pltpu.VMEM)
SMEM = pl.BlockSpec(memory_space=pltpu.SMEM)
PARAMS = pltpu.CompilerParams(vmem_limit_bytes=40 * 1024 * 1024)


def first_of(strips):
    return strips // 2 + strips // 8


def place(device, strips):
    return (device - first_of(strips)) % (2 * strips)


def tiles_of(source):
    return [source[:, k * LANES : (k + 1) * LANES] for k in range(source.shape[1] // LANES)]


def windows(tiles, lane):
    zero = jnp.zeros_like(tiles[0])
    even = [zero] + [pltpu.roll(tile, HALO, 1) for tile in tiles]
    odd = [pltpu.roll(tile, LANES - OWN + HALO, 1) for tile in tiles] + [zero]
    out = []
    for k in range(len(tiles)):
        out.append(jnp.where(lane < HALO, even[k], even[k + 1]))
        out.append(jnp.where(lane < LANES - OWN + HALO, odd[k], odd[k + 1]))
    return out


def riders(tiles, lane):
    zero = jnp.zeros_like(tiles[0])
    turned = {shift: [pltpu.roll(tile, shift, 1) for tile in tiles] for shift in (16, 48, 80, 112)}
    edge = [zero] + turned[112] + [zero]
    out = []
    for k in range(len(tiles)):
        out.append([jnp.where(lane < 112, edge[k], edge[k + 1]), turned[80][k], turned[48][k]])
        out.append([turned[48][k], turned[16][k], jnp.where(lane < 112, edge[k + 1], edge[k + 2])])
    return out


def put(out, peer, plane, value):
    out[peer, 2 * plane] = value[:HALF]
    out[peer, 2 * plane + 1] = value[HALF:]


def own_kernel(now, terms, out):
    core = lax.axis_index("c")
    lane = lax.broadcasted_iota(jnp.int32, (ROWS, LANES), 1)
    fields = windows(tiles_of(now.at[0]), lane)
    parts = riders(tiles_of(terms.at[2 * core]), lane)
    across = windows(tiles_of(terms.at[1]), lane)
    upper = (lane >= 0) & (core == 0)
    for device, (field, part, drift) in enumerate(zip(fields, parts, across)):
        peer = place(device, out.shape[0] // 2)
        put(out, peer, 0, jnp.where(lane < WIDE, field, part[0]))
        put(out, peer, 1, part[1])
        put(out, peer, 2, part[2])
        out[peer, 6] = jnp.where(upper[:HALF], drift[:HALF], drift[HALF:])


def pack_kernel(own, before, earlier, out):
    lane = lax.broadcasted_iota(jnp.int32, (ROWS, LANES), 1)
    narrow = lane[:HALF] < WIDE
    for peer in range(out.shape[0]):
        for half in (0, 1, 6):
            out[peer, half] = own[peer, half]
    for plane, source in ((1, before), (2, earlier)):
        for device, window in enumerate(windows(tiles_of(source.at[0]), lane)):
            peer = place(device, out.shape[0] // 2)
            out[peer, 2 * plane] = jnp.where(narrow, window[:HALF], own[peer, 2 * plane])
            out[peer, 2 * plane + 1] = jnp.where(narrow, window[HALF:], own[peer, 2 * plane + 1])


def two_sum(a, b):
    total = a + b
    moved = total - a
    return total, (a - (total - moved)) + (b - moved)


def split(a):
    scaled = 4097.0 * a
    upper = scaled - (scaled - a)
    return upper, a - upper


def exact_sum(top, low, axis):
    quantum = 1024.0 * jnp.max(jnp.abs(top), axis=axis, keepdims=True)
    upper = (top + quantum) - quantum
    rest = (top - upper) + low
    return jnp.sum(upper, axis=axis, keepdims=True), jnp.sum(rest, axis=axis, keepdims=True)


class Pair:
    def __init__(self, top, low):
        self.top = top + low
        self.low = low - (self.top - top)
        self.parts = split(self.top)

    def times(self, other):
        value = self.top * other.top
        (a, b), (c, d) = self.parts, other.parts
        error = (((a * c - value) + a * d) + b * c) + b * d
        return Pair(value, error + (self.top * other.low + self.low * other.top))

    def minus(self, other):
        value, error = two_sum(self.top, -other.top)
        return Pair(value, error + (self.low - other.low))

    def inverse(self):
        guess = 1.0 / self.top
        value = guess * self.top
        (a, b), (c, d) = split(guess), self.parts
        error = (((a * c - value) + a * d) + b * c) + b * d
        return Pair(guess, guess * (((1.0 - value) - error) - guess * self.low))


def krylov_kernel(strips, polynomial, got, out, coef, inner_coef, k0, k1, k2, k3, k4, z1, z2, z3, z4, work_x, work_y):
    rows = ROWS * strips
    times = KRYLOV + 2
    krylov = [k0, k1, k2, k3, k4]
    lifted = [z1, z2, z3, z4]
    lane = lax.broadcasted_iota(jnp.int32, (ROWS, LANES), 1)
    sub = lax.broadcasted_iota(jnp.int32, (ROWS, LANES), 0)
    block = lax.axis_index("c") * strips + lax.axis_index("s")
    first_col = (block == 0) & (lane == HALO)
    last_col = (block == 2 * strips - 1) & (lane == HALO + OWN - 1)

    edge = jnp.zeros((PAD, LANES), jnp.float32)
    for ref in krylov + lifted + [work_x, work_y]:
        for t in range(ref.shape[0]):
            ref[t, 0:PAD] = edge
            ref[t, PAD + rows :] = edge

    for s in range(strips):
        for c in range(2):
            peer = place(c * strips + s, strips)
            at = PAD + s * ROWS
            for plane in range(3):
                k0[times - 2 + c - 2 * plane, at : at + HALF] = got[peer, 2 * plane]
                k0[times - 2 + c - 2 * plane, at + HALF : at + ROWS] = got[peer, 2 * plane + 1]
            coef[3, s * ROWS + c * HALF : s * ROWS + (c + 1) * HALF] = got[peer, 6]

    def rider(at, c):
        last = [pltpu.roll(k0[times - 2 + c - 2 * plane, at], 32 * (plane + 1), 1) for plane in range(3)]
        last[2] = jnp.where(lane < WIDE, last[2], 0.0)
        return jnp.where(lane < 32, last[0], jnp.where(lane < 64, last[1], last[2]))

    for s in range(strips):
        there = slice(s * ROWS, (s + 1) * ROWS)
        inner = slice(PAD + s * ROWS, PAD + (s + 1) * ROWS)
        diffuse = rider(inner, 0)
        half_x = 0.5 * coef[3, there]
        half_y = 0.5 * rider(inner, 1)
        north = -diffuse - half_y
        south = half_y - diffuse
        if s == 0:
            north = jnp.where(sub == 0, 0.0, north)
        if s == strips - 1:
            south = jnp.where(sub == ROWS - 1, 0.0, south)
        coef[0, there] = 1.0 + 4.0 * diffuse
        coef[1, there] = north
        coef[2, there] = south
        coef[3, there] = jnp.where(first_col, 0.0, -diffuse - half_x)
        coef[4, there] = jnp.where(last_col, 0.0, half_x - diffuse)
        for i in range(5):
            scaled = polynomial[3] * coef[i, there]
            inner_coef[i, there] = polynomial[2] + scaled if i == 0 else scaled

    def sweep(count, terms, apply):
        chunk = min(CHUNK, rows)
        for at in range(0, rows, chunk):
            parts = [terms[i, at : at + chunk] for i in range(5)]

            def stencil(ref, t):
                middle = ref[t, at + PAD : at + PAD + chunk]
                north = ref[t, at + PAD - 1 : at + PAD - 1 + chunk]
                south = ref[t, at + PAD + 1 : at + PAD + 1 + chunk]
                west = pltpu.roll(middle, 1, 1)
                east = pltpu.roll(middle, LANES - 1, 1)
                return (
                    (parts[0] * middle + parts[3] * west)
                    + (parts[1] * north + parts[2] * south)
                    + parts[4] * east
                )

            for t in range(count):
                apply(t, slice(at + PAD, at + PAD + chunk), stencil)

    for j in range(KRYLOV):
        source, target, upper = krylov[j], krylov[j + 1], lifted[j]
        count = times - j

        def first(t, at, stencil):
            work_x[t, at] = stencil(source, t)

        def second(t, at, stencil):
            work_y[t, at] = polynomial[1] * source[t, at] + stencil(work_x, t)

        def third(t, at, stencil):
            upper[t, at] = polynomial[0] * source[t, at] + stencil(work_y, t)

        def fourth(t, at, stencil):
            target[t, at] = stencil(upper, t + 1) - upper[t, at] - source[t + 1, at]

        sweep(count, inner_coef, first)
        sweep(count, coef, second)
        sweep(count, coef, third)
        sweep(count - 1, coef, fourth)

    mine = (lane >= HALO) & (lane < HALO + OWN)
    nothing = jnp.zeros((ROWS, LANES), jnp.float32)

    def gram(index, sums):
        at = slice(PAD + index * ROWS, PAD + (index + 1) * ROWS)
        vectors = []
        for ref in krylov:
            newest = pltpu.roll(ref[ref.shape[0] - 1, at], OWN, 1)
            value = jnp.where(mine, ref[ref.shape[0] - 2, at], newest)
            vectors.append((value,) + split(value))
        out = []
        for (i, j), (top, low) in zip(PAIRS, sums):
            (_, upper, lower), (other, other_upper, other_lower) = vectors[i], vectors[j]
            top, error = two_sum(top, upper * other_upper)
            out.append((top, low + (error + (upper * other_lower + lower * other))))
        return out

    sums = [(nothing, nothing) for _ in PAIRS]
    for index in range(strips):
        sums = gram(index, sums)
    tops = [nothing, nothing]
    lows = [nothing, nothing]
    for n, (top, low) in enumerate(sums):
        for shift in (4, 2, 1):
            top, error = two_sum(top, pltpu.roll(top, shift, 0))
            low = low + pltpu.roll(low, shift, 0) + error
        tops[n // ROWS] = jnp.where(sub == n % ROWS, top, tops[n // ROWS])
        lows[n // ROWS] = jnp.where(sub == n % ROWS, low, lows[n // ROWS])
    packed = [nothing, nothing]
    for n in range(2):
        parts = exact_sum(tops[n], lows[n], 1)
        for kind in range(2):
            packed[kind] = jnp.where(lane == sub + n * ROWS, parts[kind], packed[kind])
    packed = [jnp.sum(value, axis=0, keepdims=True) for value in packed]
    packed = jnp.where(sub[:FINE] == 0, packed[0], packed[1])

    for c in range(2):
        for s in range(strips):
            peer = place(c * strips + s, strips)
            at = slice(PAD + s * ROWS, PAD + (s + 1) * ROWS)
            for pair in range(2):
                low = lifted[2 * pair]
                high = lifted[2 * pair + 1]
                turned = pltpu.roll(high[high.shape[0] - 2 + c, at], OWN, 1)
                value = jnp.where(mine, low[low.shape[0] - 2 + c, at], turned)
                for part in range(ROWS // FINE):
                    out[peer, 4 * pair + part] = value[part * FINE : (part + 1) * FINE]
            out[peer, 8] = packed


def least_squares(columns, beta_norm):
    num_columns = len(columns)
    cosines = []
    sines = []
    target = [beta_norm] + [jnp.zeros_like(beta_norm) for position in range(num_columns)]
    history = []
    triangle = []
    for column_at in range(num_columns):
        column = list(columns[column_at])
        for earlier in range(column_at):
            first_entry = column[earlier]
            second_entry = column[earlier + 1]
            column[earlier] = cosines[earlier] * first_entry + sines[earlier] * second_entry
            column[earlier + 1] = cosines[earlier] * second_entry - sines[earlier] * first_entry
        radius = jnp.sqrt(
            column[column_at] * column[column_at] + column[column_at + 1] * column[column_at + 1]
        )
        cosine = column[column_at] / radius
        sine_part = column[column_at + 1] / radius
        column[column_at] = radius
        cosines.append(cosine)
        sines.append(sine_part)
        target[column_at + 1] = -sine_part * target[column_at]
        target[column_at] = cosine * target[column_at]
        history.append(jnp.abs(target[column_at + 1]))
        triangle.append(column[: column_at + 1])
    solved = [None for position in range(num_columns)]
    for row_at in reversed(range(num_columns)):
        running_sum = target[row_at]
        for later in range(row_at + 1, num_columns):
            running_sum = running_sum - triangle[later][row_at] * solved[later]
        solved[row_at] = running_sum / triangle[row_at][row_at]
    return (solved, history)


def cycle(gram):
    size = KRYLOV + 1
    floors = [1e-12 * gram[k, k].top + 1e-30 for k in range(size)]
    upper = {}
    for k in range(size):
        pivot = jnp.maximum(gram[k, k].top, floors[k])
        root = jnp.sqrt(pivot)
        upper[k, k] = root
        for j in range(k + 1, size):
            upper[k, j] = gram[k, j].top / root
        if k + 1 < size:
            inverse = Pair(pivot, jnp.where(gram[k, k].top < floors[k], 0.0, gram[k, k].low)).inverse()
            for i in range(k + 1, size):
                factor = gram[k, i].times(inverse)
                for j in range(i, size):
                    gram[i, j] = gram[i, j].minus(factor.times(gram[k, j]))

    mapped = []
    for i in range(KRYLOV):
        column = []
        for row in range(i + 2):
            value = upper[row, i + 1]
            if row <= i:
                value = value + upper[row, i]
            for k in range(max(row - 1, 0), i):
                value = value - upper[k, i] * mapped[k][row]
            column.append(value / upper[i, i])
        mapped.append(column)

    beta_norm = upper[0, 0]
    basis = [[jnp.ones_like(beta_norm)]]
    columns = []
    for at in range(KRYLOV):
        newest = basis[-1]
        image = []
        for row in range(at + 2):
            terms = [mapped[i][row] * newest[i] for i in range(max(row - 1, 0), at + 1)]
            image.append(functools.reduce(lambda a, b: a + b, terms))
        projections = []
        rest = list(image)
        for vector in basis:
            terms = [a * b for a, b in zip(image, vector)]
            projections.append(functools.reduce(lambda a, b: a + b, terms))
        for vector, weight in zip(basis, projections):
            for row, value in enumerate(vector):
                rest[row] = rest[row] - weight * value
        terms = [value * value for value in rest]
        length = jnp.sqrt(functools.reduce(lambda a, b: a + b, terms) + 1e-06)
        columns.append(projections + [length])
        basis.append([value / length for value in rest])
    solved, history = least_squares(columns, beta_norm)
    weights = [None] * KRYLOV
    for row in reversed(range(KRYLOV)):
        terms = [solved[j] * basis[j][row] for j in range(row, KRYLOV)]
        value = functools.reduce(lambda a, b: a + b, terms)
        for later in range(row + 1, KRYLOV):
            value = value - upper[row, later] * weights[later]
        weights[row] = value / upper[row, row]
    return weights, history


def combine_kernel(partial, got, solution, history):
    lane = lax.broadcasted_iota(jnp.int32, (ROWS, LANES), 1)
    top, low = exact_sum(partial[:, 0, :], partial[:, 1, :], 0)
    gram = {}
    for n, pair in enumerate(PAIRS):
        values = [jnp.sum(jnp.where(lane[0:1] == n, row, 0.0), axis=1, keepdims=True) for row in (top, low)]
        gram[pair] = Pair(*values)
    weights, norms = cycle(gram)
    for n, norm in enumerate(norms):
        history[n] = jnp.max(norm)
    half = lane[:FINE]
    mine = (half >= HALO) & (half < HALO + OWN)
    low = jnp.where(mine, weights[0], weights[1])
    high = jnp.where(mine, weights[2], weights[3])

    def block(device, part):
        index = place(device, got.shape[0] // 2)
        value = low * got[index, part] + high * got[index, 4 + part]
        return pltpu.roll(value, LANES - HALO, 1) + pltpu.roll(value, OWN - HALO, 1)

    for k in range(got.shape[0] // 2):
        for part in range(ROWS // FINE):
            value = jnp.where(half < OWN, block(2 * k, part), block(2 * k + 1, part))
            solution[0, part * FINE : (part + 1) * FINE, k * LANES : (k + 1) * LANES] = value


def body(layers, strips, right_side, cell_terms, polynomial):
    f32 = jnp.float32
    peers = 2 * strips
    rows = ROWS * strips
    circle = [(first_of(strips) + i) % peers for i in range(peers)]

    def exchange(value):
        return lax.all_to_all(value, ("c", "s"), 0, 0, axis_index_groups=[circle], tiled=True)

    earlier = lax.ppermute(right_side, "z", [(i, i + 2) for i in range(layers - 2)])
    before = lax.ppermute(right_side, "z", [(i, i + 1) for i in range(layers - 1)])
    own = pl.pallas_call(
        own_kernel,
        out_shape=jax.ShapeDtypeStruct((peers, 7, HALF, LANES), f32),
        in_specs=[VMEM] * 2,
        out_specs=VMEM,
        compiler_params=PARAMS,
        cost_estimate=pl.CostEstimate(flops=1000000, bytes_accessed=4000000, transcendentals=0),
        name="own",
    )(right_side, cell_terms)
    sent = pl.pallas_call(
        pack_kernel,
        out_shape=jax.ShapeDtypeStruct((peers, 7, HALF, LANES), f32),
        in_specs=[VMEM] * 3,
        out_specs=VMEM,
        compiler_params=PARAMS,
        name="pack",
    )(own, before, earlier)
    got = exchange(sent)
    times = KRYLOV + 2
    field = lambda count: pltpu.VMEM((count, rows + 2 * PAD, LANES), f32)
    sent = pl.pallas_call(
        functools.partial(krylov_kernel, strips),
        out_shape=jax.ShapeDtypeStruct((peers, 9, FINE, LANES), f32),
        in_specs=[SMEM, VMEM],
        out_specs=VMEM,
        scratch_shapes=[pltpu.VMEM((5, rows, LANES), f32)] * 2
        + [field(times - j) for j in range(KRYLOV + 1)]
        + [field(times - j) for j in range(KRYLOV)]
        + [field(times), field(times)],
        compiler_params=PARAMS,
        name="krylov",
    )(polynomial, got)
    got = exchange(sent)
    partial = jnp.concatenate(exact_sum(got[:, 8, 0, :], got[:, 8, 1, :], 0))
    partial = jnp.broadcast_to(partial[None], (layers, 2, LANES))
    order = sorted(range(layers), key=lambda i: (i != layers // 2 + 1, min(i, layers - i), i))
    partial = lax.all_to_all(partial, "z", 0, 0, axis_index_groups=[order], tiled=True)
    return pl.pallas_call(
        combine_kernel,
        out_shape=(jax.ShapeDtypeStruct(right_side.shape, f32), jax.ShapeDtypeStruct((KRYLOV,), f32)),
        in_specs=[VMEM, VMEM],
        out_specs=(VMEM, SMEM),
        compiler_params=PARAMS,
        name="combine",
    )(partial, got)


def solution(mesh):
    layers = mesh.shape["tm"] // 2
    strips = mesh.shape["space"]
    fine = Mesh(mesh.devices.reshape(layers, 2, strips), ("z", "c", "s"))
    in_specs = (P(("z", "c"), "s", None), P(None, "s", None), P())
    out_specs = (P(("z", "c"), "s", None), P())
    return jax.shard_map(
        functools.partial(body, layers, strips), mesh=fine, in_specs=in_specs, out_specs=out_specs, check_vma=False
    )
```

```python
import functools

import jax
import jax.numpy as jnp
from jax import lax
from jax.experimental import pallas as pl
from jax.experimental.pallas import tpu as pltpu
from jax.sharding import Mesh, PartitionSpec as P

KRYLOV = 4
OWN = 64
HALO = 16
WIDE = OWN + 2 * HALO
HALF = 4
FINE = 2
LANES = 128
ROWS = 8
PAD = 8
CHUNK = 64
PAIRS = [(i, j) for i in range(KRYLOV + 1) for j in range(i, KRYLOV + 1)]
VMEM = pl.BlockSpec(memory_space=pltpu.VMEM)
SMEM = pl.BlockSpec(memory_space=pltpu.SMEM)
PARAMS = pltpu.CompilerParams(vmem_limit_bytes=40 * 1024 * 1024)


def first_of(strips):
    return strips + strips // 2 + strips // 8


def place(device, strips):
    return (device - first_of(strips)) % (2 * strips)


def tiles_of(source):
    return [source[:, k * LANES : (k + 1) * LANES] for k in range(source.shape[1] // LANES)]


def windows(tiles, lane):
    zero = jnp.zeros_like(tiles[0])
    even = [zero] + [pltpu.roll(tile, HALO, 1) for tile in tiles]
    odd = [pltpu.roll(tile, LANES - OWN + HALO, 1) for tile in tiles] + [zero]
    out = []
    for k in range(len(tiles)):
        out.append(jnp.where(lane < HALO, even[k], even[k + 1]))
        out.append(jnp.where(lane < LANES - OWN + HALO, odd[k], odd[k + 1]))
    return out


def riders(tiles, lane):
    zero = jnp.zeros_like(tiles[0])
    turned = {shift: [pltpu.roll(tile, shift, 1) for tile in tiles] for shift in (16, 48, 80, 112)}
    edge = [zero] + turned[112] + [zero]
    out = []
    for k in range(len(tiles)):
        out.append([jnp.where(lane < 112, edge[k], edge[k + 1]), turned[80][k], turned[48][k]])
        out.append([turned[48][k], turned[16][k], jnp.where(lane < 112, edge[k + 1], edge[k + 2])])
    return out


def put(out, peer, plane, value):
    out[peer, 2 * plane] = value[:HALF]
    out[peer, 2 * plane + 1] = value[HALF:]


def own_kernel(now, terms, out):
    core = lax.axis_index("c")
    lane = lax.broadcasted_iota(jnp.int32, (ROWS, LANES), 1)
    fields = windows(tiles_of(now.at[0]), lane)
    parts = riders(tiles_of(terms.at[2 * core]), lane)
    across = windows(tiles_of(terms.at[1]), lane)
    upper = (lane >= 0) & (core == 0)
    for device, (field, part, drift) in enumerate(zip(fields, parts, across)):
        peer = place(device, out.shape[0] // 2)
        put(out, peer, 0, jnp.where(lane < WIDE, field, part[0]))
        put(out, peer, 1, part[1])
        put(out, peer, 2, part[2])
        out[peer, 6] = jnp.where(upper[:HALF], drift[:HALF], drift[HALF:])


def pack_kernel(own, before, earlier, out):
    lane = lax.broadcasted_iota(jnp.int32, (ROWS, LANES), 1)
    narrow = lane[:HALF] < WIDE
    for peer in range(out.shape[0]):
        for half in (0, 1, 6):
            out[peer, half] = own[peer, half]
    for plane, source in ((1, before), (2, earlier)):
        for device, window in enumerate(windows(tiles_of(source.at[0]), lane)):
            peer = place(device, out.shape[0] // 2)
            out[peer, 2 * plane] = jnp.where(narrow, window[:HALF], own[peer, 2 * plane])
            out[peer, 2 * plane + 1] = jnp.where(narrow, window[HALF:], own[peer, 2 * plane + 1])


def two_sum(a, b):
    total = a + b
    moved = total - a
    return total, (a - (total - moved)) + (b - moved)


def split(a):
    scaled = 4097.0 * a
    upper = scaled - (scaled - a)
    return upper, a - upper


def exact_sum(top, low, axis):
    quantum = 1024.0 * jnp.max(jnp.abs(top), axis=axis, keepdims=True)
    upper = (top + quantum) - quantum
    rest = (top - upper) + low
    return jnp.sum(upper, axis=axis, keepdims=True), jnp.sum(rest, axis=axis, keepdims=True)


class Pair:
    def __init__(self, top, low):
        self.top = top + low
        self.low = low - (self.top - top)
        self.parts = split(self.top)

    def times(self, other):
        value = self.top * other.top
        (a, b), (c, d) = self.parts, other.parts
        error = (((a * c - value) + a * d) + b * c) + b * d
        return Pair(value, error + (self.top * other.low + self.low * other.top))

    def minus(self, other):
        value, error = two_sum(self.top, -other.top)
        return Pair(value, error + (self.low - other.low))

    def inverse(self):
        guess = 1.0 / self.top
        value = guess * self.top
        (a, b), (c, d) = split(guess), self.parts
        error = (((a * c - value) + a * d) + b * c) + b * d
        return Pair(guess, guess * (((1.0 - value) - error) - guess * self.low))


def krylov_kernel(strips, polynomial, got, out, coef, inner_coef, k0, k1, k2, k3, k4, z1, z2, z3, z4, work_x, work_y):
    rows = ROWS * strips
    times = KRYLOV + 2
    krylov = [k0, k1, k2, k3, k4]
    lifted = [z1, z2, z3, z4]
    lane = lax.broadcasted_iota(jnp.int32, (ROWS, LANES), 1)
    sub = lax.broadcasted_iota(jnp.int32, (ROWS, LANES), 0)
    block = lax.axis_index("c") * strips + lax.axis_index("s")
    first_col = (block == 0) & (lane == HALO)
    last_col = (block == 2 * strips - 1) & (lane == HALO + OWN - 1)

    edge = jnp.zeros((PAD, LANES), jnp.float32)
    for ref in krylov + lifted + [work_x, work_y]:
        for t in range(ref.shape[0]):
            ref[t, 0:PAD] = edge
            ref[t, PAD + rows :] = edge

    for s in range(strips):
        for c in range(2):
            peer = place(c * strips + s, strips)
            at = PAD + s * ROWS
            for plane in range(3):
                k0[times - 2 + c - 2 * plane, at : at + HALF] = got[peer, 2 * plane]
                k0[times - 2 + c - 2 * plane, at + HALF : at + ROWS] = got[peer, 2 * plane + 1]
            coef[3, s * ROWS + c * HALF : s * ROWS + (c + 1) * HALF] = got[peer, 6]

    def rider(at, c):
        last = [pltpu.roll(k0[times - 2 + c - 2 * plane, at], 32 * (plane + 1), 1) for plane in range(3)]
        last[2] = jnp.where(lane < WIDE, last[2], 0.0)
        return jnp.where(lane < 32, last[0], jnp.where(lane < 64, last[1], last[2]))

    for s in range(strips):
        there = slice(s * ROWS, (s + 1) * ROWS)
        inner = slice(PAD + s * ROWS, PAD + (s + 1) * ROWS)
        diffuse = rider(inner, 0)
        half_x = 0.5 * coef[3, there]
        half_y = 0.5 * rider(inner, 1)
        north = -diffuse - half_y
        south = half_y - diffuse
        if s == 0:
            north = jnp.where(sub == 0, 0.0, north)
        if s == strips - 1:
            south = jnp.where(sub == ROWS - 1, 0.0, south)
        coef[0, there] = 1.0 + 4.0 * diffuse
        coef[1, there] = north
        coef[2, there] = south
        coef[3, there] = jnp.where(first_col, 0.0, -diffuse - half_x)
        coef[4, there] = jnp.where(last_col, 0.0, half_x - diffuse)
        for i in range(5):
            scaled = polynomial[3] * coef[i, there]
            inner_coef[i, there] = polynomial[2] + scaled if i == 0 else scaled

    def sweep(count, terms, apply):
        chunk = min(CHUNK, rows)
        for at in range(0, rows, chunk):
            parts = [terms[i, at : at + chunk] for i in range(5)]

            def stencil(ref, t):
                middle = ref[t, at + PAD : at + PAD + chunk]
                north = ref[t, at + PAD - 1 : at + PAD - 1 + chunk]
                south = ref[t, at + PAD + 1 : at + PAD + 1 + chunk]
                west = pltpu.roll(middle, 1, 1)
                east = pltpu.roll(middle, LANES - 1, 1)
                return (
                    (parts[0] * middle + parts[3] * west)
                    + (parts[1] * north + parts[2] * south)
                    + parts[4] * east
                )

            for t in range(count):
                apply(t, slice(at + PAD, at + PAD + chunk), stencil)

    for j in range(KRYLOV):
        source, target, upper = krylov[j], krylov[j + 1], lifted[j]
        count = times - j

        def first(t, at, stencil):
            work_x[t, at] = stencil(source, t)

        def second(t, at, stencil):
            work_y[t, at] = polynomial[1] * source[t, at] + stencil(work_x, t)

        def third(t, at, stencil):
            upper[t, at] = polynomial[0] * source[t, at] + stencil(work_y, t)

        def fourth(t, at, stencil):
            target[t, at] = stencil(upper, t + 1) - upper[t, at] - source[t + 1, at]

        sweep(count, inner_coef, first)
        sweep(count, coef, second)
        sweep(count, coef, third)
        sweep(count - 1, coef, fourth)

    mine = (lane >= HALO) & (lane < HALO + OWN)
    nothing = jnp.zeros((ROWS, LANES), jnp.float32)

    def gram(index, sums):
        at = slice(PAD + index * ROWS, PAD + (index + 1) * ROWS)
        vectors = []
        for ref in krylov:
            newest = pltpu.roll(ref[ref.shape[0] - 1, at], OWN, 1)
            value = jnp.where(mine, ref[ref.shape[0] - 2, at], newest)
            vectors.append((value,) + split(value))
        out = []
        for (i, j), (top, low) in zip(PAIRS, sums):
            (_, upper, lower), (other, other_upper, other_lower) = vectors[i], vectors[j]
            top, error = two_sum(top, upper * other_upper)
            out.append((top, low + (error + (upper * other_lower + lower * other))))
        return out

    sums = [(nothing, nothing) for _ in PAIRS]
    for index in range(strips):
        sums = gram(index, sums)
    tops = [nothing, nothing]
    lows = [nothing, nothing]
    for n, (top, low) in enumerate(sums):
        for shift in (4, 2, 1):
            top, error = two_sum(top, pltpu.roll(top, shift, 0))
            low = low + pltpu.roll(low, shift, 0) + error
        tops[n // ROWS] = jnp.where(sub == n % ROWS, top, tops[n // ROWS])
        lows[n // ROWS] = jnp.where(sub == n % ROWS, low, lows[n // ROWS])
    packed = [nothing, nothing]
    for n in range(2):
        parts = exact_sum(tops[n], lows[n], 1)
        for kind in range(2):
            packed[kind] = jnp.where(lane == sub + n * ROWS, parts[kind], packed[kind])
    packed = [jnp.sum(value, axis=0, keepdims=True) for value in packed]
    packed = jnp.where(sub[:FINE] == 0, packed[0], packed[1])

    for c in range(2):
        for s in range(strips):
            peer = place(c * strips + s, strips)
            at = slice(PAD + s * ROWS, PAD + (s + 1) * ROWS)
            for pair in range(2):
                low = lifted[2 * pair]
                high = lifted[2 * pair + 1]
                turned = pltpu.roll(high[high.shape[0] - 2 + c, at], OWN, 1)
                value = jnp.where(mine, low[low.shape[0] - 2 + c, at], turned)
                for part in range(ROWS // FINE):
                    out[peer, 4 * pair + part] = value[part * FINE : (part + 1) * FINE]
            out[peer, 8] = packed


def least_squares(columns, beta_norm):
    num_columns = len(columns)
    cosines = []
    sines = []
    target = [beta_norm] + [jnp.zeros_like(beta_norm) for position in range(num_columns)]
    history = []
    triangle = []
    for column_at in range(num_columns):
        column = list(columns[column_at])
        for earlier in range(column_at):
            first_entry = column[earlier]
            second_entry = column[earlier + 1]
            column[earlier] = cosines[earlier] * first_entry + sines[earlier] * second_entry
            column[earlier + 1] = cosines[earlier] * second_entry - sines[earlier] * first_entry
        radius = jnp.sqrt(
            column[column_at] * column[column_at] + column[column_at + 1] * column[column_at + 1]
        )
        cosine = column[column_at] / radius
        sine_part = column[column_at + 1] / radius
        column[column_at] = radius
        cosines.append(cosine)
        sines.append(sine_part)
        target[column_at + 1] = -sine_part * target[column_at]
        target[column_at] = cosine * target[column_at]
        history.append(jnp.abs(target[column_at + 1]))
        triangle.append(column[: column_at + 1])
    solved = [None for position in range(num_columns)]
    for row_at in reversed(range(num_columns)):
        running_sum = target[row_at]
        for later in range(row_at + 1, num_columns):
            running_sum = running_sum - triangle[later][row_at] * solved[later]
        solved[row_at] = running_sum / triangle[row_at][row_at]
    return (solved, history)


def cycle(gram):
    size = KRYLOV + 1
    floors = [1e-12 * gram[k, k].top + 1e-30 for k in range(size)]
    upper = {}
    for k in range(size):
        pivot = jnp.maximum(gram[k, k].top, floors[k])
        root = jnp.sqrt(pivot)
        upper[k, k] = root
        for j in range(k + 1, size):
            upper[k, j] = gram[k, j].top / root
        if k + 1 < size:
            inverse = Pair(pivot, jnp.where(gram[k, k].top < floors[k], 0.0, gram[k, k].low)).inverse()
            for i in range(k + 1, size):
                factor = gram[k, i].times(inverse)
                for j in range(i, size):
                    gram[i, j] = gram[i, j].minus(factor.times(gram[k, j]))

    mapped = []
    for i in range(KRYLOV):
        column = []
        for row in range(i + 2):
            value = upper[row, i + 1]
            if row <= i:
                value = value + upper[row, i]
            for k in range(max(row - 1, 0), i):
                value = value - upper[k, i] * mapped[k][row]
            column.append(value / upper[i, i])
        mapped.append(column)

    beta_norm = upper[0, 0]
    basis = [[jnp.ones_like(beta_norm)]]
    columns = []
    for at in range(KRYLOV):
        newest = basis[-1]
        image = []
        for row in range(at + 2):
            terms = [mapped[i][row] * newest[i] for i in range(max(row - 1, 0), at + 1)]
            image.append(functools.reduce(lambda a, b: a + b, terms))
        projections = []
        rest = list(image)
        for vector in basis:
            terms = [a * b for a, b in zip(image, vector)]
            projections.append(functools.reduce(lambda a, b: a + b, terms))
        for vector, weight in zip(basis, projections):
            for row, value in enumerate(vector):
                rest[row] = rest[row] - weight * value
        terms = [value * value for value in rest]
        length = jnp.sqrt(functools.reduce(lambda a, b: a + b, terms) + 1e-06)
        columns.append(projections + [length])
        basis.append([value / length for value in rest])
    solved, history = least_squares(columns, beta_norm)
    weights = [None] * KRYLOV
    for row in reversed(range(KRYLOV)):
        terms = [solved[j] * basis[j][row] for j in range(row, KRYLOV)]
        value = functools.reduce(lambda a, b: a + b, terms)
        for later in range(row + 1, KRYLOV):
            value = value - upper[row, later] * weights[later]
        weights[row] = value / upper[row, row]
    return weights, history


def combine_kernel(partial, got, solution, history):
    lane = lax.broadcasted_iota(jnp.int32, (ROWS, LANES), 1)
    top, low = exact_sum(partial[:, 0, :], partial[:, 1, :], 0)
    gram = {}
    for n, pair in enumerate(PAIRS):
        values = [jnp.sum(jnp.where(lane[0:1] == n, row, 0.0), axis=1, keepdims=True) for row in (top, low)]
        gram[pair] = Pair(*values)
    weights, norms = cycle(gram)
    for n, norm in enumerate(norms):
        history[n] = jnp.max(norm)
    half = lane[:FINE]
    mine = (half >= HALO) & (half < HALO + OWN)
    low = jnp.where(mine, weights[0], weights[1])
    high = jnp.where(mine, weights[2], weights[3])

    def block(device, part):
        index = place(device, got.shape[0] // 2)
        value = low * got[index, part] + high * got[index, 4 + part]
        return pltpu.roll(value, LANES - HALO, 1) + pltpu.roll(value, OWN - HALO, 1)

    for k in range(got.shape[0] // 2):
        for part in range(ROWS // FINE):
            value = jnp.where(half < OWN, block(2 * k, part), block(2 * k + 1, part))
            solution[0, part * FINE : (part + 1) * FINE, k * LANES : (k + 1) * LANES] = value


def body(layers, strips, right_side, cell_terms, polynomial):
    f32 = jnp.float32
    peers = 2 * strips
    rows = ROWS * strips
    circle = [(first_of(strips) + i) % peers for i in range(peers)]

    def exchange(value):
        return lax.all_to_all(value, ("c", "s"), 0, 0, axis_index_groups=[circle], tiled=True)

    earlier = lax.ppermute(right_side, "z", [(i, i + 2) for i in range(layers - 2)])
    before = lax.ppermute(right_side, "z", [(i, i + 1) for i in range(layers - 1)])
    own = pl.pallas_call(
        own_kernel,
        out_shape=jax.ShapeDtypeStruct((peers, 7, HALF, LANES), f32),
        in_specs=[VMEM] * 2,
        out_specs=VMEM,
        compiler_params=PARAMS,
        cost_estimate=pl.CostEstimate(flops=1000000, bytes_accessed=4000000, transcendentals=0),
        name="own",
    )(right_side, cell_terms)
    sent = pl.pallas_call(
        pack_kernel,
        out_shape=jax.ShapeDtypeStruct((peers, 7, HALF, LANES), f32),
        in_specs=[VMEM] * 3,
        out_specs=VMEM,
        compiler_params=PARAMS,
        name="pack",
    )(own, before, earlier)
    got = exchange(sent)
    times = KRYLOV + 2
    field = lambda count: pltpu.VMEM((count, rows + 2 * PAD, LANES), f32)
    sent = pl.pallas_call(
        functools.partial(krylov_kernel, strips),
        out_shape=jax.ShapeDtypeStruct((peers, 9, FINE, LANES), f32),
        in_specs=[SMEM, VMEM],
        out_specs=VMEM,
        scratch_shapes=[pltpu.VMEM((5, rows, LANES), f32)] * 2
        + [field(times - j) for j in range(KRYLOV + 1)]
        + [field(times - j) for j in range(KRYLOV)]
        + [field(times), field(times)],
        compiler_params=PARAMS,
        name="krylov",
    )(polynomial, got)
    got = exchange(sent)
    partial = jnp.concatenate(exact_sum(got[:, 8, 0, :], got[:, 8, 1, :], 0))
    partial = jnp.broadcast_to(partial[None], (layers, 2, LANES))
    order = sorted(range(layers), key=lambda i: (i != layers // 2, min(i, layers - i), i))
    partial = lax.all_to_all(partial, "z", 0, 0, axis_index_groups=[order], tiled=True)
    return pl.pallas_call(
        combine_kernel,
        out_shape=(jax.ShapeDtypeStruct(right_side.shape, f32), jax.ShapeDtypeStruct((KRYLOV,), f32)),
        in_specs=[VMEM, VMEM],
        out_specs=(VMEM, SMEM),
        compiler_params=PARAMS,
        name="combine",
    )(partial, got)


def solution(mesh):
    layers = mesh.shape["tm"] // 2
    strips = mesh.shape["space"]
    fine = Mesh(mesh.devices.reshape(layers, 2, strips), ("z", "c", "s"))
    in_specs = (P(("z", "c"), "s", None), P(None, "s", None), P())
    out_specs = (P(("z", "c"), "s", None), P())
    return jax.shard_map(
        functools.partial(body, layers, strips), mesh=fine, in_specs=in_specs, out_specs=out_specs, check_vma=False
    )
```
